128 devices in a mesh: outer: 8 (over x_hi, y), inner: 16 (over z, x_lo, core).
Axes of the slice: x: 4 (x_hi: 2, x_lo: 2; x = x_hi * 2 + x_lo), y: 4, z: 4, core: 2. Of those that a mesh axis runs over, the one named last changes fastest.
Arguments:
- stem_activity: float32 [262144, 768], P(('outer', 'inner')), may hold values from -6 to 6
- convolution_weight: bfloat16 [2, 3, 768, 768], replicated, may hold values from -0.125 to 0.125
- convolution_bias: float32 [2, 768], replicated, may hold values from -3 to 3
- query_weight: bfloat16 [768, 768], replicated, as said below
- key_weight: bfloat16 [768, 768], replicated, may hold values from -0.21875 to 0.21875
- value_weight: bfloat16 [768, 768], replicated, may hold values from -0.21875 to 0.21875
- output_weight: bfloat16 [768, 768], replicated, may hold values from -0.21875 to 0.21875
Outputs:
- tower: float32 [262144, 768], P(('outer', 'inner'))
- attended: float32 [2048, 768], P(('outer', 'inner'))
The draws below stay inside these ranges and needn't reach their ends.
Inputs may be any that keep to these rules, and one draw needn't show every extreme that they name: `query_weight`: Real-valued weights of order 768 ** -0.5 or larger.
All inputs are finite; a program needn't handle non-finite values.
Results may differ from the reference program's by a relative error of at most 0.0003.
Values sent between devices are 32-bit elements; how exact they have to be, the bound alone decides.
A program may use at most 128 MiB of HBM per device.

```python
import jax
import jax.numpy as jnp
from jax import lax

C = 768
HEAD_DIM = 64
HEADS = 12
LAYERS = 2
BASE_DILATION = 4096
POOL = 128
BASES = 262144
POOLED = 2048
BLOCK = 256


def draw_query_weight(key, part):
    key = jax.random.fold_in(key, 7)
    base = jax.random.normal(key, (C, C), jnp.float32) * jnp.float32(C ** (-0.5))
    return base.astype(jnp.bfloat16)


def level_of(stream_key, extent, pieces, least, largest):
    def one(position, shards_of):
        draws = jax.random.uniform(jax.random.fold_in(jax.random.fold_in(stream_key, 6), position), (shards_of,), jnp.float32, least / len(pieces), largest / len(pieces))
        return jnp.repeat(jnp.exp(draws), extent[position] // shards_of).reshape((-1,) + (1,) * (len(extent) - position - 1))

    level = one(*pieces[0])
    for cut in pieces[1:]:
        level = level * one(*cut)
    return level


def scatter_about(own_key, extent, deviation, reach, shards=(), kind=jnp.bfloat16):
    loudness = level_of(own_key, extent, shards, -0.22, 0.18) if shards else 1.0
    array = jax.random.normal(own_key, extent, jnp.float32) * deviation * loudness
    return jnp.minimum(jnp.maximum(array, -reach), reach).astype(kind)


def setup_inputs(seed: int = 0) -> dict:
    seeds = jax.random.split(jax.random.key(seed), 8)
    stem_activity = scatter_about(seeds[0], (BASES, C), 1.0, 6.0, ((0, 128),), jnp.float32)
    convolution_weight = scatter_about(seeds[1], (LAYERS, 3, C, C), (3 * C) ** -0.5, 0.125)
    convolution_bias = scatter_about(seeds[2], (LAYERS, C), 0.5, 3.0, (), jnp.float32)
    query_weight = draw_query_weight(jax.random.fold_in(seeds[7], 71), 0)
    key_weight = scatter_about(seeds[4], (C, C), C ** -0.5, 0.21875)
    value_weight = scatter_about(seeds[5], (C, C), C ** -0.5, 0.21875)
    output_weight = scatter_about(seeds[6], (C, C), C ** -0.5, 0.21875)
    return {"stem_activity": stem_activity, "convolution_weight": convolution_weight, "convolution_bias": convolution_bias, "query_weight": query_weight, "key_weight": key_weight, "value_weight": value_weight, "output_weight": output_weight}


def product(left, right):
    return jnp.dot(left, right.astype(jnp.float32), preferred_element_type=jnp.float32, precision=lax.Precision.HIGHEST)


def dilated_input(receptive_field, weight, bias, span):
    active = jax.nn.gelu(receptive_field, approximate=False)
    padded = jnp.pad(active, ((span, span), (0, 0)))
    lower = padded[:-2 * span]
    upper = padded[2 * span:]
    conv = product(lower, weight[0]) + product(active, weight[1]) + product(upper, weight[2]) + bias
    return receptive_field + conv


def reference(stem_activity, convolution_weight, convolution_bias, query_weight, key_weight, value_weight, output_weight):
    receptive_field = stem_activity
    for index_of_layer in range(LAYERS):
        receptive_field = dilated_input(receptive_field, convolution_weight[index_of_layer], convolution_bias[index_of_layer], BASE_DILATION * 2 ** index_of_layer)
    tower = receptive_field
    pooled = tower.reshape(POOLED, POOL, C).mean(axis=1)
    queries = product(pooled, query_weight).reshape(-1, BLOCK, HEADS, HEAD_DIM)
    keys_all = product(pooled, key_weight).reshape(-1, BLOCK, HEADS, HEAD_DIM)
    vals = product(pooled, value_weight).reshape(-1, BLOCK, HEADS, HEAD_DIM)
    scores = jnp.einsum("nqhe,nkhe->nhqk", queries, keys_all, precision=lax.Precision.HIGHEST) / jnp.float32(HEAD_DIM ** 0.5)
    probs = jax.nn.softmax(scores, axis=-1)
    mixed = jnp.einsum("nhqk,nkhe->nqhe", probs, vals, precision=lax.Precision.HIGHEST).reshape(POOLED, C)
    attended = pooled + product(mixed, output_weight)
    return tower, attended
```

```python
import jax
import jax.numpy as jnp
from jax import lax
from jax.experimental import pallas as pl
from jax.experimental.pallas import tpu as pltpu
from jax.sharding import PartitionSpec as P

HEAD_DIM = 64
POOL = 128
GROUPS = 8
MEMBERS = 8
HALO = 3
CHUNKS = 8
IN_FLIGHT = 2
HELD = 4
AHEAD = 2
COLUMNS = 256
PAIR = 2 * HEAD_DIM
MESH = pl.DeviceIdType.MESH
F32, BF16 = jnp.float32, jnp.bfloat16


def gelu(x):
    return 0.5 * x * (1.0 + lax.erf(x * (0.5**0.5)))


def dot(left, right):
    return jnp.dot(left, right, preferred_element_type=F32)


def thirds(value):
    high = value.astype(BF16)
    rest = value - high.astype(F32)
    middle = rest.astype(BF16)
    return high, middle, (rest - middle.astype(F32)).astype(BF16)


def widened(value, weight):
    high, middle, low = thirds(value)
    return (dot(low, weight) + dot(middle, weight)) + dot(high, weight)


def swapped(member, outer):
    return member // 2 * 2 + (member + outer // 4) % 2


def tower_kernel(
    stem, weight, bias, query_weight, key_weight, value_weight, output_weight,
    tower, attended,
    rows_in, rows_out, taps, active, second, field, everyone, mixed, heads_weight,
    weight_sem, heads_sem, in_send, in_recv, halo_send, halo_recv, out_send, out_recv,
    pool_send, pool_recv, share_send, share_recv,
):
    outer, inner = lax.axis_index("outer"), lax.axis_index("inner")
    member, core = inner // 2, inner % 2
    chans = stem.shape[1]
    part = stem.shape[0] // MEMBERS
    rows = part // CHUNKS
    mine = swapped(member, outer)
    up, down = (outer + 1) % GROUPS, (outer + GROUPS - 1) % GROUPS
    neighbours = (
        (up, 2 * swapped(mine, up) + core),
        (down, 2 * swapped(mine, down) + core),
    )

    def other(step):
        return (member // 2 + step // 2) % 4 * 2 + (member + step) % 2

    barrier = pltpu.get_barrier_semaphore()

    def greet(device):
        pl.semaphore_signal(barrier, inc=1, device_id=device, device_id_type=MESH)

    for step in range(1, MEMBERS):
        greet((outer, 2 * other(step) + core))
    greet((outer, inner + 1 - 2 * core))
    for neighbour in neighbours:
        greet(neighbour)

    def load_taps(layer, tap, half):
        return pltpu.make_async_copy(
            weight.at[layer, tap],
            taps.at[layer, tap, pl.ds(half * chans, chans)],
            weight_sem.at[layer, tap, half],
        )

    def load_heads(k):
        source = (query_weight, key_weight, value_weight, output_weight)[k]
        return pltpu.make_async_copy(source, heads_weight.at[k], heads_sem.at[k])

    every_tap = [(layer, tap, half) for layer in range(2) for tap in range(3) for half in range(2)]
    for which in every_tap:
        load_taps(*which).start()
    for k in range(4):
        load_heads(k).start()

    pl.semaphore_wait(barrier, MEMBERS + len(neighbours))

    def span(chunk):
        return pl.ds(pl.multiple_of(chunk * rows, rows), rows)

    def piece(index, chunk):
        return pl.ds(pl.multiple_of(index * part + chunk * rows, rows), rows)

    def send_in(chunk, step):
        to = other(step)
        return pltpu.make_async_remote_copy(
            src_ref=stem.at[piece(swapped(to, outer), chunk)],
            dst_ref=rows_in.at[HALO + member, span(chunk)],
            send_sem=in_send.at[chunk, step],
            recv_sem=in_recv.at[chunk, member],
            device_id=(outer, 2 * to + core),
            device_id_type=MESH,
        )

    def keep_in(chunk):
        return pltpu.make_async_copy(
            stem.at[piece(mine, chunk)], rows_in.at[HALO + member, span(chunk)], in_recv.at[chunk, member]
        )

    def arrived(chunk, block):
        there = rows_in.at[HALO + block, span(chunk)]
        return pltpu.make_async_copy(there, there, in_recv.at[chunk, block])

    def send_halo(chunk, side):
        return pltpu.make_async_remote_copy(
            src_ref=rows_in.at[pl.ds(MEMBERS if side == 0 else HALO, HALO), span(chunk)],
            dst_ref=rows_in.at[pl.ds(0 if side == 0 else HALO + MEMBERS, HALO), span(chunk)],
            send_sem=halo_send.at[chunk, side],
            recv_sem=halo_recv.at[chunk, side],
            device_id=neighbours[side],
            device_id_type=MESH,
        )

    def send_out(chunk, step):
        to = other(step)
        return pltpu.make_async_remote_copy(
            src_ref=rows_out.at[to, span(chunk)],
            dst_ref=tower.at[piece(mine, chunk)],
            send_sem=out_send.at[chunk, step],
            recv_sem=out_recv.at[chunk, mine],
            device_id=(outer, 2 * to + core),
            device_id_type=MESH,
        )

    def keep_out(chunk):
        return pltpu.make_async_copy(
            rows_out.at[member, span(chunk)], tower.at[piece(mine, chunk)], out_recv.at[chunk, mine]
        )

    def returned(chunk, index):
        there = tower.at[piece(index, chunk)]
        return pltpu.make_async_copy(there, there, out_recv.at[chunk, index])

    def start_in(chunk):
        keep_in(chunk).start()
        for step in range(1, MEMBERS):
            send_in(chunk, step).start()

    def start_out(chunk):
        keep_out(chunk).start()
        for step in range(1, MEMBERS):
            send_out(chunk, step).start()

    def forward(chunk):
        for block in range(MEMBERS - HALO, MEMBERS):
            arrived(chunk, block).wait()
        send_halo(chunk, 0).start()
        for block in range(HALO):
            arrived(chunk, block).wait()
        send_halo(chunk, 1).start()
        for block in range(HALO, MEMBERS - HALO):
            arrived(chunk, block).wait()

    def split(value, into, first, columns=slice(0, 768)):
        high = value.astype(BF16)
        count, start, stop = value.shape[0], columns.start, columns.stop
        into[first : first + count, start:stop] = high
        into[first : first + count, chans + start : chans + stop] = (value - high.astype(F32)).astype(BF16)

    def inside(block):
        if 0 <= block < MEMBERS:
            return 1.0
        number = outer * MEMBERS + block
        return ((number >= 0) & (number < GROUPS * MEMBERS)).astype(F32)

    def conv(source, layer, spread, blocks, columns):
        total = bias[layer : layer + 1, columns]
        for tap in range(3):
            first = tap * spread * rows
            total = total + dot(source[first : first + blocks * rows, :], taps[layer, tap, :, columns])
        return total

    tiles = [slice(start, start + COLUMNS) for start in range(0, chans, COLUMNS)]

    def compute(chunk):
        for block in range(MEMBERS + 2 * HALO):
            split(gelu(rows_in[block, span(chunk)]) * inside(block - HALO), active, block * rows)
        for columns in tiles:
            result = conv(active, 0, 1, MEMBERS + 4, columns)
            for block in range(MEMBERS + 4):
                at = slice(block * rows, (block + 1) * rows)
                total = rows_in[block + 1, span(chunk), columns] + result[at]
                field[at, columns] = total
                split(gelu(total) * inside(block - 2), second, block * rows, columns)
        for columns in tiles:
            result = conv(second, 1, 2, MEMBERS, columns)
            for block in range(MEMBERS):
                at = slice(block * rows, (block + 1) * rows)
                before = field[(block + 2) * rows : (block + 3) * rows, columns]
                rows_out[block, span(chunk), columns] = before + result[at]

    def shelf(run, whose):
        return pl.multiple_of((run * 2 + whose) * MEMBERS * MEMBERS, MEMBERS)

    def slot(run, of):
        return pl.ds(shelf(run, core) + of * MEMBERS, MEMBERS)

    def send_pool(run, step):
        return pltpu.make_async_remote_copy(
            src_ref=everyone.at[slot(run, member)],
            dst_ref=everyone.at[slot(run, member)],
            send_sem=pool_send.at[run, step],
            recv_sem=pool_recv.at[run, member],
            device_id=(outer, 2 * other(step) + core),
            device_id_type=MESH,
        )

    def share(run):
        half = pl.ds(shelf(run, core), MEMBERS * MEMBERS)
        return pltpu.make_async_remote_copy(
            src_ref=everyone.at[half],
            dst_ref=everyone.at[half],
            send_sem=share_send.at[run],
            recv_sem=share_recv.at[run],
            device_id=(outer, inner + 1 - 2 * core),
            device_id_type=MESH,
        )

    def start_pool(run):
        everyone[slot(run, member), :] = jnp.concatenate(
            [
                jnp.sum(rows_out[block, run * POOL : (run + 1) * POOL], axis=0, keepdims=True) * (1.0 / POOL)
                for block in range(MEMBERS)
            ],
            axis=0,
        )
        for step in range(1, MEMBERS):
            send_pool(run, step).start()

    def start_share(run):
        for step in range(1, MEMBERS):
            there = everyone.at[slot(run, other(step))]
            pltpu.make_async_copy(there, there, pool_recv.at[run, other(step)]).wait()
        share(run).start()

    def finish_share(run):
        there = everyone.at[pl.ds(shelf(run, 1 - core), MEMBERS * MEMBERS)]
        pltpu.make_async_copy(there, there, share_recv.at[run]).wait()

    for chunk in range(IN_FLIGHT):
        start_in(chunk)
    for chunk in range(AHEAD):
        forward(chunk)
        start_in(chunk + IN_FLIGHT)
    for which in every_tap:
        load_taps(*which).wait()

    def step_of(chunk, _):
        @pl.when(chunk + AHEAD < CHUNKS)
        def _():
            forward(chunk + AHEAD)

        @pl.when(chunk + AHEAD + IN_FLIGHT < CHUNKS)
        def _():
            start_in(chunk + AHEAD + IN_FLIGHT)

        for side in range(2):
            send_halo(chunk, side).wait_recv()
        compute(chunk)

        @pl.when(chunk == HELD - 1)
        def _():
            start_pool(0)

        @pl.when(chunk == HELD + 1)
        def _():
            start_share(0)

        @pl.when(chunk == CHUNKS - 1)
        def _():
            start_pool(1)

        @pl.when(chunk == HELD)
        def _():
            start_out(0)

        @pl.when(chunk >= HELD)
        def _():
            start_out(chunk - HELD + 1)

        return 0

    lax.fori_loop(0, CHUNKS, step_of, 0)
    start_share(1)
    start_out(CHUNKS - HELD + 1)
    for k in range(4):
        load_heads(k).wait()
    finish_share(0)
    finish_share(1)
    for chunk in range(CHUNKS - HELD + 2, CHUNKS):
        start_out(chunk)

    count = MEMBERS * (part // POOL)
    runs = part // POOL
    total = 2 * MEMBERS * count
    parts = thirds(everyone[...])
    place = lax.broadcasted_iota(jnp.int32, (count, total), 0)
    wanted = ((place % runs * 2 + core) * MEMBERS + swapped(place // runs, outer)) * MEMBERS + member
    chosen = (lax.broadcasted_iota(jnp.int32, (count, total), 1) == wanted).astype(F32).astype(BF16)
    own = (dot(chosen, parts[2]) + dot(chosen, parts[1])) + dot(chosen, parts[0])
    lanes = lax.broadcasted_iota(jnp.int32, (1, PAIR), 1)

    def two_heads(pair, _):
        columns = pl.ds(pl.multiple_of(pair * PAIR, PAIR), PAIR)
        queries = widened(own, heads_weight[0, :, columns]) * (HEAD_DIM**-0.5)
        keys = widened(everyone[...], heads_weight[1, :, columns])
        vals = widened(everyone[...], heads_weight[2, :, columns])
        both = jnp.zeros((count, PAIR), F32)
        for half in range(2):
            mask = (lanes // HEAD_DIM == half).astype(F32)
            scores = lax.dot_general(
                queries * mask,
                keys,
                (((1,), (1,)), ((), ())),
                precision=lax.Precision.HIGHEST,
                preferred_element_type=F32,
            )
            powers = jnp.exp(scores - jnp.max(scores, axis=1, keepdims=True))
            probs = powers / jnp.sum(powers, axis=1, keepdims=True)
            both = both + mask * jnp.dot(
                probs, vals, precision=lax.Precision.HIGHEST, preferred_element_type=F32
            )
        mixed[:, columns] = both
        return 0

    lax.fori_loop(0, chans // PAIR, two_heads, 0)
    attended[...] = own + widened(mixed[...], heads_weight[3])

    for run in range(runs):
        share(run).wait_send()
        for step in range(1, MEMBERS):
            send_pool(run, step).wait_send()

    def finish(chunk, _):
        for side in range(2):
            send_halo(chunk, side).wait_send()
        for step in range(1, MEMBERS):
            send_in(chunk, step).wait_send()
            send_out(chunk, step).wait_send()
        for index in range(MEMBERS):
            returned(chunk, index).wait()
        return 0

    lax.fori_loop(0, CHUNKS, finish, 0)


def shards(stem_activity, convolution_weight, convolution_bias, query_weight, key_weight, value_weight, output_weight):
    length, chans = stem_activity.shape
    part = length // MEMBERS
    rows = part // CHUNKS
    blocks = MEMBERS + 2 * HALO
    pooled = length // POOL
    dma, vmem = pltpu.SemaphoreType.DMA, pltpu.VMEM
    far, on_core = pl.BlockSpec(memory_space=pltpu.HBM), pl.BlockSpec(memory_space=vmem)
    return pl.pallas_call(
        tower_kernel,
        out_shape=(
            vmem((length, chans), F32),
            jax.ShapeDtypeStruct((pooled, chans), F32),
        ),
        in_specs=[far, far, on_core, far, far, far, far],
        out_specs=(on_core, on_core),
        scratch_shapes=[
            vmem((blocks, part, chans), F32),
            vmem((MEMBERS, part, chans), F32),
            vmem((2, 3, 2 * chans, chans), BF16),
            vmem((blocks * rows, 2 * chans), BF16),
            vmem(((blocks - 2) * rows, 2 * chans), BF16),
            vmem(((blocks - 2) * rows, chans), F32),
            vmem((2 * MEMBERS * pooled, chans), F32),
            vmem((pooled, chans), F32),
            vmem((4, chans, chans), BF16),
            dma((2, 3, 2)),
            dma((4,)),
            dma((CHUNKS, MEMBERS)),
            dma((CHUNKS, MEMBERS)),
            dma((CHUNKS, 2)),
            dma((CHUNKS, 2)),
            dma((CHUNKS, MEMBERS)),
            dma((CHUNKS, MEMBERS)),
            dma((2, MEMBERS)),
            dma((2, MEMBERS)),
            dma((2,)),
            dma((2,)),
        ],
        compiler_params=pltpu.CompilerParams(
            collective_id=0, has_side_effects=True, vmem_limit_bytes=50 * 1024 * 1024
        ),
        cost_estimate=pl.CostEstimate(
            flops=5 * 2 * 2 * 3 * length * chans * chans, bytes_accessed=8 * length * chans, transcendentals=0
        ),
        name="tower",
    )(
        stem_activity, convolution_weight, convolution_bias,
        query_weight, key_weight, value_weight, output_weight,
    )


def solution(mesh):
    return jax.shard_map(
        shards,
        mesh=mesh,
        in_specs=(P(("outer", "inner"), None), P(), P(), P(), P(), P(), P()),
        out_specs=(P(("outer", "inner"), None), P(("outer", "inner"), None)),
        check_vma=False,
    )
```

```python
import jax
import jax.numpy as jnp
from jax import lax
from jax.experimental import pallas as pl
from jax.experimental.pallas import tpu as pltpu
from jax.sharding import PartitionSpec as P

HEAD_DIM = 64
POOL = 128
GROUPS = 8
MEMBERS = 8
HALO = 3
CHUNKS = 8
IN_FLIGHT = 3
HELD = 2
AHEAD = 2
COLUMNS = 256
PAIR = 2 * HEAD_DIM
MESH = pl.DeviceIdType.MESH
F32, BF16 = jnp.float32, jnp.bfloat16


def gelu(x):
    return 0.5 * x * (1.0 + lax.erf(x * (0.5**0.5)))


def dot(left, right):
    return jnp.dot(left, right, preferred_element_type=F32)


def thirds(value):
    high = value.astype(BF16)
    rest = value - high.astype(F32)
    middle = rest.astype(BF16)
    return high, middle, (rest - middle.astype(F32)).astype(BF16)


def widened(value, weight):
    high, middle, low = thirds(value)
    return (dot(low, weight) + dot(middle, weight)) + dot(high, weight)


def swapped(member, outer):
    return member // 2 * 2 + (member + outer // 4) % 2


def tower_kernel(
    stem, weight, bias, query_weight, key_weight, value_weight, output_weight,
    tower, attended,
    rows_in, rows_out, taps, active, second, field, everyone, mixed, heads_weight,
    weight_sem, heads_sem, in_send, in_recv, halo_send, halo_recv, out_send, out_recv,
    pool_send, pool_recv, share_send, share_recv,
):
    outer, inner = lax.axis_index("outer"), lax.axis_index("inner")
    member, core = inner // 2, inner % 2
    chans = stem.shape[1]
    part = stem.shape[0] // MEMBERS
    rows = part // CHUNKS
    mine = swapped(member, outer)
    up, down = (outer + 1) % GROUPS, (outer + GROUPS - 1) % GROUPS
    neighbours = (
        (up, 2 * swapped(mine, up) + core),
        (down, 2 * swapped(mine, down) + core),
    )

    def other(step):
        return (member // 2 + step // 2) % 4 * 2 + (member + step) % 2

    barrier = pltpu.get_barrier_semaphore()

    def greet(device):
        pl.semaphore_signal(barrier, inc=1, device_id=device, device_id_type=MESH)

    for step in range(1, MEMBERS):
        greet((outer, 2 * other(step) + core))
    greet((outer, inner + 1 - 2 * core))
    for neighbour in neighbours:
        greet(neighbour)

    def load_taps(layer, tap, half):
        return pltpu.make_async_copy(
            weight.at[layer, tap],
            taps.at[layer, tap, pl.ds(half * chans, chans)],
            weight_sem.at[layer, tap, half],
        )

    def load_heads(k):
        source = (query_weight, key_weight, value_weight, output_weight)[k]
        return pltpu.make_async_copy(source, heads_weight.at[k], heads_sem.at[k])

    every_tap = [(layer, tap, half) for layer in range(2) for tap in range(3) for half in range(2)]
    for which in every_tap:
        load_taps(*which).start()
    for k in range(4):
        load_heads(k).start()

    pl.semaphore_wait(barrier, MEMBERS + len(neighbours))

    def span(chunk):
        return pl.ds(pl.multiple_of(chunk * rows, rows), rows)

    def piece(index, chunk):
        return pl.ds(pl.multiple_of(index * part + chunk * rows, rows), rows)

    def send_in(chunk, step):
        to = other(step)
        return pltpu.make_async_remote_copy(
            src_ref=stem.at[piece(swapped(to, outer), chunk)],
            dst_ref=rows_in.at[HALO + member, span(chunk)],
            send_sem=in_send.at[chunk, step],
            recv_sem=in_recv.at[chunk, member],
            device_id=(outer, 2 * to + core),
            device_id_type=MESH,
        )

    def keep_in(chunk):
        return pltpu.make_async_copy(
            stem.at[piece(mine, chunk)], rows_in.at[HALO + member, span(chunk)], in_recv.at[chunk, member]
        )

    def arrived(chunk, block):
        there = rows_in.at[HALO + block, span(chunk)]
        return pltpu.make_async_copy(there, there, in_recv.at[chunk, block])

    def send_halo(chunk, side):
        return pltpu.make_async_remote_copy(
            src_ref=rows_in.at[pl.ds(MEMBERS if side == 0 else HALO, HALO), span(chunk)],
            dst_ref=rows_in.at[pl.ds(0 if side == 0 else HALO + MEMBERS, HALO), span(chunk)],
            send_sem=halo_send.at[chunk, side],
            recv_sem=halo_recv.at[chunk, side],
            device_id=neighbours[side],
            device_id_type=MESH,
        )

    def send_out(chunk, step):
        to = other(step)
        return pltpu.make_async_remote_copy(
            src_ref=rows_out.at[to, span(chunk)],
            dst_ref=tower.at[piece(mine, chunk)],
            send_sem=out_send.at[chunk, step],
            recv_sem=out_recv.at[chunk, mine],
            device_id=(outer, 2 * to + core),
            device_id_type=MESH,
        )

    def keep_out(chunk):
        return pltpu.make_async_copy(
            rows_out.at[member, span(chunk)], tower.at[piece(mine, chunk)], out_recv.at[chunk, mine]
        )

    def returned(chunk, index):
        there = tower.at[piece(index, chunk)]
        return pltpu.make_async_copy(there, there, out_recv.at[chunk, index])

    def start_in(chunk):
        keep_in(chunk).start()
        for step in range(1, MEMBERS):
            send_in(chunk, step).start()

    def start_out(chunk):
        keep_out(chunk).start()
        for step in range(1, MEMBERS):
            send_out(chunk, step).start()

    def forward(chunk):
        for block in range(MEMBERS - HALO, MEMBERS):
            arrived(chunk, block).wait()
        send_halo(chunk, 0).start()
        for block in range(HALO):
            arrived(chunk, block).wait()
        send_halo(chunk, 1).start()
        for block in range(HALO, MEMBERS - HALO):
            arrived(chunk, block).wait()

    def split(value, into, first, columns=slice(0, 768)):
        high = value.astype(BF16)
        count, start, stop = value.shape[0], columns.start, columns.stop
        into[first : first + count, start:stop] = high
        into[first : first + count, chans + start : chans + stop] = (value - high.astype(F32)).astype(BF16)

    def inside(block):
        if 0 <= block < MEMBERS:
            return 1.0
        number = outer * MEMBERS + block
        return ((number >= 0) & (number < GROUPS * MEMBERS)).astype(F32)

    def conv(source, layer, spread, blocks, columns):
        total = bias[layer : layer + 1, columns]
        for tap in range(3):
            first = tap * spread * rows
            total = total + dot(source[first : first + blocks * rows, :], taps[layer, tap, :, columns])
        return total

    tiles = [slice(start, start + COLUMNS) for start in range(0, chans, COLUMNS)]

    def compute(chunk):
        for block in range(MEMBERS + 2 * HALO):
            split(gelu(rows_in[block, span(chunk)]) * inside(block - HALO), active, block * rows)
        for columns in tiles:
            result = conv(active, 0, 1, MEMBERS + 4, columns)
            for block in range(MEMBERS + 4):
                at = slice(block * rows, (block + 1) * rows)
                total = rows_in[block + 1, span(chunk), columns] + result[at]
                field[at, columns] = total
                split(gelu(total) * inside(block - 2), second, block * rows, columns)
        for columns in tiles:
            result = conv(second, 1, 2, MEMBERS, columns)
            for block in range(MEMBERS):
                at = slice(block * rows, (block + 1) * rows)
                before = field[(block + 2) * rows : (block + 3) * rows, columns]
                rows_out[block, span(chunk), columns] = before + result[at]

    def shelf(run, whose):
        return pl.multiple_of((run * 2 + whose) * MEMBERS * MEMBERS, MEMBERS)

    def slot(run, of):
        return pl.ds(shelf(run, core) + of * MEMBERS, MEMBERS)

    def send_pool(run, step):
        return pltpu.make_async_remote_copy(
            src_ref=everyone.at[slot(run, member)],
            dst_ref=everyone.at[slot(run, member)],
            send_sem=pool_send.at[run, step],
            recv_sem=pool_recv.at[run, member],
            device_id=(outer, 2 * other(step) + core),
            device_id_type=MESH,
        )

    def share(run):
        half = pl.ds(shelf(run, core), MEMBERS * MEMBERS)
        return pltpu.make_async_remote_copy(
            src_ref=everyone.at[half],
            dst_ref=everyone.at[half],
            send_sem=share_send.at[run],
            recv_sem=share_recv.at[run],
            device_id=(outer, inner + 1 - 2 * core),
            device_id_type=MESH,
        )

    def start_pool(run):
        everyone[slot(run, member), :] = jnp.concatenate(
            [
                jnp.sum(rows_out[block, run * POOL : (run + 1) * POOL], axis=0, keepdims=True) * (1.0 / POOL)
                for block in range(MEMBERS)
            ],
            axis=0,
        )
        for step in range(1, MEMBERS):
            send_pool(run, step).start()

    def start_share(run):
        for step in range(1, MEMBERS):
            there = everyone.at[slot(run, other(step))]
            pltpu.make_async_copy(there, there, pool_recv.at[run, other(step)]).wait()
        share(run).start()

    def finish_share(run):
        there = everyone.at[pl.ds(shelf(run, 1 - core), MEMBERS * MEMBERS)]
        pltpu.make_async_copy(there, there, share_recv.at[run]).wait()

    for chunk in range(IN_FLIGHT):
        start_in(chunk)
    for chunk in range(AHEAD):
        forward(chunk)
        start_in(chunk + IN_FLIGHT)
    for which in every_tap:
        load_taps(*which).wait()

    def step_of(chunk, _):
        @pl.when(chunk + AHEAD < CHUNKS)
        def _():
            forward(chunk + AHEAD)

        @pl.when(chunk + AHEAD + IN_FLIGHT < CHUNKS)
        def _():
            start_in(chunk + AHEAD + IN_FLIGHT)

        for side in range(2):
            send_halo(chunk, side).wait_recv()
        compute(chunk)

        @pl.when(chunk == CHUNKS // 2 - 1)
        def _():
            start_pool(0)

        @pl.when(chunk == CHUNKS // 2 + 1)
        def _():
            start_share(0)

        @pl.when(chunk == CHUNKS - 1)
        def _():
            start_pool(1)

        @pl.when(chunk >= HELD)
        def _():
            start_out(chunk - HELD)

        return 0

    lax.fori_loop(0, CHUNKS, step_of, 0)
    start_share(1)
    for chunk in range(CHUNKS - HELD, CHUNKS):
        start_out(chunk)
    for k in range(4):
        load_heads(k).wait()
    finish_share(0)
    finish_share(1)
    count = MEMBERS * (part // POOL)
    runs = part // POOL
    total = 2 * MEMBERS * count
    parts = thirds(everyone[...])
    place = lax.broadcasted_iota(jnp.int32, (count, total), 0)
    wanted = ((place % runs * 2 + core) * MEMBERS + swapped(place // runs, outer)) * MEMBERS + member
    chosen = (lax.broadcasted_iota(jnp.int32, (count, total), 1) == wanted).astype(F32).astype(BF16)
    own = (dot(chosen, parts[2]) + dot(chosen, parts[1])) + dot(chosen, parts[0])
    lanes = lax.broadcasted_iota(jnp.int32, (1, PAIR), 1)

    def two_heads(pair, _):
        columns = pl.ds(pl.multiple_of(pair * PAIR, PAIR), PAIR)
        queries = widened(own, heads_weight[0, :, columns]) * (HEAD_DIM**-0.5)
        keys = widened(everyone[...], heads_weight[1, :, columns])
        vals = widened(everyone[...], heads_weight[2, :, columns])
        both = jnp.zeros((count, PAIR), F32)
        for half in range(2):
            mask = (lanes // HEAD_DIM == half).astype(F32)
            scores = lax.dot_general(
                queries * mask,
                keys,
                (((1,), (1,)), ((), ())),
                precision=lax.Precision.HIGHEST,
                preferred_element_type=F32,
            )
            powers = jnp.exp(scores - jnp.max(scores, axis=1, keepdims=True))
            probs = powers / jnp.sum(powers, axis=1, keepdims=True)
            both = both + mask * jnp.dot(
                probs, vals, precision=lax.Precision.HIGHEST, preferred_element_type=F32
            )
        mixed[:, columns] = both
        return 0

    lax.fori_loop(0, chans // PAIR, two_heads, 0)
    attended[...] = own + widened(mixed[...], heads_weight[3])

    for run in range(runs):
        share(run).wait_send()
        for step in range(1, MEMBERS):
            send_pool(run, step).wait_send()

    def finish(chunk, _):
        for side in range(2):
            send_halo(chunk, side).wait_send()
        for step in range(1, MEMBERS):
            send_in(chunk, step).wait_send()
            send_out(chunk, step).wait_send()
        for index in range(MEMBERS):
            returned(chunk, index).wait()
        return 0

    lax.fori_loop(0, CHUNKS, finish, 0)


def shards(stem_activity, convolution_weight, convolution_bias, query_weight, key_weight, value_weight, output_weight):
    length, chans = stem_activity.shape
    part = length // MEMBERS
    rows = part // CHUNKS
    blocks = MEMBERS + 2 * HALO
    pooled = length // POOL
    dma, vmem = pltpu.SemaphoreType.DMA, pltpu.VMEM
    far, on_core = pl.BlockSpec(memory_space=pltpu.HBM), pl.BlockSpec(memory_space=vmem)
    return pl.pallas_call(
        tower_kernel,
        out_shape=(
            vmem((length, chans), F32),
            jax.ShapeDtypeStruct((pooled, chans), F32),
        ),
        in_specs=[far, far, on_core, far, far, far, far],
        out_specs=(on_core, on_core),
        scratch_shapes=[
            vmem((blocks, part, chans), F32),
            vmem((MEMBERS, part, chans), F32),
            vmem((2, 3, 2 * chans, chans), BF16),
            vmem((blocks * rows, 2 * chans), BF16),
            vmem(((blocks - 2) * rows, 2 * chans), BF16),
            vmem(((blocks - 2) * rows, chans), F32),
            vmem((2 * MEMBERS * pooled, chans), F32),
            vmem((pooled, chans), F32),
            vmem((4, chans, chans), BF16),
            dma((2, 3, 2)),
            dma((4,)),
            dma((CHUNKS, MEMBERS)),
            dma((CHUNKS, MEMBERS)),
            dma((CHUNKS, 2)),
            dma((CHUNKS, 2)),
            dma((CHUNKS, MEMBERS)),
            dma((CHUNKS, MEMBERS)),
            dma((2, MEMBERS)),
            dma((2, MEMBERS)),
            dma((2,)),
            dma((2,)),
        ],
        compiler_params=pltpu.CompilerParams(
            collective_id=0, has_side_effects=True, vmem_limit_bytes=50 * 1024 * 1024
        ),
        cost_estimate=pl.CostEstimate(
            flops=5 * 2 * 2 * 3 * length * chans * chans, bytes_accessed=8 * length * chans, transcendentals=0
        ),
        name="tower",
    )(
        stem_activity, convolution_weight, convolution_bias,
        query_weight, key_weight, value_weight, output_weight,
    )


def solution(mesh):
    return jax.shard_map(
        shards,
        mesh=mesh,
        in_specs=(P(("outer", "inner"), None), P(), P(), P(), P(), P(), P()),
        out_specs=(P(("outer", "inner"), None), P(("outer", "inner"), None)),
        check_vma=False,
    )
```

```python
import jax
import jax.numpy as jnp
from jax import lax
from jax.experimental import pallas as pl
from jax.experimental.pallas import tpu as pltpu
from jax.sharding import PartitionSpec as P

HEAD_DIM = 64
POOL = 128
GROUPS = 8
MEMBERS = 8
HALO = 3
CHUNKS = 8
IN_FLIGHT = 3
HELD = 2
AHEAD = 1
COLUMNS = 256
HEADS_AT_ONCE = 4
MESH = pl.DeviceIdType.MESH
F32, BF16 = jnp.float32, jnp.bfloat16


def gelu(x):
    return 0.5 * x * (1.0 + lax.erf(x * (0.5**0.5)))


def dot(left, right):
    return jnp.dot(left, right, preferred_element_type=F32)


def thirds(value):
    high = value.astype(BF16)
    rest = value - high.astype(F32)
    middle = rest.astype(BF16)
    return high, middle, (rest - middle.astype(F32)).astype(BF16)


def swapped(member, outer):
    return member // 2 * 2 + (member + outer // 4) % 2


def tower_kernel(
    stem, weight, bias, query_weight, key_weight, value_weight, output_weight,
    tower, attended,
    rows_in, rows_out, taps, active, second, field, everyone, split_rows, mixed, heads_weight,
    weight_sem, heads_sem, in_send, in_recv, halo_send, halo_recv, out_send, out_recv,
    pool_send, pool_recv, share_send, share_recv,
):
    outer, inner = lax.axis_index("outer"), lax.axis_index("inner")
    member, core = inner // 2, inner % 2
    chans = stem.shape[1]
    part = stem.shape[0] // MEMBERS
    rows = part // CHUNKS
    mine = swapped(member, outer)
    up, down = (outer + 1) % GROUPS, (outer + GROUPS - 1) % GROUPS
    neighbours = (
        (up, 2 * swapped(mine, up) + core),
        (down, 2 * swapped(mine, down) + core),
    )

    def other(step):
        return (member // 2 + step // 2) % 4 * 2 + (member + step) % 2

    barrier = pltpu.get_barrier_semaphore()

    def greet(device):
        pl.semaphore_signal(barrier, inc=1, device_id=device, device_id_type=MESH)

    for step in range(1, MEMBERS):
        greet((outer, 2 * other(step) + core))
    greet((outer, inner + 1 - 2 * core))
    for neighbour in neighbours:
        greet(neighbour)

    def load_taps(layer, tap, half):
        return pltpu.make_async_copy(
            weight.at[layer, tap],
            taps.at[layer, tap, pl.ds(half * chans, chans)],
            weight_sem.at[layer, tap, half],
        )

    def load_heads(k):
        source = (query_weight, key_weight, value_weight, output_weight)[k]
        return pltpu.make_async_copy(source, heads_weight.at[k], heads_sem.at[k])

    every_tap = [(layer, tap, half) for layer in range(2) for tap in range(3) for half in range(2)]
    for which in every_tap:
        load_taps(*which).start()
    for k in range(4):
        load_heads(k).start()

    pl.semaphore_wait(barrier, MEMBERS + len(neighbours))

    def span(chunk):
        return pl.ds(pl.multiple_of(chunk * rows, rows), rows)

    def piece(index, chunk):
        return pl.ds(pl.multiple_of(index * part + chunk * rows, rows), rows)

    def send_in(chunk, step):
        to = other(step)
        return pltpu.make_async_remote_copy(
            src_ref=stem.at[piece(swapped(to, outer), chunk)],
            dst_ref=rows_in.at[HALO + member, span(chunk)],
            send_sem=in_send.at[chunk, step],
            recv_sem=in_recv.at[chunk, member],
            device_id=(outer, 2 * to + core),
            device_id_type=MESH,
        )

    def keep_in(chunk):
        return pltpu.make_async_copy(
            stem.at[piece(mine, chunk)], rows_in.at[HALO + member, span(chunk)], in_recv.at[chunk, member]
        )

    def arrived(chunk, block):
        there = rows_in.at[HALO + block, span(chunk)]
        return pltpu.make_async_copy(there, there, in_recv.at[chunk, block])

    def send_halo(chunk, side):
        return pltpu.make_async_remote_copy(
            src_ref=rows_in.at[pl.ds(MEMBERS if side == 0 else HALO, HALO), span(chunk)],
            dst_ref=rows_in.at[pl.ds(0 if side == 0 else HALO + MEMBERS, HALO), span(chunk)],
            send_sem=halo_send.at[chunk, side],
            recv_sem=halo_recv.at[chunk, side],
            device_id=neighbours[side],
            device_id_type=MESH,
        )

    def send_out(chunk, step):
        to = other(step)
        return pltpu.make_async_remote_copy(
            src_ref=rows_out.at[to, span(chunk)],
            dst_ref=tower.at[piece(mine, chunk)],
            send_sem=out_send.at[chunk, step],
            recv_sem=out_recv.at[chunk, mine],
            device_id=(outer, 2 * to + core),
            device_id_type=MESH,
        )

    def keep_out(chunk):
        return pltpu.make_async_copy(
            rows_out.at[member, span(chunk)], tower.at[piece(mine, chunk)], out_recv.at[chunk, mine]
        )

    def returned(chunk, index):
        there = tower.at[piece(index, chunk)]
        return pltpu.make_async_copy(there, there, out_recv.at[chunk, index])

    def start_in(chunk):
        keep_in(chunk).start()
        for step in range(1, MEMBERS):
            send_in(chunk, step).start()

    def start_out(chunk):
        keep_out(chunk).start()
        for step in range(1, MEMBERS):
            send_out(chunk, step).start()

    def forward(chunk):
        for block in range(MEMBERS - HALO, MEMBERS):
            arrived(chunk, block).wait()
        send_halo(chunk, 0).start()
        for block in range(HALO):
            arrived(chunk, block).wait()
        send_halo(chunk, 1).start()
        for block in range(HALO, MEMBERS - HALO):
            arrived(chunk, block).wait()

    def split(value, into, first, columns=slice(0, 768)):
        high = value.astype(BF16)
        count, start, stop = value.shape[0], columns.start, columns.stop
        into[first : first + count, start:stop] = high
        into[first : first + count, chans + start : chans + stop] = (value - high.astype(F32)).astype(BF16)

    def inside(block):
        if 0 <= block < MEMBERS:
            return 1.0
        number = outer * MEMBERS + block
        return ((number >= 0) & (number < GROUPS * MEMBERS)).astype(F32)

    def conv(source, layer, spread, blocks, columns):
        total = bias[layer : layer + 1, columns]
        for tap in range(3):
            first = tap * spread * rows
            total = total + dot(source[first : first + blocks * rows, :], taps[layer, tap, :, columns])
        return total

    tiles = [slice(start, start + COLUMNS) for start in range(0, chans, COLUMNS)]

    def activate(chunk, blocks):
        for block in blocks:
            split(gelu(rows_in[block, span(chunk)]) * inside(block - HALO), active, block * rows)

    def first_layer(chunk):
        for columns in tiles:
            result = conv(active, 0, 1, MEMBERS + 4, columns)
            for block in range(MEMBERS + 4):
                at = slice(block * rows, (block + 1) * rows)
                total = rows_in[block + 1, span(chunk), columns] + result[at]
                field[at, columns] = total
                split(gelu(total) * inside(block - 2), second, block * rows, columns)

    def second_layer(chunk, columns):
        result = conv(second, 1, 2, MEMBERS, columns)
        for block in range(MEMBERS):
            before = field[(block + 2) * rows : (block + 3) * rows, columns]
            rows_out[block, span(chunk), columns] = before + result[block * rows : (block + 1) * rows]

    def shelf(run, whose):
        return pl.multiple_of((run * 2 + whose) * MEMBERS * MEMBERS, MEMBERS)

    def slot(run, of):
        return pl.ds(shelf(run, core) + of * MEMBERS, MEMBERS)

    def send_pool(run, step):
        return pltpu.make_async_remote_copy(
            src_ref=everyone.at[slot(run, member)],
            dst_ref=everyone.at[slot(run, member)],
            send_sem=pool_send.at[run, step],
            recv_sem=pool_recv.at[run, member],
            device_id=(outer, 2 * other(step) + core),
            device_id_type=MESH,
        )

    def share(run):
        half = pl.ds(shelf(run, core), MEMBERS * MEMBERS)
        return pltpu.make_async_remote_copy(
            src_ref=everyone.at[half],
            dst_ref=everyone.at[half],
            send_sem=share_send.at[run],
            recv_sem=share_recv.at[run],
            device_id=(outer, inner + 1 - 2 * core),
            device_id_type=MESH,
        )

    def start_pool(run):
        everyone[slot(run, member), :] = jnp.concatenate(
            [
                jnp.sum(rows_out[block, run * POOL : (run + 1) * POOL], axis=0, keepdims=True) * (1.0 / POOL)
                for block in range(MEMBERS)
            ],
            axis=0,
        )
        for step in range(1, MEMBERS):
            send_pool(run, step).start()

    def start_share(run):
        for step in range(1, MEMBERS):
            there = everyone.at[slot(run, other(step))]
            pltpu.make_async_copy(there, there, pool_recv.at[run, other(step)]).wait()
        share(run).start()

    def finish_share(run):
        there = everyone.at[pl.ds(shelf(run, 1 - core), MEMBERS * MEMBERS)]
        pltpu.make_async_copy(there, there, share_recv.at[run]).wait()

    def bring(chunk):
        @pl.when(chunk + AHEAD < CHUNKS)
        def _():
            forward(chunk + AHEAD)

        @pl.when(chunk + AHEAD + IN_FLIGHT < CHUNKS)
        def _():
            start_in(chunk + AHEAD + IN_FLIGHT)

        for side in range(2):
            send_halo(chunk, side).wait_recv()

    blocks = range(MEMBERS + 2 * HALO)
    for chunk in range(IN_FLIGHT):
        start_in(chunk)
    for chunk in range(AHEAD):
        forward(chunk)
        start_in(chunk + IN_FLIGHT)
    bring(0)
    activate(0, blocks)
    for which in every_tap:
        load_taps(*which).wait()
    first_layer(0)

    def step_of(chunk, _):
        bring(chunk)
        for k, columns in enumerate(tiles):
            second_layer(chunk - 1, columns)
            activate(chunk, blocks[k :: len(tiles)])
        first_layer(chunk)

        @pl.when(chunk > HELD)
        def _():
            start_out(chunk - 1 - HELD)

        @pl.when(chunk == CHUNKS // 2)
        def _():
            start_pool(0)

        @pl.when(chunk == CHUNKS // 2 + 2)
        def _():
            start_share(0)

        return 0

    lax.fori_loop(1, CHUNKS, step_of, 0)
    for columns in tiles:
        second_layer(CHUNKS - 1, columns)
    start_pool(1)
    start_out(CHUNKS - 1 - HELD)
    start_share(1)
    for chunk in range(CHUNKS - HELD, CHUNKS):
        start_out(chunk)
    for k in range(4):
        load_heads(k).wait()
    finish_share(0)
    finish_share(1)

    runs = part // POOL
    count = MEMBERS * runs
    total = 2 * MEMBERS * count
    for k, third in enumerate(thirds(everyone[...])):
        split_rows[k * total : (k + 1) * total, :] = third

    def stacked(value, weight):
        size = value.shape[0] // 3
        result = dot(value, weight)
        return (result[2 * size :] + result[size : 2 * size]) + result[:size]

    place = lax.broadcasted_iota(jnp.int32, (count, total), 0)
    wanted = ((place % runs * 2 + core) * MEMBERS + swapped(place // runs, outer)) * MEMBERS + member
    chosen = (lax.broadcasted_iota(jnp.int32, (count, total), 1) == wanted).astype(F32).astype(BF16)
    own_parts = [dot(chosen, split_rows[k * total : (k + 1) * total, :]) for k in range(3)]
    own = (own_parts[2] + own_parts[1]) + own_parts[0]
    own_rows = jnp.concatenate([value.astype(BF16) for value in own_parts], axis=0)
    width = HEADS_AT_ONCE * HEAD_DIM
    head = lax.broadcasted_iota(jnp.int32, (1, width), 1) // HEAD_DIM
    masks = [(head == k).astype(F32) for k in range(HEADS_AT_ONCE)]

    for start in range(0, chans, width):
        columns = slice(start, start + width)
        queries = stacked(own_rows, heads_weight[0, :, columns]) * (HEAD_DIM**-0.5)
        keys = stacked(split_rows[...], heads_weight[1, :, columns])
        vals = stacked(split_rows[...], heads_weight[2, :, columns])
        scores = lax.dot_general(
            jnp.concatenate([queries * mask for mask in masks], axis=0),
            keys,
            (((1,), (1,)), ((), ())),
            precision=lax.Precision.HIGHEST,
            preferred_element_type=F32,
        )
        powers = jnp.exp(scores - jnp.max(scores, axis=1, keepdims=True))
        probs = powers / jnp.sum(powers, axis=1, keepdims=True)
        each = jnp.dot(probs, vals, precision=lax.Precision.HIGHEST, preferred_element_type=F32)
        mixed[:, columns] = sum(each[k * count : (k + 1) * count] * mask for k, mask in enumerate(masks))

    attended[...] = own + stacked(jnp.concatenate(thirds(mixed[...]), axis=0), heads_weight[3])

    for run in range(runs):
        share(run).wait_send()
        for step in range(1, MEMBERS):
            send_pool(run, step).wait_send()

    def finish(chunk, _):
        for side in range(2):
            send_halo(chunk, side).wait_send()
        for step in range(1, MEMBERS):
            send_in(chunk, step).wait_send()
            send_out(chunk, step).wait_send()
        for index in range(MEMBERS):
            returned(chunk, index).wait()
        return 0

    lax.fori_loop(0, CHUNKS, finish, 0)


def shards(stem_activity, convolution_weight, convolution_bias, query_weight, key_weight, value_weight, output_weight):
    length, chans = stem_activity.shape
    part = length // MEMBERS
    rows = part // CHUNKS
    blocks = MEMBERS + 2 * HALO
    pooled = length // POOL
    dma, vmem = pltpu.SemaphoreType.DMA, pltpu.VMEM
    far, on_core = pl.BlockSpec(memory_space=pltpu.HBM), pl.BlockSpec(memory_space=vmem)
    return pl.pallas_call(
        tower_kernel,
        out_shape=(
            vmem((length, chans), F32),
            jax.ShapeDtypeStruct((pooled, chans), F32),
        ),
        in_specs=[far, far, on_core, far, far, far, far],
        out_specs=(on_core, on_core),
        scratch_shapes=[
            vmem((blocks, part, chans), F32),
            vmem((MEMBERS, part, chans), F32),
            vmem((2, 3, 2 * chans, chans), BF16),
            vmem((blocks * rows, 2 * chans), BF16),
            vmem(((blocks - 2) * rows, 2 * chans), BF16),
            vmem(((blocks - 2) * rows, chans), F32),
            vmem((2 * MEMBERS * pooled, chans), F32),
            vmem((3 * 2 * MEMBERS * pooled, chans), BF16),
            vmem((pooled, chans), F32),
            vmem((4, chans, chans), BF16),
            dma((2, 3, 2)),
            dma((4,)),
            dma((CHUNKS, MEMBERS)),
            dma((CHUNKS, MEMBERS)),
            dma((CHUNKS, 2)),
            dma((CHUNKS, 2)),
            dma((CHUNKS, MEMBERS)),
            dma((CHUNKS, MEMBERS)),
            dma((2, MEMBERS)),
            dma((2, MEMBERS)),
            dma((2,)),
            dma((2,)),
        ],
        compiler_params=pltpu.CompilerParams(
            collective_id=0, has_side_effects=True, vmem_limit_bytes=50 * 1024 * 1024
        ),
        cost_estimate=pl.CostEstimate(
            flops=5 * 2 * 2 * 3 * length * chans * chans, bytes_accessed=8 * length * chans, transcendentals=0
        ),
        name="tower",
    )(
        stem_activity, convolution_weight, convolution_bias,
        query_weight, key_weight, value_weight, output_weight,
    )


def solution(mesh):
    return jax.shard_map(
        shards,
        mesh=mesh,
        in_specs=(P(("outer", "inner"), None), P(), P(), P(), P(), P(), P()),
        out_specs=(P(("outer", "inner"), None), P(("outer", "inner"), None)),
        check_vma=False,
    )
```

```python
import jax
import jax.numpy as jnp
from jax import lax
from jax.experimental import pallas as pl
from jax.experimental.pallas import tpu as pltpu
from jax.sharding import PartitionSpec as P

HEAD_DIM = 64
POOL = 128
GROUPS = 8
MEMBERS = 8
HALO = 3
CHUNKS = 8
IN_FLIGHT = 3
HELD = 2
AHEAD = 1
COLUMNS = 256
ORDER = (1, 2, 6, 5, 4, 3, 7)
HEADS_AT_ONCE = 4
MESH = pl.DeviceIdType.MESH
F32, BF16 = jnp.float32, jnp.bfloat16


def gelu(x):
    return 0.5 * x * (1.0 + lax.erf(x * (0.5**0.5)))


def dot(left, right):
    return jnp.dot(left, right, preferred_element_type=F32)


def thirds(value):
    high = value.astype(BF16)
    rest = value - high.astype(F32)
    middle = rest.astype(BF16)
    return high, middle, (rest - middle.astype(F32)).astype(BF16)


def swapped(member, outer):
    return member // 2 * 2 + (member + outer // 4) % 2


def tower_kernel(
    stem, weight, bias, query_weight, key_weight, value_weight, output_weight,
    tower, attended,
    rows_in, rows_out, taps, active, second, field, everyone, split_rows, mixed, heads_weight,
    weight_sem, heads_sem, in_send, in_recv, halo_send, halo_recv, out_send, out_recv,
    pool_send, pool_recv, share_send, share_recv,
):
    outer, inner = lax.axis_index("outer"), lax.axis_index("inner")
    member, core = inner // 2, inner % 2
    chans = stem.shape[1]
    part = stem.shape[0] // MEMBERS
    rows = part // CHUNKS
    mine = swapped(member, outer)
    up, down = (outer + 1) % GROUPS, (outer + GROUPS - 1) % GROUPS
    neighbours = (
        (up, 2 * swapped(mine, up) + core),
        (down, 2 * swapped(mine, down) + core),
    )

    def other(step):
        way = step // 2
        return (member // 2 + way + core * (4 - 2 * way)) % 4 * 2 + (member + step) % 2

    barrier = pltpu.get_barrier_semaphore()

    def greet(device):
        pl.semaphore_signal(barrier, inc=1, device_id=device, device_id_type=MESH)

    for step in range(1, MEMBERS):
        greet((outer, 2 * other(step) + core))
    greet((outer, inner + 1 - 2 * core))
    for neighbour in neighbours:
        greet(neighbour)

    def load_taps(layer, tap, half):
        return pltpu.make_async_copy(
            weight.at[layer, tap],
            taps.at[layer, tap, pl.ds(half * chans, chans)],
            weight_sem.at[layer, tap, half],
        )

    def load_heads(k):
        source = (query_weight, key_weight, value_weight, output_weight)[k]
        return pltpu.make_async_copy(source, heads_weight.at[k], heads_sem.at[k])

    every_tap = [(layer, tap, half) for layer in range(2) for tap in range(3) for half in range(2)]
    for which in every_tap:
        load_taps(*which).start()
    for k in range(4):
        load_heads(k).start()

    pl.semaphore_wait(barrier, MEMBERS + len(neighbours))

    def span(chunk):
        return pl.ds(pl.multiple_of(chunk * rows, rows), rows)

    def piece(index, chunk):
        return pl.ds(pl.multiple_of(index * part + chunk * rows, rows), rows)

    def send_in(chunk, step):
        to = other(step)
        return pltpu.make_async_remote_copy(
            src_ref=stem.at[piece(swapped(to, outer), chunk)],
            dst_ref=rows_in.at[HALO + member, span(chunk)],
            send_sem=in_send.at[chunk, step],
            recv_sem=in_recv.at[chunk, member],
            device_id=(outer, 2 * to + core),
            device_id_type=MESH,
        )

    def keep_in(chunk):
        return pltpu.make_async_copy(
            stem.at[piece(mine, chunk)], rows_in.at[HALO + member, span(chunk)], in_recv.at[chunk, member]
        )

    def arrived(chunk, block):
        there = rows_in.at[HALO + block, span(chunk)]
        return pltpu.make_async_copy(there, there, in_recv.at[chunk, block])

    def send_halo(chunk, side):
        return pltpu.make_async_remote_copy(
            src_ref=rows_in.at[pl.ds(MEMBERS if side == 0 else HALO, HALO), span(chunk)],
            dst_ref=rows_in.at[pl.ds(0 if side == 0 else HALO + MEMBERS, HALO), span(chunk)],
            send_sem=halo_send.at[chunk, side],
            recv_sem=halo_recv.at[chunk, side],
            device_id=neighbours[side],
            device_id_type=MESH,
        )

    def send_out(chunk, step):
        to = other(step)
        return pltpu.make_async_remote_copy(
            src_ref=rows_out.at[to, span(chunk)],
            dst_ref=tower.at[piece(mine, chunk)],
            send_sem=out_send.at[chunk, step],
            recv_sem=out_recv.at[chunk, mine],
            device_id=(outer, 2 * to + core),
            device_id_type=MESH,
        )

    def keep_out(chunk):
        return pltpu.make_async_copy(
            rows_out.at[member, span(chunk)], tower.at[piece(mine, chunk)], out_recv.at[chunk, mine]
        )

    def returned(chunk, index):
        there = tower.at[piece(index, chunk)]
        return pltpu.make_async_copy(there, there, out_recv.at[chunk, index])

    def start_in(chunk):
        keep_in(chunk).start()
        for step in ORDER:
            send_in(chunk, step).start()

    def start_out(chunk):
        keep_out(chunk).start()
        for step in ORDER:
            send_out(chunk, step).start()

    def forward(chunk):
        for block in range(MEMBERS - HALO, MEMBERS):
            arrived(chunk, block).wait()
        send_halo(chunk, 0).start()
        for block in range(HALO):
            arrived(chunk, block).wait()
        send_halo(chunk, 1).start()
        for block in range(HALO, MEMBERS - HALO):
            arrived(chunk, block).wait()

    def split(value, into, first, columns=slice(0, 768)):
        high = value.astype(BF16)
        count, start, stop = value.shape[0], columns.start, columns.stop
        into[first : first + count, start:stop] = high
        into[first : first + count, chans + start : chans + stop] = (value - high.astype(F32)).astype(BF16)

    def inside(block):
        if 0 <= block < MEMBERS:
            return 1.0
        number = outer * MEMBERS + block
        return ((number >= 0) & (number < GROUPS * MEMBERS)).astype(F32)

    def conv(source, layer, spread, blocks, columns):
        total = bias[layer : layer + 1, columns]
        for tap in range(3):
            first = tap * spread * rows
            total = total + dot(source[first : first + blocks * rows, :], taps[layer, tap, :, columns])
        return total

    tiles = [slice(start, start + COLUMNS) for start in range(0, chans, COLUMNS)]

    def activate(chunk, blocks):
        for block in blocks:
            split(gelu(rows_in[block, span(chunk)]) * inside(block - HALO), active, block * rows)

    def first_layer(chunk):
        for columns in tiles:
            result = conv(active, 0, 1, MEMBERS + 4, columns)
            for block in range(MEMBERS + 4):
                at = slice(block * rows, (block + 1) * rows)
                total = rows_in[block + 1, span(chunk), columns] + result[at]
                field[at, columns] = total
                split(gelu(total) * inside(block - 2), second, block * rows, columns)

    def second_layer(chunk, columns):
        result = conv(second, 1, 2, MEMBERS, columns)
        for block in range(MEMBERS):
            before = field[(block + 2) * rows : (block + 3) * rows, columns]
            rows_out[block, span(chunk), columns] = before + result[block * rows : (block + 1) * rows]

    def shelf(run, whose):
        return pl.multiple_of((run * 2 + whose) * MEMBERS * MEMBERS, MEMBERS)

    def slot(run, of):
        return pl.ds(shelf(run, core) + of * MEMBERS, MEMBERS)

    def send_pool(run, step):
        return pltpu.make_async_remote_copy(
            src_ref=everyone.at[slot(run, member)],
            dst_ref=everyone.at[slot(run, member)],
            send_sem=pool_send.at[run, step],
            recv_sem=pool_recv.at[run, member],
            device_id=(outer, 2 * other(step) + core),
            device_id_type=MESH,
        )

    def share(run):
        half = pl.ds(shelf(run, core), MEMBERS * MEMBERS)
        return pltpu.make_async_remote_copy(
            src_ref=everyone.at[half],
            dst_ref=everyone.at[half],
            send_sem=share_send.at[run],
            recv_sem=share_recv.at[run],
            device_id=(outer, inner + 1 - 2 * core),
            device_id_type=MESH,
        )

    def start_pool(run):
        everyone[slot(run, member), :] = jnp.concatenate(
            [
                jnp.sum(rows_out[block, run * POOL : (run + 1) * POOL], axis=0, keepdims=True) * (1.0 / POOL)
                for block in range(MEMBERS)
            ],
            axis=0,
        )
        for step in range(1, MEMBERS):
            send_pool(run, step).start()

    def start_share(run):
        for step in range(1, MEMBERS):
            there = everyone.at[slot(run, other(step))]
            pltpu.make_async_copy(there, there, pool_recv.at[run, other(step)]).wait()
        share(run).start()

    def finish_share(run):
        there = everyone.at[pl.ds(shelf(run, 1 - core), MEMBERS * MEMBERS)]
        pltpu.make_async_copy(there, there, share_recv.at[run]).wait()

    def bring(chunk):
        @pl.when(chunk + AHEAD < CHUNKS)
        def _():
            forward(chunk + AHEAD)

        @pl.when(chunk + AHEAD + IN_FLIGHT < CHUNKS)
        def _():
            start_in(chunk + AHEAD + IN_FLIGHT)

        for side in range(2):
            send_halo(chunk, side).wait_recv()

    blocks = range(MEMBERS + 2 * HALO)
    for chunk in range(IN_FLIGHT):
        start_in(chunk)
    for chunk in range(AHEAD):
        forward(chunk)
        start_in(chunk + IN_FLIGHT)
    bring(0)
    activate(0, blocks)
    for which in every_tap:
        load_taps(*which).wait()
    first_layer(0)

    def step_of(chunk, _):
        bring(chunk)
        for k, columns in enumerate(tiles):
            second_layer(chunk - 1, columns)
            activate(chunk, blocks[k :: len(tiles)])
        first_layer(chunk)

        @pl.when(chunk > HELD)
        def _():
            start_out(chunk - 1 - HELD)

        @pl.when(chunk == CHUNKS // 2)
        def _():
            start_pool(0)

        @pl.when(chunk == CHUNKS // 2 + 2)
        def _():
            start_share(0)

        return 0

    lax.fori_loop(1, CHUNKS, step_of, 0)
    for columns in tiles:
        second_layer(CHUNKS - 1, columns)
    start_pool(1)
    start_out(CHUNKS - 1 - HELD)
    start_share(1)
    for chunk in range(CHUNKS - HELD, CHUNKS):
        start_out(chunk)
    for k in range(4):
        load_heads(k).wait()
    finish_share(0)
    finish_share(1)

    runs = part // POOL
    count = MEMBERS * runs
    total = 2 * MEMBERS * count
    for k, third in enumerate(thirds(everyone[...])):
        split_rows[k * total : (k + 1) * total, :] = third

    def stacked(value, weight):
        size = value.shape[0] // 3
        result = dot(value, weight)
        return (result[2 * size :] + result[size : 2 * size]) + result[:size]

    place = lax.broadcasted_iota(jnp.int32, (count, total), 0)
    wanted = ((place % runs * 2 + core) * MEMBERS + swapped(place // runs, outer)) * MEMBERS + member
    chosen = (lax.broadcasted_iota(jnp.int32, (count, total), 1) == wanted).astype(F32).astype(BF16)
    own_parts = [dot(chosen, split_rows[k * total : (k + 1) * total, :]) for k in range(3)]
    own = (own_parts[2] + own_parts[1]) + own_parts[0]
    own_rows = jnp.concatenate([value.astype(BF16) for value in own_parts], axis=0)
    width = HEADS_AT_ONCE * HEAD_DIM
    head = lax.broadcasted_iota(jnp.int32, (1, width), 1) // HEAD_DIM
    masks = [(head == k).astype(F32) for k in range(HEADS_AT_ONCE)]

    for start in range(0, chans, width):
        columns = slice(start, start + width)
        queries = stacked(own_rows, heads_weight[0, :, columns]) * (HEAD_DIM**-0.5)
        keys = stacked(split_rows[...], heads_weight[1, :, columns])
        vals = stacked(split_rows[...], heads_weight[2, :, columns])
        scores = lax.dot_general(
            jnp.concatenate([queries * mask for mask in masks], axis=0),
            keys,
            (((1,), (1,)), ((), ())),
            precision=lax.Precision.HIGHEST,
            preferred_element_type=F32,
        )
        powers = jnp.exp(scores - jnp.max(scores, axis=1, keepdims=True))
        probs = powers / jnp.sum(powers, axis=1, keepdims=True)
        each = jnp.dot(probs, vals, precision=lax.Precision.HIGHEST, preferred_element_type=F32)
        mixed[:, columns] = sum(each[k * count : (k + 1) * count] * mask for k, mask in enumerate(masks))

    attended[...] = own + stacked(jnp.concatenate(thirds(mixed[...]), axis=0), heads_weight[3])

    for run in range(runs):
        share(run).wait_send()
        for step in range(1, MEMBERS):
            send_pool(run, step).wait_send()

    def finish(chunk, _):
        for side in range(2):
            send_halo(chunk, side).wait_send()
        for step in range(1, MEMBERS):
            send_in(chunk, step).wait_send()
            send_out(chunk, step).wait_send()
        for index in range(MEMBERS):
            returned(chunk, index).wait()
        return 0

    lax.fori_loop(0, CHUNKS, finish, 0)


def shards(stem_activity, convolution_weight, convolution_bias, query_weight, key_weight, value_weight, output_weight):
    length, chans = stem_activity.shape
    part = length // MEMBERS
    rows = part // CHUNKS
    blocks = MEMBERS + 2 * HALO
    pooled = length // POOL
    dma, vmem = pltpu.SemaphoreType.DMA, pltpu.VMEM
    far, on_core = pl.BlockSpec(memory_space=pltpu.HBM), pl.BlockSpec(memory_space=vmem)
    return pl.pallas_call(
        tower_kernel,
        out_shape=(
            vmem((length, chans), F32),
            jax.ShapeDtypeStruct((pooled, chans), F32),
        ),
        in_specs=[far, far, on_core, far, far, far, far],
        out_specs=(on_core, on_core),
        scratch_shapes=[
            vmem((blocks, part, chans), F32),
            vmem((MEMBERS, part, chans), F32),
            vmem((2, 3, 2 * chans, chans), BF16),
            vmem((blocks * rows, 2 * chans), BF16),
            vmem(((blocks - 2) * rows, 2 * chans), BF16),
            vmem(((blocks - 2) * rows, chans), F32),
            vmem((2 * MEMBERS * pooled, chans), F32),
            vmem((3 * 2 * MEMBERS * pooled, chans), BF16),
            vmem((pooled, chans), F32),
            vmem((4, chans, chans), BF16),
            dma((2, 3, 2)),
            dma((4,)),
            dma((CHUNKS, MEMBERS)),
            dma((CHUNKS, MEMBERS)),
            dma((CHUNKS, 2)),
            dma((CHUNKS, 2)),
            dma((CHUNKS, MEMBERS)),
            dma((CHUNKS, MEMBERS)),
            dma((2, MEMBERS)),
            dma((2, MEMBERS)),
            dma((2,)),
            dma((2,)),
        ],
        compiler_params=pltpu.CompilerParams(
            collective_id=0, has_side_effects=True, vmem_limit_bytes=50 * 1024 * 1024
        ),
        cost_estimate=pl.CostEstimate(
            flops=5 * 2 * 2 * 3 * length * chans * chans, bytes_accessed=8 * length * chans, transcendentals=0
        ),
        name="tower",
    )(
        stem_activity, convolution_weight, convolution_bias,
        query_weight, key_weight, value_weight, output_weight,
    )


def solution(mesh):
    return jax.shard_map(
        shards,
        mesh=mesh,
        in_specs=(P(("outer", "inner"), None), P(), P(), P(), P(), P(), P()),
        out_specs=(P(("outer", "inner"), None), P(("outer", "inner"), None)),
        check_vma=False,
    )
```

```python
import jax
import jax.numpy as jnp
from jax import lax
from jax.experimental import pallas as pl
from jax.experimental.pallas import tpu as pltpu
from jax.sharding import PartitionSpec as P

HEAD_DIM = 64
POOL = 128
GROUPS = 8
MEMBERS = 8
HALO = 3
CHUNKS = 8
IN_FLIGHT = 3
HELD = 2
AHEAD = 1
COLUMNS = 256
ORDER = (1, 2, 6, 5, 4, 3, 7)
ROUND = (2, 4, 6)
HEADS_AT_ONCE = 4
MESH = pl.DeviceIdType.MESH
F32, BF16 = jnp.float32, jnp.bfloat16


def gelu(x):
    return 0.5 * x * (1.0 + lax.erf(x * (0.5**0.5)))


def dot(left, right):
    return jnp.dot(left, right, preferred_element_type=F32)


def thirds(value):
    high = value.astype(BF16)
    rest = value - high.astype(F32)
    middle = rest.astype(BF16)
    return high, middle, (rest - middle.astype(F32)).astype(BF16)


def swapped(member, outer):
    return member // 2 * 2 + (member + outer // 4) % 2


def tower_kernel(
    stem, weight, bias, query_weight, key_weight, value_weight, output_weight,
    tower, attended,
    rows_in, rows_out, taps, active, second, field, everyone, split_rows, mixed, heads_weight,
    weight_sem, heads_sem, in_send, in_recv, halo_send, halo_recv, out_send, out_recv,
    pool_send, pool_recv, share_send, share_recv,
):
    outer, inner = lax.axis_index("outer"), lax.axis_index("inner")
    member, core = inner // 2, inner % 2
    chans = stem.shape[1]
    part = stem.shape[0] // MEMBERS
    rows = part // CHUNKS
    mine = swapped(member, outer)
    up, down = (outer + 1) % GROUPS, (outer + GROUPS - 1) % GROUPS
    neighbours = (
        (up, 2 * swapped(mine, up) + core),
        (down, 2 * swapped(mine, down) + core),
    )

    def other(step):
        way = step // 2
        return (member // 2 + way + core * (4 - 2 * way)) % 4 * 2 + (member + step) % 2

    barrier = pltpu.get_barrier_semaphore()

    def greet(device):
        pl.semaphore_signal(barrier, inc=1, device_id=device, device_id_type=MESH)

    for step in range(1, MEMBERS):
        greet((outer, 2 * other(step) + core))
    greet((outer, inner + 1 - 2 * core))
    for neighbour in neighbours:
        greet(neighbour)

    def load_taps(layer, tap, half):
        return pltpu.make_async_copy(
            weight.at[layer, tap],
            taps.at[layer, tap, pl.ds(half * chans, chans)],
            weight_sem.at[layer, tap, half],
        )

    def load_heads(k):
        source = (query_weight, key_weight, value_weight, output_weight)[k]
        return pltpu.make_async_copy(source, heads_weight.at[k], heads_sem.at[k])

    every_tap = [(layer, tap, half) for layer in range(2) for tap in range(3) for half in range(2)]
    for which in every_tap:
        load_taps(*which).start()
    for k in range(4):
        load_heads(k).start()

    pl.semaphore_wait(barrier, MEMBERS + len(neighbours))

    def span(chunk):
        return pl.ds(pl.multiple_of(chunk * rows, rows), rows)

    def piece(index, chunk):
        return pl.ds(pl.multiple_of(index * part + chunk * rows, rows), rows)

    def send_in(chunk, step):
        to = other(step)
        return pltpu.make_async_remote_copy(
            src_ref=stem.at[piece(swapped(to, outer), chunk)],
            dst_ref=rows_in.at[HALO + member, span(chunk)],
            send_sem=in_send.at[chunk, step],
            recv_sem=in_recv.at[chunk, member],
            device_id=(outer, 2 * to + core),
            device_id_type=MESH,
        )

    def keep_in(chunk):
        return pltpu.make_async_copy(
            stem.at[piece(mine, chunk)], rows_in.at[HALO + member, span(chunk)], in_recv.at[chunk, member]
        )

    def arrived(chunk, block):
        there = rows_in.at[HALO + block, span(chunk)]
        return pltpu.make_async_copy(there, there, in_recv.at[chunk, block])

    def send_halo(chunk, side):
        return pltpu.make_async_remote_copy(
            src_ref=rows_in.at[pl.ds(MEMBERS if side == 0 else HALO, HALO), span(chunk)],
            dst_ref=rows_in.at[pl.ds(0 if side == 0 else HALO + MEMBERS, HALO), span(chunk)],
            send_sem=halo_send.at[chunk, side],
            recv_sem=halo_recv.at[chunk, side],
            device_id=neighbours[side],
            device_id_type=MESH,
        )

    def send_out(chunk, step):
        to = other(step)
        return pltpu.make_async_remote_copy(
            src_ref=rows_out.at[to, span(chunk)],
            dst_ref=tower.at[piece(mine, chunk)],
            send_sem=out_send.at[chunk, step],
            recv_sem=out_recv.at[chunk, mine],
            device_id=(outer, 2 * to + core),
            device_id_type=MESH,
        )

    def keep_out(chunk):
        return pltpu.make_async_copy(
            rows_out.at[member, span(chunk)], tower.at[piece(mine, chunk)], out_recv.at[chunk, mine]
        )

    def returned(chunk, index):
        there = tower.at[piece(index, chunk)]
        return pltpu.make_async_copy(there, there, out_recv.at[chunk, index])

    def start_in(chunk):
        keep_in(chunk).start()
        for step in ORDER:
            send_in(chunk, step).start()

    def start_out(chunk):
        keep_out(chunk).start()
        for step in ORDER:
            send_out(chunk, step).start()

    def forward(chunk):
        for block in range(MEMBERS - HALO, MEMBERS):
            arrived(chunk, block).wait()
        send_halo(chunk, 0).start()
        for block in range(HALO):
            arrived(chunk, block).wait()
        send_halo(chunk, 1).start()
        for block in range(HALO, MEMBERS - HALO):
            arrived(chunk, block).wait()

    def split(value, into, first, columns=slice(0, 768)):
        high = value.astype(BF16)
        count, start, stop = value.shape[0], columns.start, columns.stop
        into[first : first + count, start:stop] = high
        into[first : first + count, chans + start : chans + stop] = (value - high.astype(F32)).astype(BF16)

    def inside(block):
        if 0 <= block < MEMBERS:
            return 1.0
        number = outer * MEMBERS + block
        return ((number >= 0) & (number < GROUPS * MEMBERS)).astype(F32)

    def conv(source, layer, spread, blocks, columns):
        total = bias[layer : layer + 1, columns]
        for tap in range(3):
            first = tap * spread * rows
            total = total + dot(source[first : first + blocks * rows, :], taps[layer, tap, :, columns])
        return total

    tiles = [slice(start, start + COLUMNS) for start in range(0, chans, COLUMNS)]

    def activate(chunk, blocks):
        for block in blocks:
            split(gelu(rows_in[block, span(chunk)]) * inside(block - HALO), active, block * rows)

    def first_layer(chunk):
        for columns in tiles:
            result = conv(active, 0, 1, MEMBERS + 4, columns)
            for block in range(MEMBERS + 4):
                at = slice(block * rows, (block + 1) * rows)
                total = rows_in[block + 1, span(chunk), columns] + result[at]
                field[at, columns] = total
                split(gelu(total) * inside(block - 2), second, block * rows, columns)

    def second_layer(chunk, columns):
        result = conv(second, 1, 2, MEMBERS, columns)
        for block in range(MEMBERS):
            before = field[(block + 2) * rows : (block + 3) * rows, columns]
            rows_out[block, span(chunk), columns] = before + result[block * rows : (block + 1) * rows]

    def shelf(run, whose):
        return pl.multiple_of((run * 2 + whose) * MEMBERS * MEMBERS, MEMBERS)

    def slot(run, of):
        return pl.ds(shelf(run, core) + of * MEMBERS, MEMBERS)

    def pair(run, of):
        return pl.ds(shelf(run, core) + of // 2 * 2 * MEMBERS, 2 * MEMBERS)

    def send_pool(run, step):
        part_of = everyone.at[slot(run, member) if step == 1 else pair(run, member)]
        return pltpu.make_async_remote_copy(
            src_ref=part_of,
            dst_ref=part_of,
            send_sem=pool_send.at[run, step],
            recv_sem=pool_recv.at[run, member],
            device_id=(outer, 2 * other(step) + core),
            device_id_type=MESH,
        )

    def share(run):
        half = pl.ds(shelf(run, core), MEMBERS * MEMBERS)
        return pltpu.make_async_remote_copy(
            src_ref=everyone.at[half],
            dst_ref=everyone.at[half],
            send_sem=share_send.at[run],
            recv_sem=share_recv.at[run],
            device_id=(outer, inner + 1 - 2 * core),
            device_id_type=MESH,
        )

    def start_pool(run):
        everyone[slot(run, member), :] = jnp.concatenate(
            [
                jnp.sum(rows_out[block, run * POOL : (run + 1) * POOL], axis=0, keepdims=True) * (1.0 / POOL)
                for block in range(MEMBERS)
            ],
            axis=0,
        )
        send_pool(run, 1).start()

    def pass_pool(run):
        there = everyone.at[slot(run, other(1))]
        pltpu.make_async_copy(there, there, pool_recv.at[run, other(1)]).wait()
        for step in ROUND:
            send_pool(run, step).start()

    def start_share(run):
        for step in ROUND:
            there = everyone.at[pair(run, other(step))]
            pltpu.make_async_copy(there, there, pool_recv.at[run, other(step)]).wait()
        share(run).start()

    def finish_share(run):
        there = everyone.at[pl.ds(shelf(run, 1 - core), MEMBERS * MEMBERS)]
        pltpu.make_async_copy(there, there, share_recv.at[run]).wait()

    def bring(chunk):
        @pl.when(chunk + AHEAD < CHUNKS)
        def _():
            forward(chunk + AHEAD)

        @pl.when(chunk + AHEAD + IN_FLIGHT < CHUNKS)
        def _():
            start_in(chunk + AHEAD + IN_FLIGHT)

        for side in range(2):
            send_halo(chunk, side).wait_recv()

    blocks = range(MEMBERS + 2 * HALO)
    for chunk in range(IN_FLIGHT):
        start_in(chunk)
    for chunk in range(AHEAD):
        forward(chunk)
        start_in(chunk + IN_FLIGHT)
    bring(0)
    activate(0, blocks)
    for which in every_tap:
        load_taps(*which).wait()
    first_layer(0)

    def step_of(chunk, _):
        bring(chunk)
        for k, columns in enumerate(tiles):
            second_layer(chunk - 1, columns)
            activate(chunk, blocks[k :: len(tiles)])
        first_layer(chunk)

        @pl.when(chunk > HELD)
        def _():
            start_out(chunk - 1 - HELD)

        @pl.when(chunk == CHUNKS // 2)
        def _():
            start_pool(0)

        @pl.when(chunk == CHUNKS // 2 + 1)
        def _():
            pass_pool(0)

        @pl.when(chunk == CHUNKS // 2 + 2)
        def _():
            start_share(0)

        return 0

    lax.fori_loop(1, CHUNKS, step_of, 0)
    for columns in tiles:
        second_layer(CHUNKS - 1, columns)
    start_pool(1)
    start_out(CHUNKS - 1 - HELD)
    pass_pool(1)
    start_out(CHUNKS - HELD)
    start_share(1)
    for chunk in range(CHUNKS - HELD + 1, CHUNKS):
        start_out(chunk)
    for k in range(4):
        load_heads(k).wait()
    finish_share(0)
    finish_share(1)

    runs = part // POOL
    count = MEMBERS * runs
    total = 2 * MEMBERS * count
    for k, third in enumerate(thirds(everyone[...])):
        split_rows[k * total : (k + 1) * total, :] = third

    def stacked(value, weight):
        size = value.shape[0] // 3
        result = dot(value, weight)
        return (result[2 * size :] + result[size : 2 * size]) + result[:size]

    place = lax.broadcasted_iota(jnp.int32, (count, total), 0)
    wanted = ((place % runs * 2 + core) * MEMBERS + swapped(place // runs, outer)) * MEMBERS + member
    chosen = (lax.broadcasted_iota(jnp.int32, (count, total), 1) == wanted).astype(F32).astype(BF16)
    own_parts = [dot(chosen, split_rows[k * total : (k + 1) * total, :]) for k in range(3)]
    own = (own_parts[2] + own_parts[1]) + own_parts[0]
    own_rows = jnp.concatenate([value.astype(BF16) for value in own_parts], axis=0)
    width = HEADS_AT_ONCE * HEAD_DIM
    head = lax.broadcasted_iota(jnp.int32, (1, width), 1) // HEAD_DIM
    masks = [(head == k).astype(F32) for k in range(HEADS_AT_ONCE)]

    for start in range(0, chans, width):
        columns = slice(start, start + width)
        queries = stacked(own_rows, heads_weight[0, :, columns]) * (HEAD_DIM**-0.5)
        keys = stacked(split_rows[...], heads_weight[1, :, columns])
        vals = stacked(split_rows[...], heads_weight[2, :, columns])
        scores = lax.dot_general(
            jnp.concatenate([queries * mask for mask in masks], axis=0),
            keys,
            (((1,), (1,)), ((), ())),
            precision=lax.Precision.HIGHEST,
            preferred_element_type=F32,
        )
        powers = jnp.exp(scores - jnp.max(scores, axis=1, keepdims=True))
        probs = powers / jnp.sum(powers, axis=1, keepdims=True)
        each = jnp.dot(probs, vals, precision=lax.Precision.HIGHEST, preferred_element_type=F32)
        mixed[:, columns] = sum(each[k * count : (k + 1) * count] * mask for k, mask in enumerate(masks))

    attended[...] = own + stacked(jnp.concatenate(thirds(mixed[...]), axis=0), heads_weight[3])

    for run in range(runs):
        share(run).wait_send()
        for step in (1, *ROUND):
            send_pool(run, step).wait_send()

    def finish(chunk, _):
        for side in range(2):
            send_halo(chunk, side).wait_send()
        for step in range(1, MEMBERS):
            send_in(chunk, step).wait_send()
            send_out(chunk, step).wait_send()
        for index in range(MEMBERS):
            returned(chunk, index).wait()
        return 0

    lax.fori_loop(0, CHUNKS, finish, 0)


def shards(stem_activity, convolution_weight, convolution_bias, query_weight, key_weight, value_weight, output_weight):
    length, chans = stem_activity.shape
    part = length // MEMBERS
    rows = part // CHUNKS
    blocks = MEMBERS + 2 * HALO
    pooled = length // POOL
    dma, vmem = pltpu.SemaphoreType.DMA, pltpu.VMEM
    far, on_core = pl.BlockSpec(memory_space=pltpu.HBM), pl.BlockSpec(memory_space=vmem)
    return pl.pallas_call(
        tower_kernel,
        out_shape=(
            vmem((length, chans), F32),
            jax.ShapeDtypeStruct((pooled, chans), F32),
        ),
        in_specs=[far, far, on_core, far, far, far, far],
        out_specs=(on_core, on_core),
        scratch_shapes=[
            vmem((blocks, part, chans), F32),
            vmem((MEMBERS, part, chans), F32),
            vmem((2, 3, 2 * chans, chans), BF16),
            vmem((blocks * rows, 2 * chans), BF16),
            vmem(((blocks - 2) * rows, 2 * chans), BF16),
            vmem(((blocks - 2) * rows, chans), F32),
            vmem((2 * MEMBERS * pooled, chans), F32),
            vmem((3 * 2 * MEMBERS * pooled, chans), BF16),
            vmem((pooled, chans), F32),
            vmem((4, chans, chans), BF16),
            dma((2, 3, 2)),
            dma((4,)),
            dma((CHUNKS, MEMBERS)),
            dma((CHUNKS, MEMBERS)),
            dma((CHUNKS, 2)),
            dma((CHUNKS, 2)),
            dma((CHUNKS, MEMBERS)),
            dma((CHUNKS, MEMBERS)),
            dma((2, MEMBERS)),
            dma((2, MEMBERS)),
            dma((2,)),
            dma((2,)),
        ],
        compiler_params=pltpu.CompilerParams(
            collective_id=0, has_side_effects=True, vmem_limit_bytes=50 * 1024 * 1024
        ),
        cost_estimate=pl.CostEstimate(
            flops=5 * 2 * 2 * 3 * length * chans * chans, bytes_accessed=8 * length * chans, transcendentals=0
        ),
        name="tower",
    )(
        stem_activity, convolution_weight, convolution_bias,
        query_weight, key_weight, value_weight, output_weight,
    )


def solution(mesh):
    return jax.shard_map(
        shards,
        mesh=mesh,
        in_specs=(P(("outer", "inner"), None), P(), P(), P(), P(), P(), P()),
        out_specs=(P(("outer", "inner"), None), P(("outer", "inner"), None)),
        check_vma=False,
    )
```

```python
import jax
import jax.numpy as jnp
from jax import lax
from jax.experimental import pallas as pl
from jax.experimental.pallas import tpu as pltpu
from jax.sharding import PartitionSpec as P

HEAD_DIM = 64
POOL = 128
GROUPS = 8
MEMBERS = 8
HALO = 3
CHUNKS = 8
IN_FLIGHT = 3
HELD = 2
AHEAD = 1
COLUMNS = 256
ORDER = (1, 2, 6, 5, 4, 3, 7)
HEADS_AT_ONCE = 4
MESH = pl.DeviceIdType.MESH
F32, BF16 = jnp.float32, jnp.bfloat16


def gelu(x):
    return 0.5 * x * (1.0 + lax.erf(x * (0.5**0.5)))


def dot(left, right):
    return jnp.dot(left, right, preferred_element_type=F32)


def thirds(value):
    high = value.astype(BF16)
    rest = value - high.astype(F32)
    middle = rest.astype(BF16)
    return high, middle, (rest - middle.astype(F32)).astype(BF16)


def swapped(member, outer):
    return member // 2 * 2 + (member + outer // 4) % 2


def tower_kernel(
    stem, weight, bias, query_weight, key_weight, value_weight, output_weight,
    tower, attended,
    rows_in, rows_out, taps, active, second, field, everyone, split_rows, mixed, heads_weight,
    weight_sem, heads_sem, in_send, in_recv, halo_send, halo_recv, out_send, out_recv,
    pool_send, pool_recv, share_send, share_recv,
):
    outer, inner = lax.axis_index("outer"), lax.axis_index("inner")
    member, core = inner // 2, inner % 2
    chans = stem.shape[1]
    part = stem.shape[0] // MEMBERS
    rows = part // CHUNKS
    mine = swapped(member, outer)
    up, down = (outer + 1) % GROUPS, (outer + GROUPS - 1) % GROUPS
    neighbours = (
        (up, 2 * swapped(mine, up) + core),
        (down, 2 * swapped(mine, down) + core),
    )

    def other(step):
        way = step // 2
        return (member // 2 + way + core * (4 - 2 * way)) % 4 * 2 + (member + step) % 2

    barrier = pltpu.get_barrier_semaphore()

    def greet(device):
        pl.semaphore_signal(barrier, inc=1, device_id=device, device_id_type=MESH)

    for step in range(1, MEMBERS):
        greet((outer, 2 * other(step) + core))
    greet((outer, inner + 1 - 2 * core))
    for neighbour in neighbours:
        greet(neighbour)

    def load_taps(layer, tap, half):
        return pltpu.make_async_copy(
            weight.at[layer, tap],
            taps.at[layer, tap, pl.ds(half * chans, chans)],
            weight_sem.at[layer, tap, half],
        )

    def load_heads(k):
        source = (query_weight, key_weight, value_weight, output_weight)[k]
        return pltpu.make_async_copy(source, heads_weight.at[k], heads_sem.at[k])

    every_tap = [(layer, tap, half) for layer in range(2) for tap in range(3) for half in range(2)]
    pl.semaphore_wait(barrier, MEMBERS + len(neighbours))

    def span(chunk):
        return pl.ds(pl.multiple_of(chunk * rows, rows), rows)

    def piece(index, chunk):
        return pl.ds(pl.multiple_of(index * part + chunk * rows, rows), rows)

    def send_in(chunk, step):
        to = other(step)
        return pltpu.make_async_remote_copy(
            src_ref=stem.at[piece(swapped(to, outer), chunk)],
            dst_ref=rows_in.at[HALO + member, span(chunk)],
            send_sem=in_send.at[chunk, step],
            recv_sem=in_recv.at[chunk, member],
            device_id=(outer, 2 * to + core),
            device_id_type=MESH,
        )

    def keep_in(chunk):
        return pltpu.make_async_copy(
            stem.at[piece(mine, chunk)], rows_in.at[HALO + member, span(chunk)], in_recv.at[chunk, member]
        )

    def arrived(chunk, block):
        there = rows_in.at[HALO + block, span(chunk)]
        return pltpu.make_async_copy(there, there, in_recv.at[chunk, block])

    def send_halo(chunk, side):
        return pltpu.make_async_remote_copy(
            src_ref=rows_in.at[pl.ds(MEMBERS if side == 0 else HALO, HALO), span(chunk)],
            dst_ref=rows_in.at[pl.ds(0 if side == 0 else HALO + MEMBERS, HALO), span(chunk)],
            send_sem=halo_send.at[chunk, side],
            recv_sem=halo_recv.at[chunk, side],
            device_id=neighbours[side],
            device_id_type=MESH,
        )

    def send_out(chunk, step):
        to = other(step)
        return pltpu.make_async_remote_copy(
            src_ref=rows_out.at[to, span(chunk)],
            dst_ref=tower.at[piece(mine, chunk)],
            send_sem=out_send.at[chunk, step],
            recv_sem=out_recv.at[chunk, mine],
            device_id=(outer, 2 * to + core),
            device_id_type=MESH,
        )

    def keep_out(chunk):
        return pltpu.make_async_copy(
            rows_out.at[member, span(chunk)], tower.at[piece(mine, chunk)], out_recv.at[chunk, mine]
        )

    def returned(chunk, index):
        there = tower.at[piece(index, chunk)]
        return pltpu.make_async_copy(there, there, out_recv.at[chunk, index])

    def start_in(chunk):
        keep_in(chunk).start()
        for step in ORDER:
            send_in(chunk, step).start()

    def start_out(chunk):
        keep_out(chunk).start()
        for step in ORDER:
            send_out(chunk, step).start()

    def forward(chunk):
        for block in range(MEMBERS - HALO, MEMBERS):
            arrived(chunk, block).wait()
        send_halo(chunk, 0).start()
        for block in range(HALO):
            arrived(chunk, block).wait()
        send_halo(chunk, 1).start()
        for block in range(HALO, MEMBERS - HALO):
            arrived(chunk, block).wait()

    def split(value, into, first, columns=slice(0, 768)):
        high = value.astype(BF16)
        count, start, stop = value.shape[0], columns.start, columns.stop
        into[first : first + count, start:stop] = high
        into[first : first + count, chans + start : chans + stop] = (value - high.astype(F32)).astype(BF16)

    def inside(block):
        if 0 <= block < MEMBERS:
            return 1.0
        number = outer * MEMBERS + block
        return ((number >= 0) & (number < GROUPS * MEMBERS)).astype(F32)

    def conv(source, layer, spread, blocks, columns):
        total = bias[layer : layer + 1, columns]
        for tap in range(3):
            first = tap * spread * rows
            total = total + dot(source[first : first + blocks * rows, :], taps[layer, tap, :, columns])
        return total

    tiles = [slice(start, start + COLUMNS) for start in range(0, chans, COLUMNS)]

    def activate(chunk, blocks):
        for block in blocks:
            split(gelu(rows_in[block, span(chunk)]) * inside(block - HALO), active, block * rows)

    def first_layer(chunk):
        for columns in tiles:
            result = conv(active, 0, 1, MEMBERS + 4, columns)
            for block in range(MEMBERS + 4):
                at = slice(block * rows, (block + 1) * rows)
                total = rows_in[block + 1, span(chunk), columns] + result[at]
                field[at, columns] = total
                split(gelu(total) * inside(block - 2), second, block * rows, columns)

    def second_layer(chunk, columns):
        result = conv(second, 1, 2, MEMBERS, columns)
        for block in range(MEMBERS):
            before = field[(block + 2) * rows : (block + 3) * rows, columns]
            rows_out[block, span(chunk), columns] = before + result[block * rows : (block + 1) * rows]

    def shelf(run, whose):
        return pl.multiple_of((run * 2 + whose) * MEMBERS * MEMBERS, MEMBERS)

    def slot(run, of):
        return pl.ds(shelf(run, core) + of * MEMBERS, MEMBERS)

    def send_pool(run, step):
        return pltpu.make_async_remote_copy(
            src_ref=everyone.at[slot(run, member)],
            dst_ref=everyone.at[slot(run, member)],
            send_sem=pool_send.at[run, step],
            recv_sem=pool_recv.at[run, member],
            device_id=(outer, 2 * other(step) + core),
            device_id_type=MESH,
        )

    def share(run):
        half = pl.ds(shelf(run, core), MEMBERS * MEMBERS)
        return pltpu.make_async_remote_copy(
            src_ref=everyone.at[half],
            dst_ref=everyone.at[half],
            send_sem=share_send.at[run],
            recv_sem=share_recv.at[run],
            device_id=(outer, inner + 1 - 2 * core),
            device_id_type=MESH,
        )

    def start_pool(run):
        everyone[slot(run, member), :] = jnp.concatenate(
            [
                jnp.sum(rows_out[block, run * POOL : (run + 1) * POOL], axis=0, keepdims=True) * (1.0 / POOL)
                for block in range(MEMBERS)
            ],
            axis=0,
        )
        for step in range(1, MEMBERS):
            send_pool(run, step).start()

    def start_share(run):
        for step in range(1, MEMBERS):
            there = everyone.at[slot(run, other(step))]
            pltpu.make_async_copy(there, there, pool_recv.at[run, other(step)]).wait()
        share(run).start()

    def finish_share(run):
        there = everyone.at[pl.ds(shelf(run, 1 - core), MEMBERS * MEMBERS)]
        pltpu.make_async_copy(there, there, share_recv.at[run]).wait()

    def bring(chunk):
        @pl.when(chunk + AHEAD < CHUNKS)
        def _():
            forward(chunk + AHEAD)

        @pl.when(chunk + AHEAD + IN_FLIGHT < CHUNKS)
        def _():
            start_in(chunk + AHEAD + IN_FLIGHT)

        for side in range(2):
            send_halo(chunk, side).wait_recv()

    blocks = range(MEMBERS + 2 * HALO)
    for chunk in range(IN_FLIGHT):
        start_in(chunk)
    for which in every_tap:
        load_taps(*which).start()
    for chunk in range(AHEAD):
        forward(chunk)
        start_in(chunk + IN_FLIGHT)
    bring(0)
    for k in range(4):
        load_heads(k).start()
    activate(0, blocks)
    for which in every_tap:
        load_taps(*which).wait()
    first_layer(0)

    def step_of(chunk, _):
        bring(chunk)
        for k, columns in enumerate(tiles):
            second_layer(chunk - 1, columns)
            activate(chunk, blocks[k :: len(tiles)])
        first_layer(chunk)

        @pl.when(chunk > HELD)
        def _():
            start_out(chunk - 1 - HELD)

        @pl.when(chunk == CHUNKS // 2)
        def _():
            start_pool(0)

        @pl.when(chunk == CHUNKS // 2 + 2)
        def _():
            start_share(0)

        return 0

    lax.fori_loop(1, CHUNKS, step_of, 0)
    for columns in tiles:
        second_layer(CHUNKS - 1, columns)
    start_pool(1)
    start_out(CHUNKS - 1 - HELD)
    start_share(1)
    for chunk in range(CHUNKS - HELD, CHUNKS):
        start_out(chunk)
    for k in range(4):
        load_heads(k).wait()
    finish_share(0)
    finish_share(1)

    runs = part // POOL
    count = MEMBERS * runs
    total = 2 * MEMBERS * count
    for k, third in enumerate(thirds(everyone[...])):
        split_rows[k * total : (k + 1) * total, :] = third

    def stacked(value, weight):
        size = value.shape[0] // 3
        result = dot(value, weight)
        return (result[2 * size :] + result[size : 2 * size]) + result[:size]

    place = lax.broadcasted_iota(jnp.int32, (count, total), 0)
    wanted = ((place % runs * 2 + core) * MEMBERS + swapped(place // runs, outer)) * MEMBERS + member
    chosen = (lax.broadcasted_iota(jnp.int32, (count, total), 1) == wanted).astype(F32).astype(BF16)
    own_parts = [dot(chosen, split_rows[k * total : (k + 1) * total, :]) for k in range(3)]
    own = (own_parts[2] + own_parts[1]) + own_parts[0]
    own_rows = jnp.concatenate([value.astype(BF16) for value in own_parts], axis=0)
    width = HEADS_AT_ONCE * HEAD_DIM
    head = lax.broadcasted_iota(jnp.int32, (1, width), 1) // HEAD_DIM
    masks = [(head == k).astype(F32) for k in range(HEADS_AT_ONCE)]

    for start in range(0, chans, width):
        columns = slice(start, start + width)
        queries = stacked(own_rows, heads_weight[0, :, columns]) * (HEAD_DIM**-0.5)
        keys = stacked(split_rows[...], heads_weight[1, :, columns])
        vals = stacked(split_rows[...], heads_weight[2, :, columns])
        scores = lax.dot_general(
            jnp.concatenate([queries * mask for mask in masks], axis=0),
            keys,
            (((1,), (1,)), ((), ())),
            precision=lax.Precision.HIGHEST,
            preferred_element_type=F32,
        )
        powers = jnp.exp(scores - jnp.max(scores, axis=1, keepdims=True))
        probs = powers / jnp.sum(powers, axis=1, keepdims=True)
        each = jnp.dot(probs, vals, precision=lax.Precision.HIGHEST, preferred_element_type=F32)
        mixed[:, columns] = sum(each[k * count : (k + 1) * count] * mask for k, mask in enumerate(masks))

    attended[...] = own + stacked(jnp.concatenate(thirds(mixed[...]), axis=0), heads_weight[3])

    for run in range(runs):
        share(run).wait_send()
        for step in range(1, MEMBERS):
            send_pool(run, step).wait_send()

    def finish(chunk, _):
        for side in range(2):
            send_halo(chunk, side).wait_send()
        for step in range(1, MEMBERS):
            send_in(chunk, step).wait_send()
            send_out(chunk, step).wait_send()
        for index in range(MEMBERS):
            returned(chunk, index).wait()
        return 0

    lax.fori_loop(0, CHUNKS, finish, 0)


def shards(stem_activity, convolution_weight, convolution_bias, query_weight, key_weight, value_weight, output_weight):
    length, chans = stem_activity.shape
    part = length // MEMBERS
    rows = part // CHUNKS
    blocks = MEMBERS + 2 * HALO
    pooled = length // POOL
    dma, vmem = pltpu.SemaphoreType.DMA, pltpu.VMEM
    far, on_core = pl.BlockSpec(memory_space=pltpu.HBM), pl.BlockSpec(memory_space=vmem)
    return pl.pallas_call(
        tower_kernel,
        out_shape=(
            vmem((length, chans), F32),
            jax.ShapeDtypeStruct((pooled, chans), F32),
        ),
        in_specs=[far, far, on_core, far, far, far, far],
        out_specs=(on_core, on_core),
        scratch_shapes=[
            vmem((blocks, part, chans), F32),
            vmem((MEMBERS, part, chans), F32),
            vmem((2, 3, 2 * chans, chans), BF16),
            vmem((blocks * rows, 2 * chans), BF16),
            vmem(((blocks - 2) * rows, 2 * chans), BF16),
            vmem(((blocks - 2) * rows, chans), F32),
            vmem((2 * MEMBERS * pooled, chans), F32),
            vmem((3 * 2 * MEMBERS * pooled, chans), BF16),
            vmem((pooled, chans), F32),
            vmem((4, chans, chans), BF16),
            dma((2, 3, 2)),
            dma((4,)),
            dma((CHUNKS, MEMBERS)),
            dma((CHUNKS, MEMBERS)),
            dma((CHUNKS, 2)),
            dma((CHUNKS, 2)),
            dma((CHUNKS, MEMBERS)),
            dma((CHUNKS, MEMBERS)),
            dma((2, MEMBERS)),
            dma((2, MEMBERS)),
            dma((2,)),
            dma((2,)),
        ],
        compiler_params=pltpu.CompilerParams(
            collective_id=0, has_side_effects=True, vmem_limit_bytes=50 * 1024 * 1024
        ),
        cost_estimate=pl.CostEstimate(
            flops=5 * 2 * 2 * 3 * length * chans * chans, bytes_accessed=8 * length * chans, transcendentals=0
        ),
        name="tower",
    )(
        stem_activity, convolution_weight, convolution_bias,
        query_weight, key_weight, value_weight, output_weight,
    )


def solution(mesh):
    return jax.shard_map(
        shards,
        mesh=mesh,
        in_specs=(P(("outer", "inner"), None), P(), P(), P(), P(), P(), P()),
        out_specs=(P(("outer", "inner"), None), P(("outer", "inner"), None)),
        check_vma=False,
    )
```

```python
import jax
import jax.numpy as jnp
from jax import lax
from jax.experimental import pallas as pl
from jax.experimental.pallas import tpu as pltpu
from jax.sharding import PartitionSpec as P

HEAD_DIM = 64
POOL = 128
GROUPS = 8
MEMBERS = 8
HALO = 3
CHUNKS = 8
IN_FLIGHT = 3
HELD = 4
AHEAD = 1
COLUMNS = 256
ORDER = (1, 2, 6, 5, 4, 3, 7)
ROUND = (2, 4, 6)
HEADS_AT_ONCE = 4
MESH = pl.DeviceIdType.MESH
F32, BF16 = jnp.float32, jnp.bfloat16


def gelu(x):
    return 0.5 * x * (1.0 + lax.erf(x * (0.5**0.5)))


def dot(left, right):
    return jnp.dot(left, right, preferred_element_type=F32)


def thirds(value):
    high = value.astype(BF16)
    rest = value - high.astype(F32)
    middle = rest.astype(BF16)
    return high, middle, (rest - middle.astype(F32)).astype(BF16)


def swapped(member, outer):
    return member // 2 * 2 + (member + outer // 4) % 2


def shelf_place(member):
    return member % 2 * (MEMBERS // 2) + member // 2


def tower_kernel(
    stem, weight, bias, query_weight, key_weight, value_weight, output_weight,
    tower, attended,
    rows_in, rows_out, taps, active, second, field, everyone, split_rows, mixed, heads_weight,
    weight_sem, heads_sem, in_send, in_recv, halo_send, halo_recv, out_send, out_recv,
    pool_send, pool_recv, share_send, share_recv,
):
    outer, inner = lax.axis_index("outer"), lax.axis_index("inner")
    member, core = inner // 2, inner % 2
    chans = stem.shape[1]
    part = stem.shape[0] // MEMBERS
    rows = part // CHUNKS
    mine = swapped(member, outer)
    up, down = (outer + 1) % GROUPS, (outer + GROUPS - 1) % GROUPS
    neighbours = (
        (up, 2 * swapped(mine, up) + core),
        (down, 2 * swapped(mine, down) + core),
    )

    has = (outer < GROUPS - 1, outer > 0)

    def other(step):
        way = step // 2
        return (member // 2 + way + core * (4 - 2 * way)) % 4 * 2 + (member + step) % 2

    barrier = pltpu.get_barrier_semaphore()

    def greet(device):
        pl.semaphore_signal(barrier, inc=1, device_id=device, device_id_type=MESH)

    for step in range(1, MEMBERS):
        greet((outer, 2 * other(step) + core))
    greet((outer, inner + 1 - 2 * core))
    for neighbour, there in zip(neighbours, has):

        @pl.when(there)
        def _():
            greet(neighbour)


    def load_taps(layer, tap, half):
        return pltpu.make_async_copy(
            weight.at[layer, tap],
            taps.at[layer, tap, pl.ds(half * chans, chans)],
            weight_sem.at[layer, tap, half],
        )

    def load_heads(k):
        source = (query_weight, key_weight, value_weight, output_weight)[k]
        return pltpu.make_async_copy(source, heads_weight.at[k], heads_sem.at[k])

    every_tap = [(layer, tap, half) for layer in range(2) for tap in range(3) for half in range(2)]
    for side in range(2):
        @pl.when(jnp.logical_not(has[side]))
        def _():
            rows_in[0 if side else HALO + MEMBERS : HALO if side else 2 * HALO + MEMBERS] = jnp.zeros(
                (HALO, part, chans), F32
            )

    pl.semaphore_wait(barrier, MEMBERS + has[0].astype(jnp.int32) + has[1].astype(jnp.int32))

    def span(chunk):
        return pl.ds(pl.multiple_of(chunk * rows, rows), rows)

    def piece(index, chunk):
        return pl.ds(pl.multiple_of(index * part + chunk * rows, rows), rows)

    def send_in(chunk, step):
        to = other(step)
        return pltpu.make_async_remote_copy(
            src_ref=stem.at[piece(swapped(to, outer), chunk)],
            dst_ref=rows_in.at[HALO + member, span(chunk)],
            send_sem=in_send.at[chunk, step],
            recv_sem=in_recv.at[chunk, member],
            device_id=(outer, 2 * to + core),
            device_id_type=MESH,
        )

    def keep_in(chunk):
        return pltpu.make_async_copy(
            stem.at[piece(mine, chunk)], rows_in.at[HALO + member, span(chunk)], in_recv.at[chunk, member]
        )

    def arrived(chunk, block):
        there = rows_in.at[HALO + block, span(chunk)]
        return pltpu.make_async_copy(there, there, in_recv.at[chunk, block])

    def send_halo(chunk, side):
        return pltpu.make_async_remote_copy(
            src_ref=rows_in.at[pl.ds(MEMBERS if side == 0 else HALO, HALO), span(chunk)],
            dst_ref=rows_in.at[pl.ds(0 if side == 0 else HALO + MEMBERS, HALO), span(chunk)],
            send_sem=halo_send.at[chunk, side],
            recv_sem=halo_recv.at[chunk, side],
            device_id=neighbours[side],
            device_id_type=MESH,
        )

    def send_out(chunk, step):
        to = other(step)
        return pltpu.make_async_remote_copy(
            src_ref=rows_out.at[to, span(chunk)],
            dst_ref=tower.at[piece(mine, chunk)],
            send_sem=out_send.at[chunk, step],
            recv_sem=out_recv.at[chunk, mine],
            device_id=(outer, 2 * to + core),
            device_id_type=MESH,
        )

    def keep_out(chunk):
        return pltpu.make_async_copy(
            rows_out.at[member, span(chunk)], tower.at[piece(mine, chunk)], out_recv.at[chunk, mine]
        )

    def returned(chunk, index):
        there = tower.at[piece(index, chunk)]
        return pltpu.make_async_copy(there, there, out_recv.at[chunk, index])

    def start_in(chunk):
        keep_in(chunk).start()
        for step in ORDER:
            send_in(chunk, step).start()

    def start_out(chunk):
        keep_out(chunk).start()
        for step in ORDER:
            send_out(chunk, step).start()

    def forward(chunk):
        for block in range(MEMBERS - HALO, MEMBERS):
            arrived(chunk, block).wait()

        @pl.when(has[0])
        def _():
            send_halo(chunk, 0).start()

        for block in range(HALO):
            arrived(chunk, block).wait()

        @pl.when(has[1])
        def _():
            send_halo(chunk, 1).start()

        for block in range(HALO, MEMBERS - HALO):
            arrived(chunk, block).wait()

    def split(value, into, first, columns=slice(0, 768)):
        high = value.astype(BF16)
        count, start, stop = value.shape[0], columns.start, columns.stop
        into[first : first + count, start:stop] = high
        into[first : first + count, chans + start : chans + stop] = (value - high.astype(F32)).astype(BF16)

    def inside(block):
        if 0 <= block < MEMBERS:
            return 1.0
        number = outer * MEMBERS + block
        return ((number >= 0) & (number < GROUPS * MEMBERS)).astype(F32)

    def conv(source, layer, spread, blocks, columns):
        total = bias[layer : layer + 1, columns]
        for tap in range(3):
            first = tap * spread * rows
            total = total + dot(source[first : first + blocks * rows, :], taps[layer, tap, :, columns])
        return total

    tiles = [slice(start, start + COLUMNS) for start in range(0, chans, COLUMNS)]

    def activate(chunk, blocks):
        for block in blocks:
            split(gelu(rows_in[block, span(chunk)]) * inside(block - HALO), active, block * rows)

    def first_layer(chunk):
        for columns in tiles:
            result = conv(active, 0, 1, MEMBERS + 4, columns)
            for block in range(MEMBERS + 4):
                at = slice(block * rows, (block + 1) * rows)
                total = rows_in[block + 1, span(chunk), columns] + result[at]
                field[at, columns] = total
                split(gelu(total) * inside(block - 2), second, block * rows, columns)

    def second_layer(chunk, columns):
        result = conv(second, 1, 2, MEMBERS, columns)
        for block in range(MEMBERS):
            before = field[(block + 2) * rows : (block + 3) * rows, columns]
            rows_out[block, span(chunk), columns] = before + result[block * rows : (block + 1) * rows]

    def shelf(run, whose):
        return pl.multiple_of((run * 2 + whose) * MEMBERS * MEMBERS, MEMBERS)

    def slot(run, of):
        return pl.ds(shelf(run, core) + shelf_place(of) * MEMBERS, MEMBERS)

    def column(run, of):
        return pl.ds(shelf(run, core) + of % 2 * (MEMBERS // 2 * MEMBERS), MEMBERS // 2 * MEMBERS)

    def send_pool(run, step):
        part_of = everyone.at[column(run, member) if step == 1 else slot(run, member)]
        return pltpu.make_async_remote_copy(
            src_ref=part_of,
            dst_ref=part_of,
            send_sem=pool_send.at[run, step],
            recv_sem=pool_recv.at[run, member],
            device_id=(outer, 2 * other(step) + core),
            device_id_type=MESH,
        )

    def share(run):
        half = pl.ds(shelf(run, core), MEMBERS * MEMBERS)
        return pltpu.make_async_remote_copy(
            src_ref=everyone.at[half],
            dst_ref=everyone.at[half],
            send_sem=share_send.at[run],
            recv_sem=share_recv.at[run],
            device_id=(outer, inner + 1 - 2 * core),
            device_id_type=MESH,
        )

    def start_pool(run):
        everyone[slot(run, member), :] = jnp.concatenate(
            [
                jnp.sum(rows_out[block, run * POOL : (run + 1) * POOL], axis=0, keepdims=True) * (1.0 / POOL)
                for block in range(MEMBERS)
            ],
            axis=0,
        )
        for step in ROUND:
            send_pool(run, step).start()

    def pass_pool(run):
        for step in ROUND:
            there = everyone.at[slot(run, other(step))]
            pltpu.make_async_copy(there, there, pool_recv.at[run, other(step)]).wait()
        send_pool(run, 1).start()

    def start_share(run):
        there = everyone.at[column(run, other(1))]
        pltpu.make_async_copy(there, there, pool_recv.at[run, other(1)]).wait()
        share(run).start()

    def finish_share(run):
        there = everyone.at[pl.ds(shelf(run, 1 - core), MEMBERS * MEMBERS)]
        pltpu.make_async_copy(there, there, share_recv.at[run]).wait()

    def bring(chunk):
        @pl.when(chunk + AHEAD < CHUNKS)
        def _():
            forward(chunk + AHEAD)

        @pl.when(chunk + AHEAD + IN_FLIGHT < CHUNKS)
        def _():
            start_in(chunk + AHEAD + IN_FLIGHT)

        for side in range(2):

            @pl.when(has[1 - side])
            def _():
                send_halo(chunk, side).wait_recv()

    blocks = range(MEMBERS + 2 * HALO)
    for chunk in range(IN_FLIGHT):
        start_in(chunk)
    for which in every_tap:
        load_taps(*which).start()
    for chunk in range(AHEAD):
        forward(chunk)
        start_in(chunk + IN_FLIGHT)
    bring(0)
    for k in range(4):
        load_heads(k).start()
    activate(0, blocks)
    for which in every_tap:
        load_taps(*which).wait()
    first_layer(0)

    def step_of(chunk, _):
        bring(chunk)
        for k, columns in enumerate(tiles):
            second_layer(chunk - 1, columns)
            activate(chunk, blocks[k :: len(tiles)])
        first_layer(chunk)

        @pl.when(chunk == HELD)
        def _():
            start_out(0)

        @pl.when(chunk >= HELD)
        def _():
            start_out(chunk - HELD + 1)

        @pl.when(chunk == CHUNKS // 2)
        def _():
            start_pool(0)

        @pl.when(chunk == CHUNKS // 2 + 1)
        def _():
            pass_pool(0)

        @pl.when(chunk == CHUNKS // 2 + 2)
        def _():
            start_share(0)

        return 0

    lax.fori_loop(1, CHUNKS, step_of, 0)
    for columns in tiles:
        second_layer(CHUNKS - 1, columns)
    start_pool(1)
    start_out(CHUNKS - HELD + 1)
    pass_pool(1)
    start_out(CHUNKS - HELD + 2)
    start_share(1)
    for chunk in range(CHUNKS - HELD + 3, CHUNKS):
        start_out(chunk)
    for k in range(4):
        load_heads(k).wait()
    finish_share(0)
    finish_share(1)

    runs = part // POOL
    count = MEMBERS * runs
    total = 2 * MEMBERS * count
    for k, third in enumerate(thirds(everyone[...])):
        split_rows[k * total : (k + 1) * total, :] = third

    def stacked(value, weight):
        size = value.shape[0] // 3
        result = dot(value, weight)
        return (result[2 * size :] + result[size : 2 * size]) + result[:size]

    place = lax.broadcasted_iota(jnp.int32, (count, total), 0)
    wanted = ((place % runs * 2 + core) * MEMBERS + shelf_place(swapped(place // runs, outer))) * MEMBERS + member
    chosen = (lax.broadcasted_iota(jnp.int32, (count, total), 1) == wanted).astype(F32).astype(BF16)
    own_parts = [dot(chosen, split_rows[k * total : (k + 1) * total, :]) for k in range(3)]
    own = (own_parts[2] + own_parts[1]) + own_parts[0]
    own_rows = jnp.concatenate([value.astype(BF16) for value in own_parts], axis=0)
    width = HEADS_AT_ONCE * HEAD_DIM
    head = lax.broadcasted_iota(jnp.int32, (1, width), 1) // HEAD_DIM
    masks = [(head == k).astype(F32) for k in range(HEADS_AT_ONCE)]

    for start in range(0, chans, width):
        columns = slice(start, start + width)
        queries = stacked(own_rows, heads_weight[0, :, columns]) * (HEAD_DIM**-0.5)
        keys = stacked(split_rows[...], heads_weight[1, :, columns])
        vals = stacked(split_rows[...], heads_weight[2, :, columns])
        scores = lax.dot_general(
            jnp.concatenate([queries * mask for mask in masks], axis=0),
            keys,
            (((1,), (1,)), ((), ())),
            precision=lax.Precision.HIGHEST,
            preferred_element_type=F32,
        )
        powers = jnp.exp(scores - jnp.max(scores, axis=1, keepdims=True))
        probs = powers / jnp.sum(powers, axis=1, keepdims=True)
        each = jnp.dot(probs, vals, precision=lax.Precision.HIGHEST, preferred_element_type=F32)
        mixed[:, columns] = sum(each[k * count : (k + 1) * count] * mask for k, mask in enumerate(masks))

    attended[...] = own + stacked(jnp.concatenate(thirds(mixed[...]), axis=0), heads_weight[3])

    for run in range(runs):
        share(run).wait_send()
        for step in (1, *ROUND):
            send_pool(run, step).wait_send()

    def finish(chunk, _):
        for side in range(2):

            @pl.when(has[side])
            def _():
                send_halo(chunk, side).wait_send()

        for step in range(1, MEMBERS):
            send_in(chunk, step).wait_send()
            send_out(chunk, step).wait_send()
        for index in range(MEMBERS):
            returned(chunk, index).wait()
        return 0

    lax.fori_loop(0, CHUNKS, finish, 0)


def shards(stem_activity, convolution_weight, convolution_bias, query_weight, key_weight, value_weight, output_weight):
    length, chans = stem_activity.shape
    part = length // MEMBERS
    rows = part // CHUNKS
    blocks = MEMBERS + 2 * HALO
    pooled = length // POOL
    dma, vmem = pltpu.SemaphoreType.DMA, pltpu.VMEM
    far, on_core = pl.BlockSpec(memory_space=pltpu.HBM), pl.BlockSpec(memory_space=vmem)
    return pl.pallas_call(
        tower_kernel,
        out_shape=(
            vmem((length, chans), F32),
            jax.ShapeDtypeStruct((pooled, chans), F32),
        ),
        in_specs=[far, far, on_core, far, far, far, far],
        out_specs=(on_core, on_core),
        scratch_shapes=[
            vmem((blocks, part, chans), F32),
            vmem((MEMBERS, part, chans), F32),
            vmem((2, 3, 2 * chans, chans), BF16),
            vmem((blocks * rows, 2 * chans), BF16),
            vmem(((blocks - 2) * rows, 2 * chans), BF16),
            vmem(((blocks - 2) * rows, chans), F32),
            vmem((2 * MEMBERS * pooled, chans), F32),
            vmem((3 * 2 * MEMBERS * pooled, chans), BF16),
            vmem((pooled, chans), F32),
            vmem((4, chans, chans), BF16),
            dma((2, 3, 2)),
            dma((4,)),
            dma((CHUNKS, MEMBERS)),
            dma((CHUNKS, MEMBERS)),
            dma((CHUNKS, 2)),
            dma((CHUNKS, 2)),
            dma((CHUNKS, MEMBERS)),
            dma((CHUNKS, MEMBERS)),
            dma((2, MEMBERS)),
            dma((2, MEMBERS)),
            dma((2,)),
            dma((2,)),
        ],
        compiler_params=pltpu.CompilerParams(
            collective_id=0, has_side_effects=True, vmem_limit_bytes=50 * 1024 * 1024
        ),
        cost_estimate=pl.CostEstimate(
            flops=5 * 2 * 2 * 3 * length * chans * chans, bytes_accessed=8 * length * chans, transcendentals=0
        ),
        name="tower",
    )(
        stem_activity, convolution_weight, convolution_bias,
        query_weight, key_weight, value_weight, output_weight,
    )


def solution(mesh):
    return jax.shard_map(
        shards,
        mesh=mesh,
        in_specs=(P(("outer", "inner"), None), P(), P(), P(), P(), P(), P()),
        out_specs=(P(("outer", "inner"), None), P(("outer", "inner"), None)),
        check_vma=False,
    )
```

```python
import jax
import jax.numpy as jnp
from jax import lax
from jax.experimental import pallas as pl
from jax.experimental.pallas import tpu as pltpu
from jax.sharding import PartitionSpec as P

HEAD_DIM = 64
POOL = 128
GROUPS = 8
MEMBERS = 8
HALO = 3
CHUNKS = 4
IN_FLIGHT = 3
HELD = 2
AHEAD = 1
COLUMNS = 256
ORDER = (1, 2, 6, 5, 4, 3, 7)
ROUND = (2, 4, 6)
HEADS_AT_ONCE = 4
MESH = pl.DeviceIdType.MESH
F32, BF16 = jnp.float32, jnp.bfloat16


def gelu(x):
    return 0.5 * x * (1.0 + lax.erf(x * (0.5**0.5)))


def dot(left, right):
    return jnp.dot(left, right, preferred_element_type=F32)


def thirds(value):
    high = value.astype(BF16)
    rest = value - high.astype(F32)
    middle = rest.astype(BF16)
    return high, middle, (rest - middle.astype(F32)).astype(BF16)


def swapped(member, outer):
    return member // 2 * 2 + (member + outer // 4) % 2


def shelf_place(member):
    return member % 2 * (MEMBERS // 2) + member // 2


def tower_kernel(
    stem, weight, bias, query_weight, key_weight, value_weight, output_weight,
    tower, attended,
    rows_in, rows_out, taps, active, second, field, everyone, split_rows, mixed, heads_weight,
    weight_sem, heads_sem, in_send, in_recv, halo_send, halo_recv, out_send, out_recv,
    pool_send, pool_recv, share_send, share_recv,
):
    outer, inner = lax.axis_index("outer"), lax.axis_index("inner")
    member, core = inner // 2, inner % 2
    chans = stem.shape[1]
    part = stem.shape[0] // MEMBERS
    rows = part // CHUNKS
    mine = swapped(member, outer)
    up, down = (outer + 1) % GROUPS, (outer + GROUPS - 1) % GROUPS
    neighbours = (
        (up, 2 * swapped(mine, up) + core),
        (down, 2 * swapped(mine, down) + core),
    )

    has = (outer < GROUPS - 1, outer > 0)

    def other(step):
        way = step // 2
        return (member // 2 + way + core * (4 - 2 * way)) % 4 * 2 + (member + step) % 2

    barrier = pltpu.get_barrier_semaphore()

    def greet(device):
        pl.semaphore_signal(barrier, inc=1, device_id=device, device_id_type=MESH)

    for step in range(1, MEMBERS):
        greet((outer, 2 * other(step) + core))
    greet((outer, inner + 1 - 2 * core))
    for neighbour, there in zip(neighbours, has):

        @pl.when(there)
        def _():
            greet(neighbour)


    def load_taps(layer, tap, half):
        return pltpu.make_async_copy(
            weight.at[layer, tap],
            taps.at[layer, tap, pl.ds(half * chans, chans)],
            weight_sem.at[layer, tap, half],
        )

    def load_heads(k):
        source = (query_weight, key_weight, value_weight, output_weight)[k]
        return pltpu.make_async_copy(source, heads_weight.at[k], heads_sem.at[k])

    every_tap = [(layer, tap, half) for layer in range(2) for tap in range(3) for half in range(2)]
    for side in range(2):
        @pl.when(jnp.logical_not(has[side]))
        def _():
            rows_in[0 if side else HALO + MEMBERS : HALO if side else 2 * HALO + MEMBERS] = jnp.zeros(
                (HALO, part, chans), F32
            )

    pl.semaphore_wait(barrier, MEMBERS + has[0].astype(jnp.int32) + has[1].astype(jnp.int32))

    def span(chunk):
        return pl.ds(pl.multiple_of(chunk * rows, rows), rows)

    def piece(index, chunk):
        return pl.ds(pl.multiple_of(index * part + chunk * rows, rows), rows)

    def send_in(chunk, step):
        to = other(step)
        return pltpu.make_async_remote_copy(
            src_ref=stem.at[piece(swapped(to, outer), chunk)],
            dst_ref=rows_in.at[HALO + member, span(chunk)],
            send_sem=in_send.at[chunk, step],
            recv_sem=in_recv.at[chunk, member],
            device_id=(outer, 2 * to + core),
            device_id_type=MESH,
        )

    def keep_in(chunk):
        return pltpu.make_async_copy(
            stem.at[piece(mine, chunk)], rows_in.at[HALO + member, span(chunk)], in_recv.at[chunk, member]
        )

    def arrived(chunk, block):
        there = rows_in.at[HALO + block, span(chunk)]
        return pltpu.make_async_copy(there, there, in_recv.at[chunk, block])

    def send_halo(chunk, side):
        return pltpu.make_async_remote_copy(
            src_ref=rows_in.at[pl.ds(MEMBERS if side == 0 else HALO, HALO), span(chunk)],
            dst_ref=rows_in.at[pl.ds(0 if side == 0 else HALO + MEMBERS, HALO), span(chunk)],
            send_sem=halo_send.at[chunk, side],
            recv_sem=halo_recv.at[chunk, side],
            device_id=neighbours[side],
            device_id_type=MESH,
        )

    def send_out(chunk, step):
        to = other(step)
        return pltpu.make_async_remote_copy(
            src_ref=rows_out.at[to, span(chunk)],
            dst_ref=tower.at[piece(mine, chunk)],
            send_sem=out_send.at[chunk, step],
            recv_sem=out_recv.at[chunk, mine],
            device_id=(outer, 2 * to + core),
            device_id_type=MESH,
        )

    def keep_out(chunk):
        return pltpu.make_async_copy(
            rows_out.at[member, span(chunk)], tower.at[piece(mine, chunk)], out_recv.at[chunk, mine]
        )

    def returned(chunk, index):
        there = tower.at[piece(index, chunk)]
        return pltpu.make_async_copy(there, there, out_recv.at[chunk, index])

    def start_in(chunk):
        keep_in(chunk).start()
        for step in ORDER:
            send_in(chunk, step).start()

    def start_out(chunk):
        keep_out(chunk).start()
        for step in ORDER:
            send_out(chunk, step).start()

    def forward(chunk):
        for block in range(MEMBERS - HALO, MEMBERS):
            arrived(chunk, block).wait()

        @pl.when(has[0])
        def _():
            send_halo(chunk, 0).start()

        for block in range(HALO):
            arrived(chunk, block).wait()

        @pl.when(has[1])
        def _():
            send_halo(chunk, 1).start()

        for block in range(HALO, MEMBERS - HALO):
            arrived(chunk, block).wait()

    def split(value, into, first, columns=slice(0, 768)):
        high = value.astype(BF16)
        count, start, stop = value.shape[0], columns.start, columns.stop
        into[first : first + count, start:stop] = high
        into[first : first + count, chans + start : chans + stop] = (value - high.astype(F32)).astype(BF16)

    def inside(block):
        if 0 <= block < MEMBERS:
            return 1.0
        number = outer * MEMBERS + block
        return ((number >= 0) & (number < GROUPS * MEMBERS)).astype(F32)

    def conv(source, layer, spread, blocks, columns):
        total = bias[layer : layer + 1, columns]
        for tap in range(3):
            first = tap * spread * rows
            total = total + dot(source[first : first + blocks * rows, :], taps[layer, tap, :, columns])
        return total

    tiles = [slice(start, start + COLUMNS) for start in range(0, chans, COLUMNS)]

    def activate(chunk, blocks):
        for block in blocks:
            split(gelu(rows_in[block, span(chunk)]) * inside(block - HALO), active, block * rows)

    def first_layer(chunk):
        for columns in tiles:
            result = conv(active, 0, 1, MEMBERS + 4, columns)
            for block in range(MEMBERS + 4):
                at = slice(block * rows, (block + 1) * rows)
                total = rows_in[block + 1, span(chunk), columns] + result[at]
                field[at, columns] = total
                split(gelu(total) * inside(block - 2), second, block * rows, columns)

    def second_layer(chunk, columns):
        result = conv(second, 1, 2, MEMBERS, columns)
        for block in range(MEMBERS):
            before = field[(block + 2) * rows : (block + 3) * rows, columns]
            rows_out[block, span(chunk), columns] = before + result[block * rows : (block + 1) * rows]

    def shelf(run, whose):
        return pl.multiple_of((run * 2 + whose) * MEMBERS * MEMBERS, MEMBERS)

    def slot(run, of):
        return pl.ds(shelf(run, core) + shelf_place(of) * MEMBERS, MEMBERS)

    def column(run, of):
        return pl.ds(shelf(run, core) + of % 2 * (MEMBERS // 2 * MEMBERS), MEMBERS // 2 * MEMBERS)

    def send_pool(run, step):
        part_of = everyone.at[column(run, member) if step == 1 else slot(run, member)]
        return pltpu.make_async_remote_copy(
            src_ref=part_of,
            dst_ref=part_of,
            send_sem=pool_send.at[run, step],
            recv_sem=pool_recv.at[run, member],
            device_id=(outer, 2 * other(step) + core),
            device_id_type=MESH,
        )

    def share(run):
        half = pl.ds(shelf(run, core), MEMBERS * MEMBERS)
        return pltpu.make_async_remote_copy(
            src_ref=everyone.at[half],
            dst_ref=everyone.at[half],
            send_sem=share_send.at[run],
            recv_sem=share_recv.at[run],
            device_id=(outer, inner + 1 - 2 * core),
            device_id_type=MESH,
        )

    def start_pool(run):
        everyone[slot(run, member), :] = jnp.concatenate(
            [
                jnp.sum(rows_out[block, run * POOL : (run + 1) * POOL], axis=0, keepdims=True) * (1.0 / POOL)
                for block in range(MEMBERS)
            ],
            axis=0,
        )
        for step in ROUND:
            send_pool(run, step).start()

    def pass_pool(run):
        for step in ROUND:
            there = everyone.at[slot(run, other(step))]
            pltpu.make_async_copy(there, there, pool_recv.at[run, other(step)]).wait()
        send_pool(run, 1).start()

    def start_share(run):
        there = everyone.at[column(run, other(1))]
        pltpu.make_async_copy(there, there, pool_recv.at[run, other(1)]).wait()
        share(run).start()

    def finish_share(run):
        there = everyone.at[pl.ds(shelf(run, 1 - core), MEMBERS * MEMBERS)]
        pltpu.make_async_copy(there, there, share_recv.at[run]).wait()

    def bring(chunk):
        @pl.when(chunk + AHEAD < CHUNKS)
        def _():
            forward(chunk + AHEAD)

        @pl.when(chunk + AHEAD + IN_FLIGHT < CHUNKS)
        def _():
            start_in(chunk + AHEAD + IN_FLIGHT)

        for side in range(2):

            @pl.when(has[1 - side])
            def _():
                send_halo(chunk, side).wait_recv()

    blocks = range(MEMBERS + 2 * HALO)
    for chunk in range(IN_FLIGHT):
        start_in(chunk)
    for which in every_tap:
        load_taps(*which).start()
    for chunk in range(AHEAD):
        forward(chunk)
        start_in(chunk + IN_FLIGHT)
    bring(0)
    for k in range(4):
        load_heads(k).start()
    activate(0, blocks)
    for which in every_tap:
        load_taps(*which).wait()
    first_layer(0)

    def step_of(chunk, _):
        bring(chunk)
        for k, columns in enumerate(tiles):
            second_layer(chunk - 1, columns)
            activate(chunk, blocks[k :: len(tiles)])
        first_layer(chunk)

        @pl.when(chunk == HELD)
        def _():
            start_out(0)

        @pl.when(chunk >= HELD)
        def _():
            start_out(chunk - HELD + 1)

        @pl.when(chunk == CHUNKS // 2)
        def _():
            start_pool(0)

        @pl.when(chunk == CHUNKS // 2 + 1)
        def _():
            pass_pool(0)

        return 0

    lax.fori_loop(1, CHUNKS, step_of, 0)
    for columns in tiles:
        second_layer(CHUNKS - 1, columns)
    start_pool(1)
    start_share(0)
    start_out(CHUNKS - HELD + 1)
    pass_pool(1)
    start_share(1)
    for k in range(4):
        load_heads(k).wait()
    finish_share(0)
    finish_share(1)

    runs = part // POOL
    count = MEMBERS * runs
    total = 2 * MEMBERS * count
    for k, third in enumerate(thirds(everyone[...])):
        split_rows[k * total : (k + 1) * total, :] = third

    def stacked(value, weight):
        size = value.shape[0] // 3
        result = dot(value, weight)
        return (result[2 * size :] + result[size : 2 * size]) + result[:size]

    place = lax.broadcasted_iota(jnp.int32, (count, total), 0)
    wanted = ((place % runs * 2 + core) * MEMBERS + shelf_place(swapped(place // runs, outer))) * MEMBERS + member
    chosen = (lax.broadcasted_iota(jnp.int32, (count, total), 1) == wanted).astype(F32).astype(BF16)
    own_parts = [dot(chosen, split_rows[k * total : (k + 1) * total, :]) for k in range(3)]
    own = (own_parts[2] + own_parts[1]) + own_parts[0]
    own_rows = jnp.concatenate([value.astype(BF16) for value in own_parts], axis=0)
    width = HEADS_AT_ONCE * HEAD_DIM
    head = lax.broadcasted_iota(jnp.int32, (1, width), 1) // HEAD_DIM
    masks = [(head == k).astype(F32) for k in range(HEADS_AT_ONCE)]

    for start in range(0, chans, width):
        columns = slice(start, start + width)
        queries = stacked(own_rows, heads_weight[0, :, columns]) * (HEAD_DIM**-0.5)
        keys = stacked(split_rows[...], heads_weight[1, :, columns])
        vals = stacked(split_rows[...], heads_weight[2, :, columns])
        scores = lax.dot_general(
            jnp.concatenate([queries * mask for mask in masks], axis=0),
            keys,
            (((1,), (1,)), ((), ())),
            precision=lax.Precision.HIGHEST,
            preferred_element_type=F32,
        )
        powers = jnp.exp(scores - jnp.max(scores, axis=1, keepdims=True))
        probs = powers / jnp.sum(powers, axis=1, keepdims=True)
        each = jnp.dot(probs, vals, precision=lax.Precision.HIGHEST, preferred_element_type=F32)
        mixed[:, columns] = sum(each[k * count : (k + 1) * count] * mask for k, mask in enumerate(masks))

    attended[...] = own + stacked(jnp.concatenate(thirds(mixed[...]), axis=0), heads_weight[3])

    for run in range(runs):
        share(run).wait_send()
        for step in (1, *ROUND):
            send_pool(run, step).wait_send()

    def finish(chunk, _):
        for side in range(2):

            @pl.when(has[side])
            def _():
                send_halo(chunk, side).wait_send()

        for step in range(1, MEMBERS):
            send_in(chunk, step).wait_send()
            send_out(chunk, step).wait_send()
        for index in range(MEMBERS):
            returned(chunk, index).wait()
        return 0

    lax.fori_loop(0, CHUNKS, finish, 0)


def shards(stem_activity, convolution_weight, convolution_bias, query_weight, key_weight, value_weight, output_weight):
    length, chans = stem_activity.shape
    part = length // MEMBERS
    rows = part // CHUNKS
    blocks = MEMBERS + 2 * HALO
    pooled = length // POOL
    dma, vmem = pltpu.SemaphoreType.DMA, pltpu.VMEM
    far, on_core = pl.BlockSpec(memory_space=pltpu.HBM), pl.BlockSpec(memory_space=vmem)
    return pl.pallas_call(
        tower_kernel,
        out_shape=(
            vmem((length, chans), F32),
            jax.ShapeDtypeStruct((pooled, chans), F32),
        ),
        in_specs=[far, far, on_core, far, far, far, far],
        out_specs=(on_core, on_core),
        scratch_shapes=[
            vmem((blocks, part, chans), F32),
            vmem((MEMBERS, part, chans), F32),
            vmem((2, 3, 2 * chans, chans), BF16),
            vmem((blocks * rows, 2 * chans), BF16),
            vmem(((blocks - 2) * rows, 2 * chans), BF16),
            vmem(((blocks - 2) * rows, chans), F32),
            vmem((2 * MEMBERS * pooled, chans), F32),
            vmem((3 * 2 * MEMBERS * pooled, chans), BF16),
            vmem((pooled, chans), F32),
            vmem((4, chans, chans), BF16),
            dma((2, 3, 2)),
            dma((4,)),
            dma((CHUNKS, MEMBERS)),
            dma((CHUNKS, MEMBERS)),
            dma((CHUNKS, 2)),
            dma((CHUNKS, 2)),
            dma((CHUNKS, MEMBERS)),
            dma((CHUNKS, MEMBERS)),
            dma((2, MEMBERS)),
            dma((2, MEMBERS)),
            dma((2,)),
            dma((2,)),
        ],
        compiler_params=pltpu.CompilerParams(
            collective_id=0, has_side_effects=True, vmem_limit_bytes=50 * 1024 * 1024
        ),
        cost_estimate=pl.CostEstimate(
            flops=5 * 2 * 2 * 3 * length * chans * chans, bytes_accessed=8 * length * chans, transcendentals=0
        ),
        name="tower",
    )(
        stem_activity, convolution_weight, convolution_bias,
        query_weight, key_weight, value_weight, output_weight,
    )


def solution(mesh):
    return jax.shard_map(
        shards,
        mesh=mesh,
        in_specs=(P(("outer", "inner"), None), P(), P(), P(), P(), P(), P()),
        out_specs=(P(("outer", "inner"), None), P(("outer", "inner"), None)),
        check_vma=False,
    )
```

```python
import jax
import jax.numpy as jnp
from jax import lax
from jax.experimental import pallas as pl
from jax.experimental.pallas import tpu as pltpu
from jax.sharding import PartitionSpec as P

HEAD_DIM = 64
POOL = 128
GROUPS = 8
MEMBERS = 8
HALO = 3
CHUNKS = 8
IN_FLIGHT = 3
HELD = 4
AHEAD = 1
COLUMNS = 256
ORDER = (1, 2, 6, 5, 4, 3, 7)
ROUND = (2, 4, 6)
HEADS_AT_ONCE = 4
MESH = pl.DeviceIdType.MESH
F32, BF16 = jnp.float32, jnp.bfloat16


def gelu(x):
    return 0.5 * x * (1.0 + lax.erf(x * (0.5**0.5)))


def dot(left, right):
    return jnp.dot(left, right, preferred_element_type=F32)


def thirds(value):
    high = value.astype(BF16)
    rest = value - high.astype(F32)
    middle = rest.astype(BF16)
    return high, middle, (rest - middle.astype(F32)).astype(BF16)


def swapped(member, outer):
    return member // 2 * 2 + (member + outer // 4) % 2


def shelf_place(member):
    return member % 2 * (MEMBERS // 2) + member // 2


def tower_kernel(
    stem, weight, bias, query_weight, key_weight, value_weight, output_weight,
    tower, attended,
    rows_in, rows_out, taps, active, second, field, everyone, split_rows, mixed, heads_weight,
    weight_sem, heads_sem, in_send, in_recv, halo_send, halo_recv, out_send, out_recv,
    pool_send, pool_recv, share_send, share_recv,
):
    outer, inner = lax.axis_index("outer"), lax.axis_index("inner")
    member, core = inner // 2, inner % 2
    chans = stem.shape[1]
    part = stem.shape[0] // MEMBERS
    rows = part // CHUNKS
    mine = swapped(member, outer)
    up, down = (outer + 1) % GROUPS, (outer + GROUPS - 1) % GROUPS
    neighbours = (
        (up, 2 * swapped(mine, up) + core),
        (down, 2 * swapped(mine, down) + core),
    )

    has = (outer < GROUPS - 1, outer > 0)

    def other(step):
        way = step // 2
        return (member // 2 + way + core * (4 - 2 * way)) % 4 * 2 + (member + step) % 2

    barrier = pltpu.get_barrier_semaphore()

    def greet(device):
        pl.semaphore_signal(barrier, inc=1, device_id=device, device_id_type=MESH)

    for step in range(1, MEMBERS):
        greet((outer, 2 * other(step) + core))
    greet((outer, inner + 1 - 2 * core))
    for neighbour, there in zip(neighbours, has):

        @pl.when(there)
        def _():
            greet(neighbour)


    def load_taps(layer, tap, half):
        return pltpu.make_async_copy(
            weight.at[layer, tap],
            taps.at[layer, tap, pl.ds(half * chans, chans)],
            weight_sem.at[layer, tap, half],
        )

    def load_heads(k):
        source = (query_weight, key_weight, value_weight, output_weight)[k]
        return pltpu.make_async_copy(source, heads_weight.at[k], heads_sem.at[k])

    every_tap = [(layer, tap, half) for layer in range(2) for tap in range(3) for half in range(2)]
    for side in range(2):
        @pl.when(jnp.logical_not(has[side]))
        def _():
            rows_in[0 if side else HALO + MEMBERS : HALO if side else 2 * HALO + MEMBERS] = jnp.zeros(
                (HALO, part, chans), F32
            )

    pl.semaphore_wait(barrier, MEMBERS + has[0].astype(jnp.int32) + has[1].astype(jnp.int32))

    def span(chunk):
        return pl.ds(pl.multiple_of(chunk * rows, rows), rows)

    def piece(index, chunk):
        return pl.ds(pl.multiple_of(index * part + chunk * rows, rows), rows)

    def send_in(chunk, step):
        to = other(step)
        return pltpu.make_async_remote_copy(
            src_ref=stem.at[piece(swapped(to, outer), chunk)],
            dst_ref=rows_in.at[HALO + member, span(chunk)],
            send_sem=in_send.at[chunk, step],
            recv_sem=in_recv.at[chunk, member],
            device_id=(outer, 2 * to + core),
            device_id_type=MESH,
        )

    def keep_in(chunk):
        return pltpu.make_async_copy(
            stem.at[piece(mine, chunk)], rows_in.at[HALO + member, span(chunk)], in_recv.at[chunk, member]
        )

    def arrived(chunk, block):
        there = rows_in.at[HALO + block, span(chunk)]
        return pltpu.make_async_copy(there, there, in_recv.at[chunk, block])

    def send_halo(chunk, side):
        return pltpu.make_async_remote_copy(
            src_ref=rows_in.at[pl.ds(MEMBERS if side == 0 else HALO, HALO), span(chunk)],
            dst_ref=rows_in.at[pl.ds(0 if side == 0 else HALO + MEMBERS, HALO), span(chunk)],
            send_sem=halo_send.at[chunk, side],
            recv_sem=halo_recv.at[chunk, side],
            device_id=neighbours[side],
            device_id_type=MESH,
        )

    def send_out(chunk, step):
        to = other(step)
        return pltpu.make_async_remote_copy(
            src_ref=rows_out.at[to, span(chunk)],
            dst_ref=tower.at[piece(mine, chunk)],
            send_sem=out_send.at[chunk, step],
            recv_sem=out_recv.at[chunk, mine],
            device_id=(outer, 2 * to + core),
            device_id_type=MESH,
        )

    def keep_out(chunk):
        return pltpu.make_async_copy(
            rows_out.at[member, span(chunk)], tower.at[piece(mine, chunk)], out_recv.at[chunk, mine]
        )

    def returned(chunk, index):
        there = tower.at[piece(index, chunk)]
        return pltpu.make_async_copy(there, there, out_recv.at[chunk, index])

    def start_in(chunk):
        keep_in(chunk).start()
        for step in ORDER:
            send_in(chunk, step).start()

    def start_out(chunk):
        keep_out(chunk).start()
        for step in ORDER:
            send_out(chunk, step).start()

    def forward(chunk):
        for block in range(MEMBERS - HALO, MEMBERS):
            arrived(chunk, block).wait()

        @pl.when(has[0])
        def _():
            send_halo(chunk, 0).start()

        for block in range(HALO):
            arrived(chunk, block).wait()

        @pl.when(has[1])
        def _():
            send_halo(chunk, 1).start()

        for block in range(HALO, MEMBERS - HALO):
            arrived(chunk, block).wait()

    def split(value, into, first, columns=slice(0, 768)):
        high = value.astype(BF16)
        count, start, stop = value.shape[0], columns.start, columns.stop
        into[first : first + count, start:stop] = high
        into[first : first + count, chans + start : chans + stop] = (value - high.astype(F32)).astype(BF16)

    def inside(block):
        if 0 <= block < MEMBERS:
            return 1.0
        number = outer * MEMBERS + block
        return ((number >= 0) & (number < GROUPS * MEMBERS)).astype(F32)

    def conv(source, layer, spread, blocks, columns):
        total = bias[layer : layer + 1, columns]
        for tap in range(3):
            first = tap * spread * rows
            total = total + dot(source[first : first + blocks * rows, :], taps[layer, tap, :, columns])
        return total

    tiles = [slice(start, start + COLUMNS) for start in range(0, chans, COLUMNS)]

    def activate(chunk, blocks):
        for block in blocks:
            split(gelu(rows_in[block, span(chunk)]) * inside(block - HALO), active, block * rows)

    def first_layer(chunk):
        for columns in tiles:
            result = conv(active, 0, 1, MEMBERS + 4, columns)
            for block in range(MEMBERS + 4):
                at = slice(block * rows, (block + 1) * rows)
                total = rows_in[block + 1, span(chunk), columns] + result[at]
                field[at, columns] = total
                split(gelu(total) * inside(block - 2), second, block * rows, columns)

    def second_layer(chunk, columns):
        result = conv(second, 1, 2, MEMBERS, columns)
        for block in range(MEMBERS):
            before = field[(block + 2) * rows : (block + 3) * rows, columns]
            rows_out[block, span(chunk), columns] = before + result[block * rows : (block + 1) * rows]

    def shelf(run, whose):
        return pl.multiple_of((run * 2 + whose) * MEMBERS * MEMBERS, MEMBERS)

    def slot(run, of):
        return pl.ds(shelf(run, core) + shelf_place(of) * MEMBERS, MEMBERS)

    def column(run, of):
        return pl.ds(shelf(run, core) + of % 2 * (MEMBERS // 2 * MEMBERS), MEMBERS // 2 * MEMBERS)

    def send_pool(run, lot, step):
        part_of = everyone.at[(slot(run, member), slot(run, other(1)), column(run, member))[lot]]
        return pltpu.make_async_remote_copy(
            src_ref=part_of,
            dst_ref=part_of,
            send_sem=pool_send.at[run, lot, step],
            recv_sem=pool_recv.at[run, lot, member],
            device_id=(outer, 2 * other(step) + core),
            device_id_type=MESH,
        )

    def pool_arrived(run, lot, step):
        origin = other(step)
        across = origin // 2 * 2 + 1 - origin % 2
        there = everyone.at[(slot(run, origin), slot(run, across), column(run, origin))[lot]]
        pltpu.make_async_copy(there, there, pool_recv.at[run, lot, origin]).wait()

    pool_legs = (
        ([(0, 1)], [(lot, step) for lot in (0, 1) for step in ROUND]),
        ([(0, step) for step in ROUND], [(2, 1)]),
    )

    def share(run):
        half = pl.ds(shelf(run, core), MEMBERS * MEMBERS)
        return pltpu.make_async_remote_copy(
            src_ref=everyone.at[half],
            dst_ref=everyone.at[half],
            send_sem=share_send.at[run],
            recv_sem=share_recv.at[run],
            device_id=(outer, inner + 1 - 2 * core),
            device_id_type=MESH,
        )

    def start_pool(run):
        everyone[slot(run, member), :] = jnp.concatenate(
            [
                jnp.sum(rows_out[block, run * POOL : (run + 1) * POOL], axis=0, keepdims=True) * (1.0 / POOL)
                for block in range(MEMBERS)
            ],
            axis=0,
        )
        for lot, step in pool_legs[run][0]:
            send_pool(run, lot, step).start()

    def pass_pool(run):
        for lot, step in pool_legs[run][0]:
            pool_arrived(run, lot, step)
        for lot, step in pool_legs[run][1]:
            send_pool(run, lot, step).start()

    def start_share(run):
        for lot, step in pool_legs[run][1]:
            pool_arrived(run, lot, step)
        share(run).start()

    def finish_share(run):
        there = everyone.at[pl.ds(shelf(run, 1 - core), MEMBERS * MEMBERS)]
        pltpu.make_async_copy(there, there, share_recv.at[run]).wait()

    def bring(chunk):
        @pl.when(chunk + AHEAD < CHUNKS)
        def _():
            forward(chunk + AHEAD)

        @pl.when(chunk + AHEAD + IN_FLIGHT < CHUNKS)
        def _():
            start_in(chunk + AHEAD + IN_FLIGHT)

        for side in range(2):

            @pl.when(has[1 - side])
            def _():
                send_halo(chunk, side).wait_recv()

    blocks = range(MEMBERS + 2 * HALO)
    for chunk in range(IN_FLIGHT):
        start_in(chunk)
    for which in every_tap:
        load_taps(*which).start()
    for chunk in range(AHEAD):
        forward(chunk)
        start_in(chunk + IN_FLIGHT)
    bring(0)
    for k in range(4):
        load_heads(k).start()
    activate(0, blocks)
    for which in every_tap:
        load_taps(*which).wait()
    first_layer(0)

    def step_of(chunk, _):
        bring(chunk)
        for k, columns in enumerate(tiles):
            second_layer(chunk - 1, columns)
            activate(chunk, blocks[k :: len(tiles)])
        first_layer(chunk)

        @pl.when(chunk == HELD)
        def _():
            start_out(0)

        @pl.when(chunk >= HELD)
        def _():
            start_out(chunk - HELD + 1)

        @pl.when(chunk == CHUNKS // 2)
        def _():
            start_pool(0)

        @pl.when(chunk == CHUNKS // 2 + 1)
        def _():
            pass_pool(0)

        @pl.when(chunk == CHUNKS // 2 + 2)
        def _():
            start_share(0)

        return 0

    lax.fori_loop(1, CHUNKS, step_of, 0)
    for columns in tiles:
        second_layer(CHUNKS - 1, columns)
    start_pool(1)
    start_out(CHUNKS - HELD + 1)
    pass_pool(1)
    start_out(CHUNKS - HELD + 2)
    start_share(1)
    for chunk in range(CHUNKS - HELD + 3, CHUNKS):
        start_out(chunk)
    for k in range(4):
        load_heads(k).wait()
    finish_share(0)
    finish_share(1)

    runs = part // POOL
    count = MEMBERS * runs
    total = 2 * MEMBERS * count
    for k, third in enumerate(thirds(everyone[...])):
        split_rows[k * total : (k + 1) * total, :] = third

    def stacked(value, weight):
        size = value.shape[0] // 3
        result = dot(value, weight)
        return (result[2 * size :] + result[size : 2 * size]) + result[:size]

    place = lax.broadcasted_iota(jnp.int32, (count, total), 0)
    wanted = ((place % runs * 2 + core) * MEMBERS + shelf_place(swapped(place // runs, outer))) * MEMBERS + member
    chosen = (lax.broadcasted_iota(jnp.int32, (count, total), 1) == wanted).astype(F32).astype(BF16)
    own_parts = [dot(chosen, split_rows[k * total : (k + 1) * total, :]) for k in range(3)]
    own = (own_parts[2] + own_parts[1]) + own_parts[0]
    own_rows = jnp.concatenate([value.astype(BF16) for value in own_parts], axis=0)
    width = HEADS_AT_ONCE * HEAD_DIM
    head = lax.broadcasted_iota(jnp.int32, (1, width), 1) // HEAD_DIM
    masks = [(head == k).astype(F32) for k in range(HEADS_AT_ONCE)]

    for start in range(0, chans, width):
        columns = slice(start, start + width)
        queries = stacked(own_rows, heads_weight[0, :, columns]) * (HEAD_DIM**-0.5)
        keys = stacked(split_rows[...], heads_weight[1, :, columns])
        vals = stacked(split_rows[...], heads_weight[2, :, columns])
        scores = lax.dot_general(
            jnp.concatenate([queries * mask for mask in masks], axis=0),
            keys,
            (((1,), (1,)), ((), ())),
            precision=lax.Precision.HIGHEST,
            preferred_element_type=F32,
        )
        powers = jnp.exp(scores - jnp.max(scores, axis=1, keepdims=True))
        probs = powers / jnp.sum(powers, axis=1, keepdims=True)
        each = jnp.dot(probs, vals, precision=lax.Precision.HIGHEST, preferred_element_type=F32)
        mixed[:, columns] = sum(each[k * count : (k + 1) * count] * mask for k, mask in enumerate(masks))

    attended[...] = own + stacked(jnp.concatenate(thirds(mixed[...]), axis=0), heads_weight[3])

    for run in range(runs):
        share(run).wait_send()
        for lot, step in pool_legs[run][0] + pool_legs[run][1]:
            send_pool(run, lot, step).wait_send()

    def finish(chunk, _):
        for side in range(2):

            @pl.when(has[side])
            def _():
                send_halo(chunk, side).wait_send()

        for step in range(1, MEMBERS):
            send_in(chunk, step).wait_send()
            send_out(chunk, step).wait_send()
        for index in range(MEMBERS):
            returned(chunk, index).wait()
        return 0

    lax.fori_loop(0, CHUNKS, finish, 0)


def shards(stem_activity, convolution_weight, convolution_bias, query_weight, key_weight, value_weight, output_weight):
    length, chans = stem_activity.shape
    part = length // MEMBERS
    rows = part // CHUNKS
    blocks = MEMBERS + 2 * HALO
    pooled = length // POOL
    dma, vmem = pltpu.SemaphoreType.DMA, pltpu.VMEM
    far, on_core = pl.BlockSpec(memory_space=pltpu.HBM), pl.BlockSpec(memory_space=vmem)
    return pl.pallas_call(
        tower_kernel,
        out_shape=(
            vmem((length, chans), F32),
            jax.ShapeDtypeStruct((pooled, chans), F32),
        ),
        in_specs=[far, far, on_core, far, far, far, far],
        out_specs=(on_core, on_core),
        scratch_shapes=[
            vmem((blocks, part, chans), F32),
            vmem((MEMBERS, part, chans), F32),
            vmem((2, 3, 2 * chans, chans), BF16),
            vmem((blocks * rows, 2 * chans), BF16),
            vmem(((blocks - 2) * rows, 2 * chans), BF16),
            vmem(((blocks - 2) * rows, chans), F32),
            vmem((2 * MEMBERS * pooled, chans), F32),
            vmem((3 * 2 * MEMBERS * pooled, chans), BF16),
            vmem((pooled, chans), F32),
            vmem((4, chans, chans), BF16),
            dma((2, 3, 2)),
            dma((4,)),
            dma((CHUNKS, MEMBERS)),
            dma((CHUNKS, MEMBERS)),
            dma((CHUNKS, 2)),
            dma((CHUNKS, 2)),
            dma((CHUNKS, MEMBERS)),
            dma((CHUNKS, MEMBERS)),
            dma((2, 3, MEMBERS)),
            dma((2, 3, MEMBERS)),
            dma((2,)),
            dma((2,)),
        ],
        compiler_params=pltpu.CompilerParams(
            collective_id=0, has_side_effects=True, vmem_limit_bytes=50 * 1024 * 1024
        ),
        cost_estimate=pl.CostEstimate(
            flops=5 * 2 * 2 * 3 * length * chans * chans, bytes_accessed=8 * length * chans, transcendentals=0
        ),
        name="tower",
    )(
        stem_activity, convolution_weight, convolution_bias,
        query_weight, key_weight, value_weight, output_weight,
    )


def solution(mesh):
    return jax.shard_map(
        shards,
        mesh=mesh,
        in_specs=(P(("outer", "inner"), None), P(), P(), P(), P(), P(), P()),
        out_specs=(P(("outer", "inner"), None), P(("outer", "inner"), None)),
        check_vma=False,
    )
```

```python
import jax
import jax.numpy as jnp
from jax import lax
from jax.experimental import pallas as pl
from jax.experimental.pallas import tpu as pltpu
from jax.sharding import PartitionSpec as P

HEAD_DIM = 64
POOL = 128
GROUPS = 8
MEMBERS = 8
HALO = 3
CHUNKS = 8
IN_FLIGHT = 3
HELD = 4
AHEAD = 1
COLUMNS = 256
ORDER = (1, 2, 6, 5, 4, 3, 7)
ROUND = (2, 4, 6)
HEADS_AT_ONCE = 4
MESH = pl.DeviceIdType.MESH
F32, BF16 = jnp.float32, jnp.bfloat16


EDGE = 4.0 * 2.0**0.5
NUMERATOR = (
    -1.60960333262415e-02,
    -2.95459980854025e-03,
    -7.34990630326855e-04,
    -5.69250639462346e-05,
    -2.10102402082508e-06,
    2.77068142495902e-08,
    -2.72614225801306e-10,
)
DENOMINATOR = (
    -1.42647390514189e-02,
    -7.37332916720468e-03,
    -1.68282697438203e-03,
    -2.13374055278905e-04,
    -1.45660718464996e-05,
)


def horner(square, factors, scale):
    terms = [factor * scale * 0.5**k for k, factor in enumerate(factors)]
    total = terms[-1]
    for term in terms[-2::-1]:
        total = total * square + term
    return total


def gelu(x):
    inner = jnp.minimum(jnp.maximum(x, -EDGE), EDGE)
    square = inner * inner
    below = horner(square, DENOMINATOR, 1.0)
    inverse = pl.reciprocal(below, approx=True)
    inverse = inverse * (2.0 - below * inverse)
    inverse = inverse * (2.0 - below * inverse)
    ratio = inner * horner(square, NUMERATOR, 0.5**0.5) * inverse
    half = 0.5 * x
    return half + half * jnp.minimum(jnp.maximum(ratio, -1.0), 1.0)


def dot(left, right):
    return jnp.dot(left, right, preferred_element_type=F32)


def thirds(value):
    high = value.astype(BF16)
    rest = value - high.astype(F32)
    middle = rest.astype(BF16)
    return high, middle, (rest - middle.astype(F32)).astype(BF16)


def swapped(member, outer):
    return member // 2 * 2 + (member + outer // 4) % 2


def shelf_place(member):
    return member % 2 * (MEMBERS // 2) + member // 2


def tower_kernel(
    stem, weight, bias, query_weight, key_weight, value_weight, output_weight,
    tower, attended,
    rows_in, rows_out, taps, active, second, field, everyone, split_rows, mixed, heads_weight,
    weight_sem, heads_sem, in_send, in_recv, halo_send, halo_recv, out_send, out_recv,
    pool_send, pool_recv, share_send, share_recv,
):
    outer, inner = lax.axis_index("outer"), lax.axis_index("inner")
    member, core = inner // 2, inner % 2
    chans = stem.shape[1]
    part = stem.shape[0] // MEMBERS
    rows = part // CHUNKS
    mine = swapped(member, outer)
    up, down = (outer + 1) % GROUPS, (outer + GROUPS - 1) % GROUPS
    neighbours = (
        (up, 2 * swapped(mine, up) + core),
        (down, 2 * swapped(mine, down) + core),
    )

    has = (outer < GROUPS - 1, outer > 0)

    def other(step):
        way = step // 2
        return (member // 2 + way + core * (4 - 2 * way)) % 4 * 2 + (member + step) % 2

    barrier = pltpu.get_barrier_semaphore()

    def greet(device):
        pl.semaphore_signal(barrier, inc=1, device_id=device, device_id_type=MESH)

    for step in range(1, MEMBERS):
        greet((outer, 2 * other(step) + core))
    greet((outer, inner + 1 - 2 * core))
    for neighbour, there in zip(neighbours, has):

        @pl.when(there)
        def _():
            greet(neighbour)


    def load_taps(layer, tap, half):
        return pltpu.make_async_copy(
            weight.at[layer, tap],
            taps.at[layer, pl.ds((2 * tap + half) * chans, chans)],
            weight_sem.at[layer, tap, half],
        )

    def load_heads(k):
        source = (query_weight, key_weight, value_weight, output_weight)[k]
        return pltpu.make_async_copy(source, heads_weight.at[k], heads_sem.at[k])

    every_tap = [(layer, tap, half) for layer in range(2) for tap in range(3) for half in range(2)]
    for side in range(2):
        @pl.when(jnp.logical_not(has[side]))
        def _():
            rows_in[0 if side else HALO + MEMBERS : HALO if side else 2 * HALO + MEMBERS] = jnp.zeros(
                (HALO, part, chans), F32
            )

    pl.semaphore_wait(barrier, MEMBERS + has[0].astype(jnp.int32) + has[1].astype(jnp.int32))

    def span(chunk):
        return pl.ds(pl.multiple_of(chunk * rows, rows), rows)

    def piece(index, chunk):
        return pl.ds(pl.multiple_of(index * part + chunk * rows, rows), rows)

    def send_in(chunk, step):
        to = other(step)
        return pltpu.make_async_remote_copy(
            src_ref=stem.at[piece(swapped(to, outer), chunk)],
            dst_ref=rows_in.at[HALO + member, span(chunk)],
            send_sem=in_send.at[chunk, step],
            recv_sem=in_recv.at[chunk, member],
            device_id=(outer, 2 * to + core),
            device_id_type=MESH,
        )

    def keep_in(chunk):
        return pltpu.make_async_copy(
            stem.at[piece(mine, chunk)], rows_in.at[HALO + member, span(chunk)], in_recv.at[chunk, member]
        )

    def arrived(chunk, block):
        there = rows_in.at[HALO + block, span(chunk)]
        return pltpu.make_async_copy(there, there, in_recv.at[chunk, block])

    def send_halo(chunk, side):
        return pltpu.make_async_remote_copy(
            src_ref=rows_in.at[pl.ds(MEMBERS if side == 0 else HALO, HALO), span(chunk)],
            dst_ref=rows_in.at[pl.ds(0 if side == 0 else HALO + MEMBERS, HALO), span(chunk)],
            send_sem=halo_send.at[chunk, side],
            recv_sem=halo_recv.at[chunk, side],
            device_id=neighbours[side],
            device_id_type=MESH,
        )

    def send_out(chunk, step):
        to = other(step)
        return pltpu.make_async_remote_copy(
            src_ref=rows_out.at[to, span(chunk)],
            dst_ref=tower.at[piece(mine, chunk)],
            send_sem=out_send.at[chunk, step],
            recv_sem=out_recv.at[chunk, mine],
            device_id=(outer, 2 * to + core),
            device_id_type=MESH,
        )

    def keep_out(chunk):
        return pltpu.make_async_copy(
            rows_out.at[member, span(chunk)], tower.at[piece(mine, chunk)], out_recv.at[chunk, mine]
        )

    def returned(chunk, index):
        there = tower.at[piece(index, chunk)]
        return pltpu.make_async_copy(there, there, out_recv.at[chunk, index])

    def start_in(chunk):
        keep_in(chunk).start()
        for step in ORDER:
            send_in(chunk, step).start()

    def start_out(chunk):
        keep_out(chunk).start()
        for step in ORDER:
            send_out(chunk, step).start()

    def forward(chunk):
        for block in range(MEMBERS - HALO, MEMBERS):
            arrived(chunk, block).wait()

        @pl.when(has[0])
        def _():
            send_halo(chunk, 0).start()

        for block in range(HALO):
            arrived(chunk, block).wait()

        @pl.when(has[1])
        def _():
            send_halo(chunk, 1).start()

        for block in range(HALO, MEMBERS - HALO):
            arrived(chunk, block).wait()

    def split(value, into, first, columns=slice(0, 768)):
        high = value.astype(BF16)
        count, start, stop = value.shape[0], columns.start, columns.stop
        into[first : first + count, start:stop] = high
        into[first : first + count, chans + start : chans + stop] = (value - high.astype(F32)).astype(BF16)

    def inside(block):
        if 0 <= block < MEMBERS:
            return 1.0
        number = outer * MEMBERS + block
        return ((number >= 0) & (number < GROUPS * MEMBERS)).astype(F32)

    def conv(source, layer, spread, blocks, columns):
        lower = [tap * spread * rows for tap in range(3)]
        shifted = jnp.concatenate([source[first : first + blocks * rows, :] for first in lower], axis=1)
        return dot(shifted, taps[layer, :, columns]) + bias[layer : layer + 1, columns]

    tiles = [slice(start, start + COLUMNS) for start in range(0, chans, COLUMNS)]

    def activate(chunk, blocks):
        for block in blocks:
            split(gelu(rows_in[block, span(chunk)]) * inside(block - HALO), active, block * rows)

    def first_layer(chunk):
        for columns in tiles:
            result = conv(active, 0, 1, MEMBERS + 4, columns)
            for block in range(MEMBERS + 4):
                at = slice(block * rows, (block + 1) * rows)
                total = rows_in[block + 1, span(chunk), columns] + result[at]
                field[at, columns] = total
                split(gelu(total) * inside(block - 2), second, block * rows, columns)

    def second_layer(chunk, columns):
        result = conv(second, 1, 2, MEMBERS, columns)
        for block in range(MEMBERS):
            before = field[(block + 2) * rows : (block + 3) * rows, columns]
            rows_out[block, span(chunk), columns] = before + result[block * rows : (block + 1) * rows]

    def shelf(run, whose):
        return pl.multiple_of((run * 2 + whose) * MEMBERS * MEMBERS, MEMBERS)

    def slot(run, of):
        return pl.ds(shelf(run, core) + shelf_place(of) * MEMBERS, MEMBERS)

    def column(run, of):
        return pl.ds(shelf(run, core) + of % 2 * (MEMBERS // 2 * MEMBERS), MEMBERS // 2 * MEMBERS)

    def send_pool(run, step):
        part_of = everyone.at[column(run, member) if step == 1 else slot(run, member)]
        return pltpu.make_async_remote_copy(
            src_ref=part_of,
            dst_ref=part_of,
            send_sem=pool_send.at[run, step],
            recv_sem=pool_recv.at[run, member],
            device_id=(outer, 2 * other(step) + core),
            device_id_type=MESH,
        )

    def share(run):
        half = pl.ds(shelf(run, core), MEMBERS * MEMBERS)
        return pltpu.make_async_remote_copy(
            src_ref=everyone.at[half],
            dst_ref=everyone.at[half],
            send_sem=share_send.at[run],
            recv_sem=share_recv.at[run],
            device_id=(outer, inner + 1 - 2 * core),
            device_id_type=MESH,
        )

    def start_pool(run):
        everyone[slot(run, member), :] = jnp.concatenate(
            [
                jnp.sum(rows_out[block, run * POOL : (run + 1) * POOL], axis=0, keepdims=True) * (1.0 / POOL)
                for block in range(MEMBERS)
            ],
            axis=0,
        )
        for step in ROUND:
            send_pool(run, step).start()

    def pass_pool(run):
        for step in ROUND:
            there = everyone.at[slot(run, other(step))]
            pltpu.make_async_copy(there, there, pool_recv.at[run, other(step)]).wait()
        send_pool(run, 1).start()

    def start_share(run):
        there = everyone.at[column(run, other(1))]
        pltpu.make_async_copy(there, there, pool_recv.at[run, other(1)]).wait()
        share(run).start()

    def finish_share(run):
        there = everyone.at[pl.ds(shelf(run, 1 - core), MEMBERS * MEMBERS)]
        pltpu.make_async_copy(there, there, share_recv.at[run]).wait()

    def bring(chunk):
        @pl.when(chunk + AHEAD < CHUNKS)
        def _():
            forward(chunk + AHEAD)

        @pl.when(chunk + AHEAD + IN_FLIGHT < CHUNKS)
        def _():
            start_in(chunk + AHEAD + IN_FLIGHT)

        for side in range(2):

            @pl.when(has[1 - side])
            def _():
                send_halo(chunk, side).wait_recv()

    blocks = range(MEMBERS + 2 * HALO)
    for chunk in range(IN_FLIGHT):
        start_in(chunk)
    for which in every_tap:
        load_taps(*which).start()
    for chunk in range(AHEAD):
        forward(chunk)
        start_in(chunk + IN_FLIGHT)
    bring(0)
    for k in range(4):
        load_heads(k).start()
    activate(0, blocks)
    for which in every_tap:
        load_taps(*which).wait()
    first_layer(0)

    def step_of(chunk, _):
        bring(chunk)
        for k, columns in enumerate(tiles):
            second_layer(chunk - 1, columns)
            activate(chunk, blocks[k :: len(tiles)])
        first_layer(chunk)

        @pl.when(chunk == HELD)
        def _():
            start_out(0)

        @pl.when(chunk >= HELD)
        def _():
            start_out(chunk - HELD + 1)

        @pl.when(chunk == CHUNKS // 2)
        def _():
            start_pool(0)

        @pl.when(chunk == CHUNKS // 2 + 1)
        def _():
            pass_pool(0)

        @pl.when(chunk == CHUNKS // 2 + 2)
        def _():
            start_share(0)

        return 0

    lax.fori_loop(1, CHUNKS, step_of, 0)
    for columns in tiles:
        second_layer(CHUNKS - 1, columns)
    start_pool(1)
    start_out(CHUNKS - HELD + 1)
    pass_pool(1)
    start_out(CHUNKS - HELD + 2)
    start_share(1)
    for chunk in range(CHUNKS - HELD + 3, CHUNKS):
        start_out(chunk)
    for k in range(4):
        load_heads(k).wait()
    finish_share(0)
    finish_share(1)

    runs = part // POOL
    count = MEMBERS * runs
    total = 2 * MEMBERS * count
    for k, third in enumerate(thirds(everyone[...])):
        split_rows[k * total : (k + 1) * total, :] = third

    def stacked(value, weight):
        size = value.shape[0] // 3
        result = dot(value, weight)
        return (result[2 * size :] + result[size : 2 * size]) + result[:size]

    place = lax.broadcasted_iota(jnp.int32, (count, total), 0)
    wanted = ((place % runs * 2 + core) * MEMBERS + shelf_place(swapped(place // runs, outer))) * MEMBERS + member
    chosen = (lax.broadcasted_iota(jnp.int32, (count, total), 1) == wanted).astype(F32).astype(BF16)
    own_parts = [dot(chosen, split_rows[k * total : (k + 1) * total, :]) for k in range(3)]
    own = (own_parts[2] + own_parts[1]) + own_parts[0]
    own_rows = jnp.concatenate([value.astype(BF16) for value in own_parts], axis=0)
    width = HEADS_AT_ONCE * HEAD_DIM
    head = lax.broadcasted_iota(jnp.int32, (1, width), 1) // HEAD_DIM
    masks = [(head == k).astype(F32) for k in range(HEADS_AT_ONCE)]

    for start in range(0, chans, width):
        columns = slice(start, start + width)
        queries = stacked(own_rows, heads_weight[0, :, columns]) * (HEAD_DIM**-0.5)
        keys = stacked(split_rows[...], heads_weight[1, :, columns])
        vals = stacked(split_rows[...], heads_weight[2, :, columns])
        scores = lax.dot_general(
            jnp.concatenate([queries * mask for mask in masks], axis=0),
            keys,
            (((1,), (1,)), ((), ())),
            precision=lax.Precision.HIGHEST,
            preferred_element_type=F32,
        )
        powers = jnp.exp(scores - jnp.max(scores, axis=1, keepdims=True))
        probs = powers / jnp.sum(powers, axis=1, keepdims=True)
        each = jnp.dot(probs, vals, precision=lax.Precision.HIGHEST, preferred_element_type=F32)
        mixed[:, columns] = sum(each[k * count : (k + 1) * count] * mask for k, mask in enumerate(masks))

    attended[...] = own + stacked(jnp.concatenate(thirds(mixed[...]), axis=0), heads_weight[3])

    for run in range(runs):
        share(run).wait_send()
        for step in (1, *ROUND):
            send_pool(run, step).wait_send()

    def finish(chunk, _):
        for side in range(2):

            @pl.when(has[side])
            def _():
                send_halo(chunk, side).wait_send()

        for step in range(1, MEMBERS):
            send_in(chunk, step).wait_send()
            send_out(chunk, step).wait_send()
        for index in range(MEMBERS):
            returned(chunk, index).wait()
        return 0

    lax.fori_loop(0, CHUNKS, finish, 0)


def shards(stem_activity, convolution_weight, convolution_bias, query_weight, key_weight, value_weight, output_weight):
    length, chans = stem_activity.shape
    part = length // MEMBERS
    rows = part // CHUNKS
    blocks = MEMBERS + 2 * HALO
    pooled = length // POOL
    dma, vmem = pltpu.SemaphoreType.DMA, pltpu.VMEM
    far, on_core = pl.BlockSpec(memory_space=pltpu.HBM), pl.BlockSpec(memory_space=vmem)
    return pl.pallas_call(
        tower_kernel,
        out_shape=(
            vmem((length, chans), F32),
            jax.ShapeDtypeStruct((pooled, chans), F32),
        ),
        in_specs=[far, far, on_core, far, far, far, far],
        out_specs=(on_core, on_core),
        scratch_shapes=[
            vmem((blocks, part, chans), F32),
            vmem((MEMBERS, part, chans), F32),
            vmem((2, 3 * 2 * chans, chans), BF16),
            vmem((blocks * rows, 2 * chans), BF16),
            vmem(((blocks - 2) * rows, 2 * chans), BF16),
            vmem(((blocks - 2) * rows, chans), F32),
            vmem((2 * MEMBERS * pooled, chans), F32),
            vmem((3 * 2 * MEMBERS * pooled, chans), BF16),
            vmem((pooled, chans), F32),
            vmem((4, chans, chans), BF16),
            dma((2, 3, 2)),
            dma((4,)),
            dma((CHUNKS, MEMBERS)),
            dma((CHUNKS, MEMBERS)),
            dma((CHUNKS, 2)),
            dma((CHUNKS, 2)),
            dma((CHUNKS, MEMBERS)),
            dma((CHUNKS, MEMBERS)),
            dma((2, MEMBERS)),
            dma((2, MEMBERS)),
            dma((2,)),
            dma((2,)),
        ],
        compiler_params=pltpu.CompilerParams(
            collective_id=0, has_side_effects=True, vmem_limit_bytes=50 * 1024 * 1024
        ),
        cost_estimate=pl.CostEstimate(
            flops=5 * 2 * 2 * 3 * length * chans * chans, bytes_accessed=8 * length * chans, transcendentals=0
        ),
        name="tower",
    )(
        stem_activity, convolution_weight, convolution_bias,
        query_weight, key_weight, value_weight, output_weight,
    )


def solution(mesh):
    return jax.shard_map(
        shards,
        mesh=mesh,
        in_specs=(P(("outer", "inner"), None), P(), P(), P(), P(), P(), P()),
        out_specs=(P(("outer", "inner"), None), P(("outer", "inner"), None)),
        check_vma=False,
    )
```

```python
import jax
import jax.numpy as jnp
from jax import lax
from jax.experimental import pallas as pl
from jax.experimental.pallas import tpu as pltpu
from jax.sharding import PartitionSpec as P

HEAD_DIM = 64
POOL = 128
GROUPS = 8
MEMBERS = 8
HALO = 3
CHUNKS = 8
IN_FLIGHT = 3
HELD = 3
AHEAD = 1
COLUMNS = 256
ORDER = (1, 2, 6, 5, 4, 3, 7)
HEADS_AT_ONCE = 4
MESH = pl.DeviceIdType.MESH
F32, BF16 = jnp.float32, jnp.bfloat16


def gelu(x):
    return 0.5 * x * (1.0 + lax.erf(x * (0.5**0.5)))


def dot(left, right):
    return jnp.dot(left, right, preferred_element_type=F32)


def thirds(value):
    high = value.astype(BF16)
    rest = value - high.astype(F32)
    middle = rest.astype(BF16)
    return high, middle, (rest - middle.astype(F32)).astype(BF16)


def swapped(member, outer):
    return member // 2 * 2 + (member + outer // 4) % 2


def shelf_place(member):
    return member % 2 * (MEMBERS // 2) + member // 2


def tower_kernel(
    stem, weight, bias, query_weight, key_weight, value_weight, output_weight,
    tower, attended,
    rows_in, rows_out, taps, active, second, field, everyone, split_rows, mixed, heads_weight,
    weight_sem, heads_sem, in_send, in_recv, halo_send, halo_recv, out_send, out_recv,
    pool_send, pool_recv, share_send, share_recv,
):
    outer, inner = lax.axis_index("outer"), lax.axis_index("inner")
    member, core = inner // 2, inner % 2
    chans = stem.shape[1]
    part = stem.shape[0] // MEMBERS
    rows = part // CHUNKS
    mine = swapped(member, outer)
    up, down = (outer + 1) % GROUPS, (outer + GROUPS - 1) % GROUPS
    neighbours = (
        (up, 2 * swapped(mine, up) + core),
        (down, 2 * swapped(mine, down) + core),
    )

    has = (outer < GROUPS - 1, outer > 0)

    def other(step):
        way = step // 2
        return (member // 2 + way + core * (4 - 2 * way)) % 4 * 2 + (member + step) % 2

    barrier = pltpu.get_barrier_semaphore()

    def greet(device):
        pl.semaphore_signal(barrier, inc=1, device_id=device, device_id_type=MESH)

    for step in range(1, MEMBERS):
        greet((outer, 2 * other(step) + core))
    greet((outer, inner + 1 - 2 * core))
    for neighbour, there in zip(neighbours, has):

        @pl.when(there)
        def _():
            greet(neighbour)


    def load_taps(layer, tap, half):
        return pltpu.make_async_copy(
            weight.at[layer, tap],
            taps.at[layer, tap, pl.ds(half * chans, chans)],
            weight_sem.at[layer, tap, half],
        )

    def load_heads(k):
        source = (query_weight, key_weight, value_weight, output_weight)[k]
        return pltpu.make_async_copy(source, heads_weight.at[k], heads_sem.at[k])

    every_tap = [(layer, tap, half) for layer in range(2) for tap in range(3) for half in range(2)]
    for side in range(2):
        @pl.when(jnp.logical_not(has[side]))
        def _():
            rows_in[0 if side else HALO + MEMBERS : HALO if side else 2 * HALO + MEMBERS] = jnp.zeros(
                (HALO, part, chans), F32
            )

    pl.semaphore_wait(barrier, MEMBERS + has[0].astype(jnp.int32) + has[1].astype(jnp.int32))

    def span(chunk):
        return pl.ds(pl.multiple_of(chunk * rows, rows), rows)

    def piece(index, chunk):
        return pl.ds(pl.multiple_of(index * part + chunk * rows, rows), rows)

    def send_in(chunk, step):
        to = other(step)
        return pltpu.make_async_remote_copy(
            src_ref=stem.at[piece(swapped(to, outer), chunk)],
            dst_ref=rows_in.at[HALO + member, span(chunk)],
            send_sem=in_send.at[chunk, step],
            recv_sem=in_recv.at[chunk, member],
            device_id=(outer, 2 * to + core),
            device_id_type=MESH,
        )

    def keep_in(chunk):
        return pltpu.make_async_copy(
            stem.at[piece(mine, chunk)], rows_in.at[HALO + member, span(chunk)], in_recv.at[chunk, member]
        )

    def arrived(chunk, block):
        there = rows_in.at[HALO + block, span(chunk)]
        return pltpu.make_async_copy(there, there, in_recv.at[chunk, block])

    def send_halo(chunk, side):
        return pltpu.make_async_remote_copy(
            src_ref=rows_in.at[pl.ds(MEMBERS if side == 0 else HALO, HALO), span(chunk)],
            dst_ref=rows_in.at[pl.ds(0 if side == 0 else HALO + MEMBERS, HALO), span(chunk)],
            send_sem=halo_send.at[chunk, side],
            recv_sem=halo_recv.at[chunk, side],
            device_id=neighbours[side],
            device_id_type=MESH,
        )

    def send_out(chunk, step):
        to = other(step)
        return pltpu.make_async_remote_copy(
            src_ref=rows_out.at[to, span(chunk)],
            dst_ref=tower.at[piece(mine, chunk)],
            send_sem=out_send.at[chunk, step],
            recv_sem=out_recv.at[chunk, mine],
            device_id=(outer, 2 * to + core),
            device_id_type=MESH,
        )

    def keep_out(chunk):
        return pltpu.make_async_copy(
            rows_out.at[member, span(chunk)], tower.at[piece(mine, chunk)], out_recv.at[chunk, mine]
        )

    def returned(chunk, index):
        there = tower.at[piece(index, chunk)]
        return pltpu.make_async_copy(there, there, out_recv.at[chunk, index])

    def start_in(chunk):
        keep_in(chunk).start()
        for step in ORDER:
            send_in(chunk, step).start()

    def start_out(chunk):
        keep_out(chunk).start()
        for step in ORDER:
            send_out(chunk, step).start()

    def forward(chunk):
        for block in range(MEMBERS - HALO, MEMBERS):
            arrived(chunk, block).wait()

        @pl.when(has[0])
        def _():
            send_halo(chunk, 0).start()

        for block in range(HALO):
            arrived(chunk, block).wait()

        @pl.when(has[1])
        def _():
            send_halo(chunk, 1).start()

        for block in range(HALO, MEMBERS - HALO):
            arrived(chunk, block).wait()

    def split(value, into, first, columns=slice(0, 768)):
        high = value.astype(BF16)
        count, start, stop = value.shape[0], columns.start, columns.stop
        into[first : first + count, start:stop] = high
        into[first : first + count, chans + start : chans + stop] = (value - high.astype(F32)).astype(BF16)

    def inside(block):
        if 0 <= block < MEMBERS:
            return 1.0
        number = outer * MEMBERS + block
        return ((number >= 0) & (number < GROUPS * MEMBERS)).astype(F32)

    def conv(source, layer, spread, blocks, columns):
        total = bias[layer : layer + 1, columns]
        for tap in range(3):
            first = tap * spread * rows
            total = total + dot(source[first : first + blocks * rows, :], taps[layer, tap, :, columns])
        return total

    tiles = [slice(start, start + COLUMNS) for start in range(0, chans, COLUMNS)]

    def activate(chunk, blocks):
        for block in blocks:
            split(gelu(rows_in[block, span(chunk)]) * inside(block - HALO), active, block * rows)

    def first_layer(chunk):
        for columns in tiles:
            result = conv(active, 0, 1, MEMBERS + 4, columns)
            for block in range(MEMBERS + 4):
                at = slice(block * rows, (block + 1) * rows)
                total = rows_in[block + 1, span(chunk), columns] + result[at]
                field[at, columns] = total
                split(gelu(total) * inside(block - 2), second, block * rows, columns)

    def second_layer(chunk, columns):
        result = conv(second, 1, 2, MEMBERS, columns)
        for block in range(MEMBERS):
            before = field[(block + 2) * rows : (block + 3) * rows, columns]
            rows_out[block, span(chunk), columns] = before + result[block * rows : (block + 1) * rows]

    def shelf(run, whose):
        return pl.multiple_of((run * 2 + whose) * MEMBERS * MEMBERS, MEMBERS)

    def slot(run, of):
        return pl.ds(shelf(run, core) + shelf_place(of) * MEMBERS, MEMBERS)

    def send_pool(run, step):
        part_of = everyone.at[slot(run, member)]
        return pltpu.make_async_remote_copy(
            src_ref=part_of,
            dst_ref=part_of,
            send_sem=pool_send.at[run, step],
            recv_sem=pool_recv.at[run, member],
            device_id=(outer, 2 * other(step) + core),
            device_id_type=MESH,
        )

    def share(run):
        half = pl.ds(shelf(run, core), MEMBERS * MEMBERS)
        return pltpu.make_async_remote_copy(
            src_ref=everyone.at[half],
            dst_ref=everyone.at[half],
            send_sem=share_send.at[run],
            recv_sem=share_recv.at[run],
            device_id=(outer, inner + 1 - 2 * core),
            device_id_type=MESH,
        )

    def start_pool(run):
        everyone[slot(run, member), :] = jnp.concatenate(
            [
                jnp.sum(rows_out[block, run * POOL : (run + 1) * POOL], axis=0, keepdims=True) * (1.0 / POOL)
                for block in range(MEMBERS)
            ],
            axis=0,
        )
        for step in ORDER:
            send_pool(run, step).start()

    def start_share(run):
        for step in ORDER:
            there = everyone.at[slot(run, other(step))]
            pltpu.make_async_copy(there, there, pool_recv.at[run, other(step)]).wait()
        share(run).start()

    def finish_share(run):
        there = everyone.at[pl.ds(shelf(run, 1 - core), MEMBERS * MEMBERS)]
        pltpu.make_async_copy(there, there, share_recv.at[run]).wait()

    def bring(chunk):
        @pl.when(chunk + AHEAD < CHUNKS)
        def _():
            forward(chunk + AHEAD)

        @pl.when(chunk + AHEAD + IN_FLIGHT < CHUNKS)
        def _():
            start_in(chunk + AHEAD + IN_FLIGHT)

        for side in range(2):

            @pl.when(has[1 - side])
            def _():
                send_halo(chunk, side).wait_recv()

    blocks = range(MEMBERS + 2 * HALO)
    for chunk in range(IN_FLIGHT):
        start_in(chunk)
    for which in every_tap:
        load_taps(*which).start()
    for chunk in range(AHEAD):
        forward(chunk)
        start_in(chunk + IN_FLIGHT)
    bring(0)
    for k in range(4):
        load_heads(k).start()
    activate(0, blocks)
    for which in every_tap:
        load_taps(*which).wait()
    first_layer(0)

    def step_of(chunk, _):
        bring(chunk)
        for k, columns in enumerate(tiles):
            second_layer(chunk - 1, columns)
            activate(chunk, blocks[k :: len(tiles)])
        first_layer(chunk)

        @pl.when(chunk == HELD)
        def _():
            start_out(0)

        @pl.when(chunk >= HELD)
        def _():
            start_out(chunk - HELD + 1)

        @pl.when(chunk == CHUNKS // 2)
        def _():
            start_pool(0)

        @pl.when(chunk == CHUNKS // 2 + 2)
        def _():
            start_share(0)

        return 0

    lax.fori_loop(1, CHUNKS, step_of, 0)
    for columns in tiles:
        second_layer(CHUNKS - 1, columns)
    start_pool(1)
    start_out(CHUNKS - HELD + 1)
    start_share(1)
    for chunk in range(CHUNKS - HELD + 2, CHUNKS):
        start_out(chunk)
    for k in range(4):
        load_heads(k).wait()
    finish_share(0)
    finish_share(1)

    runs = part // POOL
    count = MEMBERS * runs
    total = 2 * MEMBERS * count
    for k, third in enumerate(thirds(everyone[...])):
        split_rows[k * total : (k + 1) * total, :] = third

    def stacked(value, weight):
        size = value.shape[0] // 3
        result = dot(value, weight)
        return (result[2 * size :] + result[size : 2 * size]) + result[:size]

    place = lax.broadcasted_iota(jnp.int32, (count, total), 0)
    wanted = ((place % runs * 2 + core) * MEMBERS + shelf_place(swapped(place // runs, outer))) * MEMBERS + member
    chosen = (lax.broadcasted_iota(jnp.int32, (count, total), 1) == wanted).astype(F32).astype(BF16)
    own_parts = [dot(chosen, split_rows[k * total : (k + 1) * total, :]) for k in range(3)]
    own = (own_parts[2] + own_parts[1]) + own_parts[0]
    own_rows = jnp.concatenate([value.astype(BF16) for value in own_parts], axis=0)
    width = HEADS_AT_ONCE * HEAD_DIM
    head = lax.broadcasted_iota(jnp.int32, (1, width), 1) // HEAD_DIM
    masks = [(head == k).astype(F32) for k in range(HEADS_AT_ONCE)]

    for start in range(0, chans, width):
        columns = slice(start, start + width)
        queries = stacked(own_rows, heads_weight[0, :, columns]) * (HEAD_DIM**-0.5)
        keys = stacked(split_rows[...], heads_weight[1, :, columns])
        vals = stacked(split_rows[...], heads_weight[2, :, columns])
        scores = lax.dot_general(
            jnp.concatenate([queries * mask for mask in masks], axis=0),
            keys,
            (((1,), (1,)), ((), ())),
            precision=lax.Precision.HIGHEST,
            preferred_element_type=F32,
        )
        powers = jnp.exp(scores - jnp.max(scores, axis=1, keepdims=True))
        probs = powers / jnp.sum(powers, axis=1, keepdims=True)
        each = jnp.dot(probs, vals, precision=lax.Precision.HIGHEST, preferred_element_type=F32)
        mixed[:, columns] = sum(each[k * count : (k + 1) * count] * mask for k, mask in enumerate(masks))

    attended[...] = own + stacked(jnp.concatenate(thirds(mixed[...]), axis=0), heads_weight[3])

    for run in range(runs):
        share(run).wait_send()
        for step in ORDER:
            send_pool(run, step).wait_send()

    def finish(chunk, _):
        for side in range(2):

            @pl.when(has[side])
            def _():
                send_halo(chunk, side).wait_send()

        for step in range(1, MEMBERS):
            send_in(chunk, step).wait_send()
            send_out(chunk, step).wait_send()
        for index in range(MEMBERS):
            returned(chunk, index).wait()
        return 0

    lax.fori_loop(0, CHUNKS, finish, 0)


def shards(stem_activity, convolution_weight, convolution_bias, query_weight, key_weight, value_weight, output_weight):
    length, chans = stem_activity.shape
    part = length // MEMBERS
    rows = part // CHUNKS
    blocks = MEMBERS + 2 * HALO
    pooled = length // POOL
    dma, vmem = pltpu.SemaphoreType.DMA, pltpu.VMEM
    far, on_core = pl.BlockSpec(memory_space=pltpu.HBM), pl.BlockSpec(memory_space=vmem)
    return pl.pallas_call(
        tower_kernel,
        out_shape=(
            vmem((length, chans), F32),
            jax.ShapeDtypeStruct((pooled, chans), F32),
        ),
        in_specs=[far, far, on_core, far, far, far, far],
        out_specs=(on_core, on_core),
        scratch_shapes=[
            vmem((blocks, part, chans), F32),
            vmem((MEMBERS, part, chans), F32),
            vmem((2, 3, 2 * chans, chans), BF16),
            vmem((blocks * rows, 2 * chans), BF16),
            vmem(((blocks - 2) * rows, 2 * chans), BF16),
            vmem(((blocks - 2) * rows, chans), F32),
            vmem((2 * MEMBERS * pooled, chans), F32),
            vmem((3 * 2 * MEMBERS * pooled, chans), BF16),
            vmem((pooled, chans), F32),
            vmem((4, chans, chans), BF16),
            dma((2, 3, 2)),
            dma((4,)),
            dma((CHUNKS, MEMBERS)),
            dma((CHUNKS, MEMBERS)),
            dma((CHUNKS, 2)),
            dma((CHUNKS, 2)),
            dma((CHUNKS, MEMBERS)),
            dma((CHUNKS, MEMBERS)),
            dma((2, MEMBERS)),
            dma((2, MEMBERS)),
            dma((2,)),
            dma((2,)),
        ],
        compiler_params=pltpu.CompilerParams(
            collective_id=0, has_side_effects=True, vmem_limit_bytes=50 * 1024 * 1024
        ),
        cost_estimate=pl.CostEstimate(
            flops=5 * 2 * 2 * 3 * length * chans * chans, bytes_accessed=8 * length * chans, transcendentals=0
        ),
        name="tower",
    )(
        stem_activity, convolution_weight, convolution_bias,
        query_weight, key_weight, value_weight, output_weight,
    )


def solution(mesh):
    return jax.shard_map(
        shards,
        mesh=mesh,
        in_specs=(P(("outer", "inner"), None), P(), P(), P(), P(), P(), P()),
        out_specs=(P(("outer", "inner"), None), P(("outer", "inner"), None)),
        check_vma=False,
    )
```

```python
import jax
import jax.numpy as jnp
from jax import lax
from jax.experimental import pallas as pl
from jax.experimental.pallas import tpu as pltpu
from jax.sharding import PartitionSpec as P

HEAD_DIM = 64
POOL = 128
GROUPS = 8
MEMBERS = 8
HALO = 3
CHUNKS = 8
IN_FLIGHT = 3
HELD = 4
AHEAD = 1
COLUMNS = 256
ORDER = (1, 2, 6, 5, 4, 3, 7)
ROUND = (2, 4, 6)
HEADS_AT_ONCE = 4
WRITES = 16
MESH = pl.DeviceIdType.MESH
F32, BF16 = jnp.float32, jnp.bfloat16


def gelu(x):
    return 0.5 * x * (1.0 + lax.erf(x * (0.5**0.5)))


def dot(left, right):
    return jnp.dot(left, right, preferred_element_type=F32)


def thirds(value):
    high = value.astype(BF16)
    rest = value - high.astype(F32)
    middle = rest.astype(BF16)
    return high, middle, (rest - middle.astype(F32)).astype(BF16)


def swapped(member, outer):
    return member // 2 * 2 + (member + outer // 4) % 2


def shelf_place(member):
    return member % 2 * (MEMBERS // 2) + member // 2


def tower_kernel(
    stem, weight, bias, query_weight, key_weight, value_weight, output_weight,
    tower, attended,
    rows_in, rows_out, taps, active, second, field, everyone, split_rows, mixed, heads_weight,
    weight_sem, heads_sem, in_send, in_recv, halo_send, halo_recv, out_send, out_recv,
    pool_send, pool_recv, share_send, share_recv,
):
    outer, inner = lax.axis_index("outer"), lax.axis_index("inner")
    member, core = inner // 2, inner % 2
    chans = stem.shape[1]
    part = stem.shape[0] // MEMBERS
    rows = part // CHUNKS
    mine = swapped(member, outer)
    up, down = (outer + 1) % GROUPS, (outer + GROUPS - 1) % GROUPS
    neighbours = (
        (up, 2 * swapped(mine, up) + core),
        (down, 2 * swapped(mine, down) + core),
    )

    has = (outer < GROUPS - 1, outer > 0)

    def other(step):
        way = step // 2
        return (member // 2 + way + core * (4 - 2 * way)) % 4 * 2 + (member + step) % 2

    barrier = pltpu.get_barrier_semaphore()

    def greet(device):
        pl.semaphore_signal(barrier, inc=1, device_id=device, device_id_type=MESH)

    for step in range(1, MEMBERS):
        greet((outer, 2 * other(step) + core))
    greet((outer, inner + 1 - 2 * core))
    for neighbour, there in zip(neighbours, has):

        @pl.when(there)
        def _():
            greet(neighbour)


    def load_taps(layer, tap, half):
        return pltpu.make_async_copy(
            weight.at[layer, tap],
            taps.at[layer, tap, pl.ds(half * chans, chans)],
            weight_sem.at[layer, tap, half],
        )

    def load_heads(k):
        source = (query_weight, key_weight, value_weight, output_weight)[k]
        return pltpu.make_async_copy(source, heads_weight.at[k], heads_sem.at[k])

    every_tap = [(layer, tap, half) for layer in range(2) for tap in range(3) for half in range(2)]
    for side in range(2):
        @pl.when(jnp.logical_not(has[side]))
        def _():
            rows_in[0 if side else HALO + MEMBERS : HALO if side else 2 * HALO + MEMBERS] = jnp.zeros(
                (HALO, part, chans), F32
            )

    pl.semaphore_wait(barrier, MEMBERS + has[0].astype(jnp.int32) + has[1].astype(jnp.int32))

    def span(chunk):
        return pl.ds(pl.multiple_of(chunk * rows, rows), rows)

    def piece(index, chunk):
        return pl.ds(pl.multiple_of(index * part + chunk * rows, rows), rows)

    def send_in(chunk, step):
        to = other(step)
        return pltpu.make_async_remote_copy(
            src_ref=stem.at[piece(swapped(to, outer), chunk)],
            dst_ref=rows_in.at[HALO + member, span(chunk)],
            send_sem=in_send.at[chunk, step],
            recv_sem=in_recv.at[chunk, member],
            device_id=(outer, 2 * to + core),
            device_id_type=MESH,
        )

    def keep_in(chunk):
        return pltpu.make_async_copy(
            stem.at[piece(mine, chunk)], rows_in.at[HALO + member, span(chunk)], in_recv.at[chunk, member]
        )

    def arrived(chunk, block):
        there = rows_in.at[HALO + block, span(chunk)]
        return pltpu.make_async_copy(there, there, in_recv.at[chunk, block])

    def send_halo(chunk, side):
        return pltpu.make_async_remote_copy(
            src_ref=rows_in.at[pl.ds(MEMBERS if side == 0 else HALO, HALO), span(chunk)],
            dst_ref=rows_in.at[pl.ds(0 if side == 0 else HALO + MEMBERS, HALO), span(chunk)],
            send_sem=halo_send.at[chunk, side],
            recv_sem=halo_recv.at[chunk, side],
            device_id=neighbours[side],
            device_id_type=MESH,
        )

    def send_out(chunk, step):
        to = other(step)
        return pltpu.make_async_remote_copy(
            src_ref=rows_out.at[to, span(chunk)],
            dst_ref=tower.at[piece(mine, chunk)],
            send_sem=out_send.at[chunk, step],
            recv_sem=out_recv.at[chunk, mine],
            device_id=(outer, 2 * to + core),
            device_id_type=MESH,
        )

    def keep_out(chunk):
        return pltpu.make_async_copy(
            rows_out.at[member, span(chunk)], tower.at[piece(mine, chunk)], out_recv.at[chunk, mine]
        )

    def returned(chunk, index):
        there = tower.at[piece(index, chunk)]
        return pltpu.make_async_copy(there, there, out_recv.at[chunk, index])

    def start_in(chunk):
        keep_in(chunk).start()
        for step in ORDER:
            send_in(chunk, step).start()

    def start_out(chunk):
        keep_out(chunk).start()
        for step in ORDER:
            send_out(chunk, step).start()

    def forward(chunk):
        for block in range(MEMBERS - HALO, MEMBERS):
            arrived(chunk, block).wait()

        @pl.when(has[0])
        def _():
            send_halo(chunk, 0).start()

        for block in range(HALO):
            arrived(chunk, block).wait()

        @pl.when(has[1])
        def _():
            send_halo(chunk, 1).start()

        for block in range(HALO, MEMBERS - HALO):
            arrived(chunk, block).wait()

    def split(value, into, first, columns=slice(0, 768)):
        high = value.astype(BF16)
        count, start, stop = value.shape[0], columns.start, columns.stop
        into[first : first + count, start:stop] = high
        into[first : first + count, chans + start : chans + stop] = (value - high.astype(F32)).astype(BF16)

    def inside(block):
        if 0 <= block < MEMBERS:
            return 1.0
        number = outer * MEMBERS + block
        return ((number >= 0) & (number < GROUPS * MEMBERS)).astype(F32)

    def conv(source, layer, spread, blocks, columns):
        total = bias[layer : layer + 1, columns]
        for tap in range(3):
            first = tap * spread * rows
            total = total + dot(source[first : first + blocks * rows, :], taps[layer, tap, :, columns])
        return total

    tiles = [slice(start, start + COLUMNS) for start in range(0, chans, COLUMNS)]

    def activate(chunk, blocks):
        for block in blocks:
            split(gelu(rows_in[block, span(chunk)]) * inside(block - HALO), active, block * rows)

    def first_layer(chunk):
        for columns in tiles:
            result = conv(active, 0, 1, MEMBERS + 4, columns)
            for block in range(MEMBERS + 4):
                at = slice(block * rows, (block + 1) * rows)
                total = rows_in[block + 1, span(chunk), columns] + result[at]
                field[at, columns] = total
                split(gelu(total) * inside(block - 2), second, block * rows, columns)

    def second_layer(chunk, columns):
        result = conv(second, 1, 2, MEMBERS, columns)
        for block in range(MEMBERS):
            before = field[(block + 2) * rows : (block + 3) * rows, columns]
            rows_out[block, span(chunk), columns] = before + result[block * rows : (block + 1) * rows]

    def shelf(run, whose):
        return pl.multiple_of((run * 2 + whose) * MEMBERS * MEMBERS, MEMBERS)

    def slot(run, of):
        return pl.ds(shelf(run, core) + shelf_place(of) * MEMBERS, MEMBERS)

    def column(run, of):
        return pl.ds(shelf(run, core) + of % 2 * (MEMBERS // 2 * MEMBERS), MEMBERS // 2 * MEMBERS)

    def send_pool(run, step):
        part_of = everyone.at[column(run, member) if step == 1 else slot(run, member)]
        return pltpu.make_async_remote_copy(
            src_ref=part_of,
            dst_ref=part_of,
            send_sem=pool_send.at[run, step],
            recv_sem=pool_recv.at[run, member],
            device_id=(outer, 2 * other(step) + core),
            device_id_type=MESH,
        )

    def share(run):
        half = pl.ds(shelf(run, core), MEMBERS * MEMBERS)
        return pltpu.make_async_remote_copy(
            src_ref=everyone.at[half],
            dst_ref=everyone.at[half],
            send_sem=share_send.at[run],
            recv_sem=share_recv.at[run],
            device_id=(outer, inner + 1 - 2 * core),
            device_id_type=MESH,
        )

    def start_pool(run):
        everyone[slot(run, member), :] = jnp.concatenate(
            [
                jnp.sum(rows_out[block, run * POOL : (run + 1) * POOL], axis=0, keepdims=True) * (1.0 / POOL)
                for block in range(MEMBERS)
            ],
            axis=0,
        )
        for step in ROUND:
            send_pool(run, step).start()

    def pass_pool(run):
        for step in ROUND:
            there = everyone.at[slot(run, other(step))]
            pltpu.make_async_copy(there, there, pool_recv.at[run, other(step)]).wait()
        send_pool(run, 1).start()

    def start_share(run):
        there = everyone.at[column(run, other(1))]
        pltpu.make_async_copy(there, there, pool_recv.at[run, other(1)]).wait()
        share(run).start()

    def finish_share(run):
        there = everyone.at[pl.ds(shelf(run, 1 - core), MEMBERS * MEMBERS)]
        pltpu.make_async_copy(there, there, share_recv.at[run]).wait()

    def bring(chunk):
        @pl.when(chunk + AHEAD < CHUNKS)
        def _():
            forward(chunk + AHEAD)

        @pl.when(chunk + AHEAD + IN_FLIGHT < CHUNKS)
        def _():
            start_in(chunk + AHEAD + IN_FLIGHT)

        for side in range(2):

            @pl.when(has[1 - side])
            def _():
                send_halo(chunk, side).wait_recv()

    blocks = range(MEMBERS + 2 * HALO)
    for chunk in range(IN_FLIGHT):
        start_in(chunk)
    for which in every_tap:
        load_taps(*which).start()
    for chunk in range(AHEAD):
        forward(chunk)
        start_in(chunk + IN_FLIGHT)
    bring(0)
    for k in range(4):
        load_heads(k).start()
    activate(0, blocks)
    for which in every_tap:
        load_taps(*which).wait()
    first_layer(0)

    def step_of(chunk, _):
        bring(chunk)
        for k, columns in enumerate(tiles):
            second_layer(chunk - 1, columns)
            activate(chunk, blocks[k :: len(tiles)])
        first_layer(chunk)

        @pl.when(chunk == HELD)
        def _():
            start_out(0)

        @pl.when(chunk >= HELD)
        def _():
            start_out(chunk - HELD + 1)

        @pl.when(chunk == CHUNKS // 2)
        def _():
            start_pool(0)

        @pl.when(chunk == CHUNKS // 2 + 1)
        def _():
            pass_pool(0)

        @pl.when(chunk == CHUNKS // 2 + 2)
        def _():
            start_share(0)

        return 0

    lax.fori_loop(1, CHUNKS, step_of, 0)
    for columns in tiles:
        second_layer(CHUNKS - 1, columns)
    start_pool(1)
    start_out(CHUNKS - HELD + 1)
    pass_pool(1)
    start_out(CHUNKS - HELD + 2)
    start_share(1)
    for chunk in range(CHUNKS - HELD + 3, CHUNKS):
        start_out(chunk)
    for k in range(4):
        load_heads(k).wait()
    finish_share(0)
    finish_share(1)

    runs = part // POOL
    count = MEMBERS * runs
    total = 2 * MEMBERS * count
    for k, third in enumerate(thirds(everyone[...])):
        split_rows[k * total : (k + 1) * total, :] = third

    def stacked(value, weight):
        size = value.shape[0] // 3
        result = dot(value, weight)
        return (result[2 * size :] + result[size : 2 * size]) + result[:size]

    place = lax.broadcasted_iota(jnp.int32, (count, total), 0)
    wanted = ((place % runs * 2 + core) * MEMBERS + shelf_place(swapped(place // runs, outer))) * MEMBERS + member
    chosen = (lax.broadcasted_iota(jnp.int32, (count, total), 1) == wanted).astype(F32).astype(BF16)
    own_parts = [dot(chosen, split_rows[k * total : (k + 1) * total, :]) for k in range(3)]
    own = (own_parts[2] + own_parts[1]) + own_parts[0]
    own_rows = jnp.concatenate([value.astype(BF16) for value in own_parts], axis=0)
    width = HEADS_AT_ONCE * HEAD_DIM
    head = lax.broadcasted_iota(jnp.int32, (1, width), 1) // HEAD_DIM
    masks = [(head == k).astype(F32) for k in range(HEADS_AT_ONCE)]

    for start in range(0, chans, width):
        columns = slice(start, start + width)
        queries = stacked(own_rows, heads_weight[0, :, columns]) * (HEAD_DIM**-0.5)
        keys = stacked(split_rows[...], heads_weight[1, :, columns])
        vals = stacked(split_rows[...], heads_weight[2, :, columns])
        scores = lax.dot_general(
            jnp.concatenate([queries * mask for mask in masks], axis=0),
            keys,
            (((1,), (1,)), ((), ())),
            precision=lax.Precision.HIGHEST,
            preferred_element_type=F32,
        )
        powers = jnp.exp(scores - jnp.max(scores, axis=1, keepdims=True))
        probs = powers / jnp.sum(powers, axis=1, keepdims=True)
        each = jnp.dot(probs, vals, precision=lax.Precision.HIGHEST, preferred_element_type=F32)
        mixed[:, columns] = sum(each[k * count : (k + 1) * count] * mask for k, mask in enumerate(masks))

    attended[...] = own + stacked(jnp.concatenate(thirds(mixed[...]), axis=0), heads_weight[3])

    for run in range(runs):
        share(run).wait_send()
        for step in (1, *ROUND):
            send_pool(run, step).wait_send()

    def finish(chunk, _):
        for side in range(2):

            @pl.when(has[side])
            def _():
                send_halo(chunk, side).wait_send()

        for step in range(1, MEMBERS):
            send_in(chunk, step).wait_send()
            send_out(chunk, step).wait_send()
        for index in range(MEMBERS):
            returned(chunk, index).wait()
        return 0

    lax.fori_loop(0, CHUNKS, finish, 0)


def write_kernel(tower, attended, tower_out, attended_out, sems):
    size = tower.shape[0] // WRITES
    copies = [
        pltpu.make_async_copy(tower.at[pl.ds(k * size, size)], tower_out.at[pl.ds(k * size, size)], sems.at[k])
        for k in range(WRITES)
    ]
    copies.append(pltpu.make_async_copy(attended, attended_out, sems.at[WRITES]))
    for copy in copies:
        copy.start()
    for copy in copies:
        copy.wait()


def shards(stem_activity, convolution_weight, convolution_bias, query_weight, key_weight, value_weight, output_weight):
    length, chans = stem_activity.shape
    part = length // MEMBERS
    rows = part // CHUNKS
    blocks = MEMBERS + 2 * HALO
    pooled = length // POOL
    dma, vmem = pltpu.SemaphoreType.DMA, pltpu.VMEM
    far, on_core = pl.BlockSpec(memory_space=pltpu.HBM), pl.BlockSpec(memory_space=vmem)
    results = pl.pallas_call(
        tower_kernel,
        out_shape=(
            vmem((length, chans), F32),
            vmem((pooled, chans), F32),
        ),
        in_specs=[far, far, on_core, far, far, far, far],
        out_specs=(on_core, on_core),
        scratch_shapes=[
            vmem((blocks, part, chans), F32),
            vmem((MEMBERS, part, chans), F32),
            vmem((2, 3, 2 * chans, chans), BF16),
            vmem((blocks * rows, 2 * chans), BF16),
            vmem(((blocks - 2) * rows, 2 * chans), BF16),
            vmem(((blocks - 2) * rows, chans), F32),
            vmem((2 * MEMBERS * pooled, chans), F32),
            vmem((3 * 2 * MEMBERS * pooled, chans), BF16),
            vmem((pooled, chans), F32),
            vmem((4, chans, chans), BF16),
            dma((2, 3, 2)),
            dma((4,)),
            dma((CHUNKS, MEMBERS)),
            dma((CHUNKS, MEMBERS)),
            dma((CHUNKS, 2)),
            dma((CHUNKS, 2)),
            dma((CHUNKS, MEMBERS)),
            dma((CHUNKS, MEMBERS)),
            dma((2, MEMBERS)),
            dma((2, MEMBERS)),
            dma((2,)),
            dma((2,)),
        ],
        compiler_params=pltpu.CompilerParams(
            collective_id=0, has_side_effects=True, vmem_limit_bytes=50 * 1024 * 1024
        ),
        cost_estimate=pl.CostEstimate(
            flops=5 * 2 * 2 * 3 * length * chans * chans, bytes_accessed=8 * length * chans, transcendentals=0
        ),
        name="tower",
    )(
        stem_activity, convolution_weight, convolution_bias,
        query_weight, key_weight, value_weight, output_weight,
    )
    return pl.pallas_call(
        write_kernel,
        out_shape=[jax.ShapeDtypeStruct(result.shape, F32) for result in results],
        in_specs=[on_core, on_core],
        out_specs=[far, far],
        scratch_shapes=[dma((WRITES + 1,))],
        cost_estimate=pl.CostEstimate(flops=0, bytes_accessed=8 * length * chans, transcendentals=0),
        name="write",
    )(*results)


def solution(mesh):
    return jax.shard_map(
        shards,
        mesh=mesh,
        in_specs=(P(("outer", "inner"), None), P(), P(), P(), P(), P(), P()),
        out_specs=(P(("outer", "inner"), None), P(("outer", "inner"), None)),
        check_vma=False,
    )
```

```python
import jax
import jax.numpy as jnp
from jax import lax
from jax.experimental import pallas as pl
from jax.experimental.pallas import tpu as pltpu
from jax.sharding import PartitionSpec as P

HEAD_DIM = 64
POOL = 128
GROUPS = 8
MEMBERS = 8
HALO = 3
CHUNKS = 8
IN_FLIGHT = 3
HELD = 4
AHEAD = 1
COLUMNS = 256
ORDER = (1, 2, 6, 5, 4, 3, 7)
ROUND = (2, 4, 6)
HEADS_AT_ONCE = 4
MESH = pl.DeviceIdType.MESH
F32, BF16 = jnp.float32, jnp.bfloat16


def gelu(x):
    return 0.5 * x * (1.0 + lax.erf(x * (0.5**0.5)))


def dot(left, right):
    return jnp.dot(left, right, preferred_element_type=F32)


def thirds(value):
    high = value.astype(BF16)
    rest = value - high.astype(F32)
    middle = rest.astype(BF16)
    return high, middle, (rest - middle.astype(F32)).astype(BF16)


def swapped(member, outer):
    return member // 2 * 2 + (member + outer // 4) % 2


def shelf_place(member):
    return member % 2 * (MEMBERS // 2) + member // 2


def tower_kernel(
    stem, weight, bias, query_weight, key_weight, value_weight, output_weight,
    tower, attended,
    rows_in, rows_out, taps, active, second, field, everyone, split_rows, mixed, heads_weight,
    weight_sem, heads_sem, in_send, in_recv, halo_send, halo_recv, out_send, out_recv,
    pool_send, pool_recv, share_send, share_recv,
):
    outer, inner = lax.axis_index("outer"), lax.axis_index("inner")
    member, core = inner // 2, inner % 2
    chans = stem.shape[1]
    part = stem.shape[0] // MEMBERS
    rows = part // CHUNKS
    mine = swapped(member, outer)
    up, down = (outer + 1) % GROUPS, (outer + GROUPS - 1) % GROUPS
    neighbours = (
        (up, 2 * swapped(mine, up) + core),
        (down, 2 * swapped(mine, down) + core),
    )

    has = (outer < GROUPS - 1, outer > 0)

    def other(step):
        way = step // 2
        return (member // 2 + way + core * (4 - 2 * way)) % 4 * 2 + (member + step) % 2

    barrier = pltpu.get_barrier_semaphore()

    def greet(device):
        pl.semaphore_signal(barrier, inc=1, device_id=device, device_id_type=MESH)

    for step in range(1, MEMBERS):
        greet((outer, 2 * other(step) + core))
    greet((outer, inner + 1 - 2 * core))
    for neighbour, there in zip(neighbours, has):

        @pl.when(there)
        def _():
            greet(neighbour)


    def load_taps(layer, tap, half):
        return pltpu.make_async_copy(
            weight.at[layer, tap],
            taps.at[layer, tap, pl.ds(half * chans, chans)],
            weight_sem.at[layer, tap, half],
        )

    def load_heads(k):
        source = (query_weight, key_weight, value_weight, output_weight)[k]
        return pltpu.make_async_copy(source, heads_weight.at[k], heads_sem.at[k])

    every_tap = [(layer, tap, half) for layer in range(2) for tap in range(3) for half in range(2)]
    pl.semaphore_wait(barrier, MEMBERS + has[0].astype(jnp.int32) + has[1].astype(jnp.int32))

    def span(chunk):
        return pl.ds(pl.multiple_of(chunk * rows, rows), rows)

    def piece(index, chunk):
        return pl.ds(pl.multiple_of(index * part + chunk * rows, rows), rows)

    def send_in(chunk, step):
        to = other(step)
        return pltpu.make_async_remote_copy(
            src_ref=stem.at[piece(swapped(to, outer), chunk)],
            dst_ref=rows_in.at[HALO + member, span(chunk)],
            send_sem=in_send.at[chunk, step],
            recv_sem=in_recv.at[chunk, member],
            device_id=(outer, 2 * to + core),
            device_id_type=MESH,
        )

    def keep_in(chunk):
        return pltpu.make_async_copy(
            stem.at[piece(mine, chunk)], rows_in.at[HALO + member, span(chunk)], in_recv.at[chunk, member]
        )

    def arrived(chunk, block):
        there = rows_in.at[HALO + block, span(chunk)]
        return pltpu.make_async_copy(there, there, in_recv.at[chunk, block])

    def send_halo(chunk, side):
        return pltpu.make_async_remote_copy(
            src_ref=rows_in.at[pl.ds(MEMBERS if side == 0 else HALO, HALO), span(chunk)],
            dst_ref=rows_in.at[pl.ds(0 if side == 0 else HALO + MEMBERS, HALO), span(chunk)],
            send_sem=halo_send.at[chunk, side],
            recv_sem=halo_recv.at[chunk, side],
            device_id=neighbours[side],
            device_id_type=MESH,
        )

    def send_out(chunk, step):
        to = other(step)
        return pltpu.make_async_remote_copy(
            src_ref=rows_out.at[to, span(chunk)],
            dst_ref=tower.at[piece(mine, chunk)],
            send_sem=out_send.at[chunk, step],
            recv_sem=out_recv.at[chunk, mine],
            device_id=(outer, 2 * to + core),
            device_id_type=MESH,
        )

    def keep_out(chunk):
        return pltpu.make_async_copy(
            rows_out.at[member, span(chunk)], tower.at[piece(mine, chunk)], out_recv.at[chunk, mine]
        )

    def returned(chunk, index):
        there = tower.at[piece(index, chunk)]
        return pltpu.make_async_copy(there, there, out_recv.at[chunk, index])

    def start_in(chunk):
        keep_in(chunk).start()
        for step in ORDER:
            send_in(chunk, step).start()

    def start_out(chunk):
        keep_out(chunk).start()
        for step in ORDER:
            send_out(chunk, step).start()

    def forward(chunk):
        for block in range(MEMBERS - HALO, MEMBERS):
            arrived(chunk, block).wait()

        @pl.when(has[0])
        def _():
            send_halo(chunk, 0).start()

        for block in range(HALO):
            arrived(chunk, block).wait()

        @pl.when(has[1])
        def _():
            send_halo(chunk, 1).start()

        for block in range(HALO, MEMBERS - HALO):
            arrived(chunk, block).wait()

    def split(value, into, first, columns=slice(0, 768)):
        high = value.astype(BF16)
        count, start, stop = value.shape[0], columns.start, columns.stop
        into[first : first + count, start:stop] = high
        into[first : first + count, chans + start : chans + stop] = (value - high.astype(F32)).astype(BF16)

    def inside(block):
        if 0 <= block < MEMBERS:
            return 1.0
        number = outer * MEMBERS + block
        return ((number >= 0) & (number < GROUPS * MEMBERS)).astype(F32)

    def conv(source, layer, spread, blocks, columns):
        total = bias[layer : layer + 1, columns]
        for tap in range(3):
            first = tap * spread * rows
            total = total + dot(source[first : first + blocks * rows, :], taps[layer, tap, :, columns])
        return total

    tiles = [slice(start, start + COLUMNS) for start in range(0, chans, COLUMNS)]

    def activate(chunk, blocks):
        for block in blocks:
            split(gelu(rows_in[block, span(chunk)]) * inside(block - HALO), active, block * rows)

    def first_layer(chunk):
        for columns in tiles:
            result = conv(active, 0, 1, MEMBERS + 4, columns)
            for block in range(MEMBERS + 4):
                at = slice(block * rows, (block + 1) * rows)
                total = rows_in[block + 1, span(chunk), columns] + result[at]
                field[at, columns] = total
                split(gelu(total) * inside(block - 2), second, block * rows, columns)

    def second_layer(chunk, columns):
        result = conv(second, 1, 2, MEMBERS, columns)
        for block in range(MEMBERS):
            before = field[(block + 2) * rows : (block + 3) * rows, columns]
            rows_out[block, span(chunk), columns] = before + result[block * rows : (block + 1) * rows]

    def shelf(run, whose):
        return pl.multiple_of((run * 2 + whose) * MEMBERS * MEMBERS, MEMBERS)

    def slot(run, of):
        return pl.ds(shelf(run, core) + shelf_place(of) * MEMBERS, MEMBERS)

    def column(run, of):
        return pl.ds(shelf(run, core) + of % 2 * (MEMBERS // 2 * MEMBERS), MEMBERS // 2 * MEMBERS)

    def send_pool(run, step):
        part_of = everyone.at[column(run, member) if step == 1 else slot(run, member)]
        return pltpu.make_async_remote_copy(
            src_ref=part_of,
            dst_ref=part_of,
            send_sem=pool_send.at[run, step],
            recv_sem=pool_recv.at[run, member],
            device_id=(outer, 2 * other(step) + core),
            device_id_type=MESH,
        )

    def share(run):
        half = pl.ds(shelf(run, core), MEMBERS * MEMBERS)
        return pltpu.make_async_remote_copy(
            src_ref=everyone.at[half],
            dst_ref=everyone.at[half],
            send_sem=share_send.at[run],
            recv_sem=share_recv.at[run],
            device_id=(outer, inner + 1 - 2 * core),
            device_id_type=MESH,
        )

    def start_pool(run):
        everyone[slot(run, member), :] = jnp.concatenate(
            [
                jnp.sum(rows_out[block, run * POOL : (run + 1) * POOL], axis=0, keepdims=True) * (1.0 / POOL)
                for block in range(MEMBERS)
            ],
            axis=0,
        )
        for step in ROUND:
            send_pool(run, step).start()

    def pass_pool(run):
        for step in ROUND:
            there = everyone.at[slot(run, other(step))]
            pltpu.make_async_copy(there, there, pool_recv.at[run, other(step)]).wait()
        send_pool(run, 1).start()

    def start_share(run):
        there = everyone.at[column(run, other(1))]
        pltpu.make_async_copy(there, there, pool_recv.at[run, other(1)]).wait()
        share(run).start()

    def finish_share(run):
        there = everyone.at[pl.ds(shelf(run, 1 - core), MEMBERS * MEMBERS)]
        pltpu.make_async_copy(there, there, share_recv.at[run]).wait()

    def bring(chunk):
        @pl.when(chunk + AHEAD < CHUNKS)
        def _():
            forward(chunk + AHEAD)

        @pl.when(chunk + AHEAD + IN_FLIGHT < CHUNKS)
        def _():
            start_in(chunk + AHEAD + IN_FLIGHT)

        for side in range(2):

            @pl.when(has[1 - side])
            def _():
                send_halo(chunk, side).wait_recv()

    blocks = range(MEMBERS + 2 * HALO)
    for chunk in range(IN_FLIGHT):
        start_in(chunk)
    for which in every_tap:
        load_taps(*which).start()
    for side in range(2):
        @pl.when(jnp.logical_not(has[side]))
        def _():
            rows_in[0 if side else HALO + MEMBERS : HALO if side else 2 * HALO + MEMBERS] = jnp.zeros(
                (HALO, part, chans), F32
            )

    for chunk in range(AHEAD):
        forward(chunk)
        start_in(chunk + IN_FLIGHT)
    bring(0)
    for k in range(4):
        load_heads(k).start()
    activate(0, blocks)
    for which in every_tap:
        load_taps(*which).wait()
    first_layer(0)

    def step_of(chunk, _):
        bring(chunk)
        for k, columns in enumerate(tiles):
            second_layer(chunk - 1, columns)
            activate(chunk, blocks[k :: len(tiles)])
        first_layer(chunk)

        @pl.when(chunk == HELD)
        def _():
            start_out(0)

        @pl.when(chunk >= HELD)
        def _():
            start_out(chunk - HELD + 1)

        @pl.when(chunk == CHUNKS // 2)
        def _():
            start_pool(0)

        @pl.when(chunk == CHUNKS // 2 + 1)
        def _():
            pass_pool(0)

        @pl.when(chunk == CHUNKS // 2 + 2)
        def _():
            start_share(0)

        return 0

    lax.fori_loop(1, CHUNKS, step_of, 0)
    for columns in tiles:
        second_layer(CHUNKS - 1, columns)
    start_pool(1)
    start_out(CHUNKS - HELD + 1)
    pass_pool(1)
    start_out(CHUNKS - HELD + 2)
    start_share(1)
    for chunk in range(CHUNKS - HELD + 3, CHUNKS):
        start_out(chunk)
    for k in range(4):
        load_heads(k).wait()
    finish_share(0)
    finish_share(1)

    runs = part // POOL
    count = MEMBERS * runs
    total = 2 * MEMBERS * count
    for k, third in enumerate(thirds(everyone[...])):
        split_rows[k * total : (k + 1) * total, :] = third

    def stacked(value, weight):
        size = value.shape[0] // 3
        result = dot(value, weight)
        return (result[2 * size :] + result[size : 2 * size]) + result[:size]

    place = lax.broadcasted_iota(jnp.int32, (count, total), 0)
    wanted = ((place % runs * 2 + core) * MEMBERS + shelf_place(swapped(place // runs, outer))) * MEMBERS + member
    chosen = (lax.broadcasted_iota(jnp.int32, (count, total), 1) == wanted).astype(F32).astype(BF16)
    own_parts = [dot(chosen, split_rows[k * total : (k + 1) * total, :]) for k in range(3)]
    own = (own_parts[2] + own_parts[1]) + own_parts[0]
    own_rows = jnp.concatenate([value.astype(BF16) for value in own_parts], axis=0)
    width = HEADS_AT_ONCE * HEAD_DIM
    head = lax.broadcasted_iota(jnp.int32, (1, width), 1) // HEAD_DIM
    masks = [(head == k).astype(F32) for k in range(HEADS_AT_ONCE)]

    for start in range(0, chans, width):
        columns = slice(start, start + width)
        queries = stacked(own_rows, heads_weight[0, :, columns]) * (HEAD_DIM**-0.5)
        keys = stacked(split_rows[...], heads_weight[1, :, columns])
        vals = stacked(split_rows[...], heads_weight[2, :, columns])
        scores = lax.dot_general(
            jnp.concatenate([queries * mask for mask in masks], axis=0),
            keys,
            (((1,), (1,)), ((), ())),
            precision=lax.Precision.HIGHEST,
            preferred_element_type=F32,
        )
        powers = jnp.exp(scores - jnp.max(scores, axis=1, keepdims=True))
        probs = powers / jnp.sum(powers, axis=1, keepdims=True)
        each = jnp.dot(probs, vals, precision=lax.Precision.HIGHEST, preferred_element_type=F32)
        mixed[:, columns] = sum(each[k * count : (k + 1) * count] * mask for k, mask in enumerate(masks))

    attended[...] = own + stacked(jnp.concatenate(thirds(mixed[...]), axis=0), heads_weight[3])

    for run in range(runs):
        share(run).wait_send()
        for step in (1, *ROUND):
            send_pool(run, step).wait_send()

    def finish(chunk, _):
        for side in range(2):

            @pl.when(has[side])
            def _():
                send_halo(chunk, side).wait_send()

        for step in range(1, MEMBERS):
            send_in(chunk, step).wait_send()
            send_out(chunk, step).wait_send()
        for index in range(MEMBERS):
            returned(chunk, index).wait()
        return 0

    lax.fori_loop(0, CHUNKS, finish, 0)


def shards(stem_activity, convolution_weight, convolution_bias, query_weight, key_weight, value_weight, output_weight):
    length, chans = stem_activity.shape
    part = length // MEMBERS
    rows = part // CHUNKS
    blocks = MEMBERS + 2 * HALO
    pooled = length // POOL
    dma, vmem = pltpu.SemaphoreType.DMA, pltpu.VMEM
    far, on_core = pl.BlockSpec(memory_space=pltpu.HBM), pl.BlockSpec(memory_space=vmem)
    return pl.pallas_call(
        tower_kernel,
        out_shape=(
            vmem((length, chans), F32),
            jax.ShapeDtypeStruct((pooled, chans), F32),
        ),
        in_specs=[far, far, on_core, far, far, far, far],
        out_specs=(on_core, on_core),
        scratch_shapes=[
            vmem((blocks, part, chans), F32),
            vmem((MEMBERS, part, chans), F32),
            vmem((2, 3, 2 * chans, chans), BF16),
            vmem((blocks * rows, 2 * chans), BF16),
            vmem(((blocks - 2) * rows, 2 * chans), BF16),
            vmem(((blocks - 2) * rows, chans), F32),
            vmem((2 * MEMBERS * pooled, chans), F32),
            vmem((3 * 2 * MEMBERS * pooled, chans), BF16),
            vmem((pooled, chans), F32),
            vmem((4, chans, chans), BF16),
            dma((2, 3, 2)),
            dma((4,)),
            dma((CHUNKS, MEMBERS)),
            dma((CHUNKS, MEMBERS)),
            dma((CHUNKS, 2)),
            dma((CHUNKS, 2)),
            dma((CHUNKS, MEMBERS)),
            dma((CHUNKS, MEMBERS)),
            dma((2, MEMBERS)),
            dma((2, MEMBERS)),
            dma((2,)),
            dma((2,)),
        ],
        compiler_params=pltpu.CompilerParams(
            collective_id=0, has_side_effects=True, vmem_limit_bytes=50 * 1024 * 1024
        ),
        cost_estimate=pl.CostEstimate(
            flops=5 * 2 * 2 * 3 * length * chans * chans, bytes_accessed=8 * length * chans, transcendentals=0
        ),
        name="tower",
    )(
        stem_activity, convolution_weight, convolution_bias,
        query_weight, key_weight, value_weight, output_weight,
    )


def solution(mesh):
    return jax.shard_map(
        shards,
        mesh=mesh,
        in_specs=(P(("outer", "inner"), None), P(), P(), P(), P(), P(), P()),
        out_specs=(P(("outer", "inner"), None), P(("outer", "inner"), None)),
        check_vma=False,
    )
```

```python
import jax
import jax.numpy as jnp
from jax import lax
from jax.experimental import pallas as pl
from jax.experimental.pallas import tpu as pltpu
from jax.sharding import PartitionSpec as P

HEAD_DIM = 64
POOL = 128
GROUPS = 8
MEMBERS = 8
HALO = 3
CHUNKS = 8
IN_FLIGHT = 6
HELD = 4
AHEAD = 1
COLUMNS = 256
ORDER = (1, 2, 6, 5, 4, 3, 7)
ROUND = (2, 4, 6)
HEADS_AT_ONCE = 4
MESH = pl.DeviceIdType.MESH
F32, BF16 = jnp.float32, jnp.bfloat16


def gelu(x):
    return 0.5 * x * (1.0 + lax.erf(x * (0.5**0.5)))


def dot(left, right):
    return jnp.dot(left, right, preferred_element_type=F32)


def thirds(value):
    high = value.astype(BF16)
    rest = value - high.astype(F32)
    middle = rest.astype(BF16)
    return high, middle, (rest - middle.astype(F32)).astype(BF16)


def swapped(member, outer):
    return member // 2 * 2 + (member + outer // 4) % 2


def shelf_place(member):
    return member % 2 * (MEMBERS // 2) + member // 2


def tower_kernel(
    stem, weight, bias, query_weight, key_weight, value_weight, output_weight,
    tower, attended,
    rows_in, rows_out, taps, active, second, field, everyone, split_rows, mixed, heads_weight,
    weight_sem, heads_sem, in_send, in_recv, halo_send, halo_recv, out_send, out_recv,
    pool_send, pool_recv, share_send, share_recv,
):
    outer, inner = lax.axis_index("outer"), lax.axis_index("inner")
    member, core = inner // 2, inner % 2
    chans = stem.shape[1]
    part = stem.shape[0] // MEMBERS
    rows = part // CHUNKS
    mine = swapped(member, outer)
    up, down = (outer + 1) % GROUPS, (outer + GROUPS - 1) % GROUPS
    neighbours = (
        (up, 2 * swapped(mine, up) + core),
        (down, 2 * swapped(mine, down) + core),
    )

    has = (outer < GROUPS - 1, outer > 0)

    def other(step):
        way = step // 2
        return (member // 2 + way + core * (4 - 2 * way)) % 4 * 2 + (member + step) % 2

    barrier = pltpu.get_barrier_semaphore()

    def greet(device):
        pl.semaphore_signal(barrier, inc=1, device_id=device, device_id_type=MESH)

    for step in range(1, MEMBERS):
        greet((outer, 2 * other(step) + core))
    greet((outer, inner + 1 - 2 * core))
    for neighbour, there in zip(neighbours, has):

        @pl.when(there)
        def _():
            greet(neighbour)


    def load_taps(layer, tap, half):
        return pltpu.make_async_copy(
            weight.at[layer, tap],
            taps.at[layer, tap, pl.ds(half * chans, chans)],
            weight_sem.at[layer, tap, half],
        )

    def load_heads(k):
        source = (query_weight, key_weight, value_weight, output_weight)[k]
        return pltpu.make_async_copy(source, heads_weight.at[k], heads_sem.at[k])

    every_tap = [(layer, tap, half) for layer in range(2) for tap in range(3) for half in range(2)]
    pl.semaphore_wait(barrier, MEMBERS + has[0].astype(jnp.int32) + has[1].astype(jnp.int32))

    def span(chunk):
        return pl.ds(pl.multiple_of(chunk * rows, rows), rows)

    def piece(index, chunk):
        return pl.ds(pl.multiple_of(index * part + chunk * rows, rows), rows)

    def send_in(chunk, step):
        to = other(step)
        return pltpu.make_async_remote_copy(
            src_ref=stem.at[piece(swapped(to, outer), chunk)],
            dst_ref=rows_in.at[HALO + member, span(chunk)],
            send_sem=in_send.at[chunk, step],
            recv_sem=in_recv.at[chunk, member],
            device_id=(outer, 2 * to + core),
            device_id_type=MESH,
        )

    def keep_in(chunk):
        return pltpu.make_async_copy(
            stem.at[piece(mine, chunk)], rows_in.at[HALO + member, span(chunk)], in_recv.at[chunk, member]
        )

    def arrived(chunk, block):
        there = rows_in.at[HALO + block, span(chunk)]
        return pltpu.make_async_copy(there, there, in_recv.at[chunk, block])

    def send_halo(chunk, side):
        return pltpu.make_async_remote_copy(
            src_ref=rows_in.at[pl.ds(MEMBERS if side == 0 else HALO, HALO), span(chunk)],
            dst_ref=rows_in.at[pl.ds(0 if side == 0 else HALO + MEMBERS, HALO), span(chunk)],
            send_sem=halo_send.at[chunk, side],
            recv_sem=halo_recv.at[chunk, side],
            device_id=neighbours[side],
            device_id_type=MESH,
        )

    def send_out(chunk, step):
        to = other(step)
        return pltpu.make_async_remote_copy(
            src_ref=rows_out.at[to, span(chunk)],
            dst_ref=tower.at[piece(mine, chunk)],
            send_sem=out_send.at[chunk, step],
            recv_sem=out_recv.at[chunk, mine],
            device_id=(outer, 2 * to + core),
            device_id_type=MESH,
        )

    def keep_out(chunk):
        return pltpu.make_async_copy(
            rows_out.at[member, span(chunk)], tower.at[piece(mine, chunk)], out_recv.at[chunk, mine]
        )

    def returned(chunk, index):
        there = tower.at[piece(index, chunk)]
        return pltpu.make_async_copy(there, there, out_recv.at[chunk, index])

    def start_in(chunk):
        keep_in(chunk).start()
        for step in ORDER:
            send_in(chunk, step).start()

    def start_out(chunk):
        keep_out(chunk).start()
        for step in ORDER:
            send_out(chunk, step).start()

    def forward(chunk):
        for block in range(MEMBERS - HALO, MEMBERS):
            arrived(chunk, block).wait()

        @pl.when(has[0])
        def _():
            send_halo(chunk, 0).start()

        for block in range(HALO):
            arrived(chunk, block).wait()

        @pl.when(has[1])
        def _():
            send_halo(chunk, 1).start()

        for block in range(HALO, MEMBERS - HALO):
            arrived(chunk, block).wait()

    def split(value, into, first, columns=slice(0, 768)):
        high = value.astype(BF16)
        count, start, stop = value.shape[0], columns.start, columns.stop
        into[first : first + count, start:stop] = high
        into[first : first + count, chans + start : chans + stop] = (value - high.astype(F32)).astype(BF16)

    def inside(block):
        if 0 <= block < MEMBERS:
            return 1.0
        number = outer * MEMBERS + block
        return ((number >= 0) & (number < GROUPS * MEMBERS)).astype(F32)

    def conv(source, layer, spread, blocks, columns):
        total = bias[layer : layer + 1, columns]
        for tap in range(3):
            first = tap * spread * rows
            total = total + dot(source[first : first + blocks * rows, :], taps[layer, tap, :, columns])
        return total

    tiles = [slice(start, start + COLUMNS) for start in range(0, chans, COLUMNS)]

    def activate(chunk, blocks):
        for block in blocks:
            split(gelu(rows_in[block, span(chunk)]) * inside(block - HALO), active, block * rows)

    def first_layer(chunk):
        for columns in tiles:
            result = conv(active, 0, 1, MEMBERS + 4, columns)
            for block in range(MEMBERS + 4):
                at = slice(block * rows, (block + 1) * rows)
                total = rows_in[block + 1, span(chunk), columns] + result[at]
                field[at, columns] = total
                split(gelu(total) * inside(block - 2), second, block * rows, columns)

    def second_layer(chunk, columns):
        result = conv(second, 1, 2, MEMBERS, columns)
        for block in range(MEMBERS):
            before = field[(block + 2) * rows : (block + 3) * rows, columns]
            rows_out[block, span(chunk), columns] = before + result[block * rows : (block + 1) * rows]

    def shelf(run, whose):
        return pl.multiple_of((run * 2 + whose) * MEMBERS * MEMBERS, MEMBERS)

    def slot(run, of):
        return pl.ds(shelf(run, core) + shelf_place(of) * MEMBERS, MEMBERS)

    def column(run, of):
        return pl.ds(shelf(run, core) + of % 2 * (MEMBERS // 2 * MEMBERS), MEMBERS // 2 * MEMBERS)

    def send_pool(run, step):
        part_of = everyone.at[column(run, member) if step == 1 else slot(run, member)]
        return pltpu.make_async_remote_copy(
            src_ref=part_of,
            dst_ref=part_of,
            send_sem=pool_send.at[run, step],
            recv_sem=pool_recv.at[run, member],
            device_id=(outer, 2 * other(step) + core),
            device_id_type=MESH,
        )

    def share(run):
        half = pl.ds(shelf(run, core), MEMBERS * MEMBERS)
        return pltpu.make_async_remote_copy(
            src_ref=everyone.at[half],
            dst_ref=everyone.at[half],
            send_sem=share_send.at[run],
            recv_sem=share_recv.at[run],
            device_id=(outer, inner + 1 - 2 * core),
            device_id_type=MESH,
        )

    def start_pool(run):
        everyone[slot(run, member), :] = jnp.concatenate(
            [
                jnp.sum(rows_out[block, run * POOL : (run + 1) * POOL], axis=0, keepdims=True) * (1.0 / POOL)
                for block in range(MEMBERS)
            ],
            axis=0,
        )
        for step in ROUND:
            send_pool(run, step).start()

    def pass_pool(run):
        for step in ROUND:
            there = everyone.at[slot(run, other(step))]
            pltpu.make_async_copy(there, there, pool_recv.at[run, other(step)]).wait()
        send_pool(run, 1).start()

    def start_share(run):
        there = everyone.at[column(run, other(1))]
        pltpu.make_async_copy(there, there, pool_recv.at[run, other(1)]).wait()
        share(run).start()

    def finish_share(run):
        there = everyone.at[pl.ds(shelf(run, 1 - core), MEMBERS * MEMBERS)]
        pltpu.make_async_copy(there, there, share_recv.at[run]).wait()

    def bring(chunk):
        @pl.when(chunk + AHEAD < CHUNKS)
        def _():
            forward(chunk + AHEAD)

        @pl.when(chunk + AHEAD + IN_FLIGHT < CHUNKS)
        def _():
            start_in(chunk + AHEAD + IN_FLIGHT)

        for side in range(2):

            @pl.when(has[1 - side])
            def _():
                send_halo(chunk, side).wait_recv()

    blocks = range(MEMBERS + 2 * HALO)
    for chunk in range(IN_FLIGHT):
        start_in(chunk)
    for which in every_tap:
        load_taps(*which).start()
    for side in range(2):
        @pl.when(jnp.logical_not(has[side]))
        def _():
            rows_in[0 if side else HALO + MEMBERS : HALO if side else 2 * HALO + MEMBERS] = jnp.zeros(
                (HALO, part, chans), F32
            )

    for chunk in range(AHEAD):
        forward(chunk)
        start_in(chunk + IN_FLIGHT)
    bring(0)
    for k in range(4):
        load_heads(k).start()
    activate(0, blocks)
    for which in every_tap:
        load_taps(*which).wait()
    first_layer(0)

    def step_of(chunk, _):
        bring(chunk)
        for k, columns in enumerate(tiles):
            second_layer(chunk - 1, columns)
            activate(chunk, blocks[k :: len(tiles)])
        first_layer(chunk)

        @pl.when(chunk == HELD)
        def _():
            start_out(0)

        @pl.when(chunk >= HELD)
        def _():
            start_out(chunk - HELD + 1)

        @pl.when(chunk == CHUNKS // 2)
        def _():
            start_pool(0)

        @pl.when(chunk == CHUNKS // 2 + 1)
        def _():
            pass_pool(0)

        @pl.when(chunk == CHUNKS // 2 + 2)
        def _():
            start_share(0)

        return 0

    lax.fori_loop(1, CHUNKS, step_of, 0)
    for columns in tiles:
        second_layer(CHUNKS - 1, columns)
    start_pool(1)
    start_out(CHUNKS - HELD + 1)
    pass_pool(1)
    start_out(CHUNKS - HELD + 2)
    start_share(1)
    for chunk in range(CHUNKS - HELD + 3, CHUNKS):
        start_out(chunk)
    for k in range(4):
        load_heads(k).wait()
    finish_share(0)
    finish_share(1)

    runs = part // POOL
    count = MEMBERS * runs
    total = 2 * MEMBERS * count
    for k, third in enumerate(thirds(everyone[...])):
        split_rows[k * total : (k + 1) * total, :] = third

    def stacked(value, weight):
        size = value.shape[0] // 3
        result = dot(value, weight)
        return (result[2 * size :] + result[size : 2 * size]) + result[:size]

    place = lax.broadcasted_iota(jnp.int32, (count, total), 0)
    wanted = ((place % runs * 2 + core) * MEMBERS + shelf_place(swapped(place // runs, outer))) * MEMBERS + member
    chosen = (lax.broadcasted_iota(jnp.int32, (count, total), 1) == wanted).astype(F32).astype(BF16)
    own_parts = [dot(chosen, split_rows[k * total : (k + 1) * total, :]) for k in range(3)]
    own = (own_parts[2] + own_parts[1]) + own_parts[0]
    own_rows = jnp.concatenate([value.astype(BF16) for value in own_parts], axis=0)
    width = HEADS_AT_ONCE * HEAD_DIM
    head = lax.broadcasted_iota(jnp.int32, (1, width), 1) // HEAD_DIM
    masks = [(head == k).astype(F32) for k in range(HEADS_AT_ONCE)]

    for start in range(0, chans, width):
        columns = slice(start, start + width)
        queries = stacked(own_rows, heads_weight[0, :, columns]) * (HEAD_DIM**-0.5)
        keys = stacked(split_rows[...], heads_weight[1, :, columns])
        vals = stacked(split_rows[...], heads_weight[2, :, columns])
        scores = lax.dot_general(
            jnp.concatenate([queries * mask for mask in masks], axis=0),
            keys,
            (((1,), (1,)), ((), ())),
            precision=lax.Precision.HIGHEST,
            preferred_element_type=F32,
        )
        powers = jnp.exp(scores - jnp.max(scores, axis=1, keepdims=True))
        probs = powers / jnp.sum(powers, axis=1, keepdims=True)
        each = jnp.dot(probs, vals, precision=lax.Precision.HIGHEST, preferred_element_type=F32)
        mixed[:, columns] = sum(each[k * count : (k + 1) * count] * mask for k, mask in enumerate(masks))

    attended[...] = own + stacked(jnp.concatenate(thirds(mixed[...]), axis=0), heads_weight[3])

    for run in range(runs):
        share(run).wait_send()
        for step in (1, *ROUND):
            send_pool(run, step).wait_send()

    def finish(chunk, _):
        for side in range(2):

            @pl.when(has[side])
            def _():
                send_halo(chunk, side).wait_send()

        for step in range(1, MEMBERS):
            send_in(chunk, step).wait_send()
            send_out(chunk, step).wait_send()
        for index in range(MEMBERS):
            returned(chunk, index).wait()
        return 0

    lax.fori_loop(0, CHUNKS, finish, 0)


def shards(stem_activity, convolution_weight, convolution_bias, query_weight, key_weight, value_weight, output_weight):
    length, chans = stem_activity.shape
    part = length // MEMBERS
    rows = part // CHUNKS
    blocks = MEMBERS + 2 * HALO
    pooled = length // POOL
    dma, vmem = pltpu.SemaphoreType.DMA, pltpu.VMEM
    far, on_core = pl.BlockSpec(memory_space=pltpu.HBM), pl.BlockSpec(memory_space=vmem)
    return pl.pallas_call(
        tower_kernel,
        out_shape=(
            vmem((length, chans), F32),
            jax.ShapeDtypeStruct((pooled, chans), F32),
        ),
        in_specs=[far, far, on_core, far, far, far, far],
        out_specs=(on_core, on_core),
        scratch_shapes=[
            vmem((blocks, part, chans), F32),
            vmem((MEMBERS, part, chans), F32),
            vmem((2, 3, 2 * chans, chans), BF16),
            vmem((blocks * rows, 2 * chans), BF16),
            vmem(((blocks - 2) * rows, 2 * chans), BF16),
            vmem(((blocks - 2) * rows, chans), F32),
            vmem((2 * MEMBERS * pooled, chans), F32),
            vmem((3 * 2 * MEMBERS * pooled, chans), BF16),
            vmem((pooled, chans), F32),
            vmem((4, chans, chans), BF16),
            dma((2, 3, 2)),
            dma((4,)),
            dma((CHUNKS, MEMBERS)),
            dma((CHUNKS, MEMBERS)),
            dma((CHUNKS, 2)),
            dma((CHUNKS, 2)),
            dma((CHUNKS, MEMBERS)),
            dma((CHUNKS, MEMBERS)),
            dma((2, MEMBERS)),
            dma((2, MEMBERS)),
            dma((2,)),
            dma((2,)),
        ],
        compiler_params=pltpu.CompilerParams(
            collective_id=0, has_side_effects=True, vmem_limit_bytes=50 * 1024 * 1024
        ),
        cost_estimate=pl.CostEstimate(
            flops=5 * 2 * 2 * 3 * length * chans * chans, bytes_accessed=8 * length * chans, transcendentals=0
        ),
        name="tower",
    )(
        stem_activity, convolution_weight, convolution_bias,
        query_weight, key_weight, value_weight, output_weight,
    )


def solution(mesh):
    return jax.shard_map(
        shards,
        mesh=mesh,
        in_specs=(P(("outer", "inner"), None), P(), P(), P(), P(), P(), P()),
        out_specs=(P(("outer", "inner"), None), P(("outer", "inner"), None)),
        check_vma=False,
    )
```

```python
import jax
import jax.numpy as jnp
from jax import lax
from jax.experimental import pallas as pl
from jax.experimental.pallas import tpu as pltpu
from jax.sharding import PartitionSpec as P

HEAD_DIM = 64
POOL = 128
GROUPS = 8
MEMBERS = 8
HALO = 3
CHUNKS = 8
IN_FLIGHT = 6
HELD = 3
AHEAD = 1
COLUMNS = 256
ORDER = (1, 2, 6, 5, 4, 3, 7)
ROUND = (2, 4, 6)
HEADS_AT_ONCE = 4
MESH = pl.DeviceIdType.MESH
F32, BF16 = jnp.float32, jnp.bfloat16


def gelu(x):
    return 0.5 * x * (1.0 + lax.erf(x * (0.5**0.5)))


def dot(left, right):
    return jnp.dot(left, right, preferred_element_type=F32)


def thirds(value):
    high = value.astype(BF16)
    rest = value - high.astype(F32)
    middle = rest.astype(BF16)
    return high, middle, (rest - middle.astype(F32)).astype(BF16)


def swapped(member, outer):
    return member // 2 * 2 + (member + outer // 4) % 2


def shelf_place(member):
    return member % 2 * (MEMBERS // 2) + member // 2


def tower_kernel(
    stem, weight, bias, query_weight, key_weight, value_weight, output_weight,
    tower, attended,
    rows_in, rows_out, taps, active, second, field, everyone, split_rows, mixed, heads_weight,
    weight_sem, heads_sem, in_send, in_recv, halo_send, halo_recv, out_send, out_recv,
    pool_send, pool_recv, share_send, share_recv,
):
    outer, inner = lax.axis_index("outer"), lax.axis_index("inner")
    member, core = inner // 2, inner % 2
    chans = stem.shape[1]
    part = stem.shape[0] // MEMBERS
    rows = part // CHUNKS
    mine = swapped(member, outer)
    up, down = (outer + 1) % GROUPS, (outer + GROUPS - 1) % GROUPS
    neighbours = (
        (up, 2 * swapped(mine, up) + core),
        (down, 2 * swapped(mine, down) + core),
    )

    has = (outer < GROUPS - 1, outer > 0)

    def other(step):
        way = step // 2
        return (member // 2 + way + core * (4 - 2 * way)) % 4 * 2 + (member + step) % 2

    barrier = pltpu.get_barrier_semaphore()

    def greet(device):
        pl.semaphore_signal(barrier, inc=1, device_id=device, device_id_type=MESH)

    for step in range(1, MEMBERS):
        greet((outer, 2 * other(step) + core))
    greet((outer, inner + 1 - 2 * core))
    for neighbour, there in zip(neighbours, has):

        @pl.when(there)
        def _():
            greet(neighbour)


    def load_taps(layer, tap, half):
        return pltpu.make_async_copy(
            weight.at[layer, tap],
            taps.at[layer, tap, pl.ds(half * chans, chans)],
            weight_sem.at[layer, tap, half],
        )

    def load_heads(k):
        source = (query_weight, key_weight, value_weight, output_weight)[k]
        return pltpu.make_async_copy(source, heads_weight.at[k], heads_sem.at[k])

    every_tap = [(layer, tap, half) for layer in range(2) for tap in range(3) for half in range(2)]
    pl.semaphore_wait(barrier, MEMBERS + has[0].astype(jnp.int32) + has[1].astype(jnp.int32))

    def span(chunk):
        return pl.ds(pl.multiple_of(chunk * rows, rows), rows)

    def piece(index, chunk):
        return pl.ds(pl.multiple_of(index * part + chunk * rows, rows), rows)

    def send_in(chunk, step):
        to = other(step)
        return pltpu.make_async_remote_copy(
            src_ref=stem.at[piece(swapped(to, outer), chunk)],
            dst_ref=rows_in.at[HALO + member, span(chunk)],
            send_sem=in_send.at[chunk, step],
            recv_sem=in_recv.at[chunk, member],
            device_id=(outer, 2 * to + core),
            device_id_type=MESH,
        )

    def keep_in(chunk):
        return pltpu.make_async_copy(
            stem.at[piece(mine, chunk)], rows_in.at[HALO + member, span(chunk)], in_recv.at[chunk, member]
        )

    def arrived(chunk, block):
        there = rows_in.at[HALO + block, span(chunk)]
        return pltpu.make_async_copy(there, there, in_recv.at[chunk, block])

    def send_halo(chunk, side):
        return pltpu.make_async_remote_copy(
            src_ref=rows_in.at[pl.ds(MEMBERS if side == 0 else HALO, HALO), span(chunk)],
            dst_ref=rows_in.at[pl.ds(0 if side == 0 else HALO + MEMBERS, HALO), span(chunk)],
            send_sem=halo_send.at[chunk, side],
            recv_sem=halo_recv.at[chunk, side],
            device_id=neighbours[side],
            device_id_type=MESH,
        )

    def send_out(chunk, step):
        to = other(step)
        return pltpu.make_async_remote_copy(
            src_ref=rows_out.at[to, span(chunk)],
            dst_ref=tower.at[piece(mine, chunk)],
            send_sem=out_send.at[chunk, step],
            recv_sem=out_recv.at[chunk, mine],
            device_id=(outer, 2 * to + core),
            device_id_type=MESH,
        )

    def keep_out(chunk):
        return pltpu.make_async_copy(
            rows_out.at[member, span(chunk)], tower.at[piece(mine, chunk)], out_recv.at[chunk, mine]
        )

    def returned(chunk, index):
        there = tower.at[piece(index, chunk)]
        return pltpu.make_async_copy(there, there, out_recv.at[chunk, index])

    def start_in(chunk):
        keep_in(chunk).start()
        for step in ORDER:
            send_in(chunk, step).start()

    def start_out(chunk):
        keep_out(chunk).start()
        for step in ORDER:
            send_out(chunk, step).start()

    def forward(chunk):
        for block in range(MEMBERS - HALO, MEMBERS):
            arrived(chunk, block).wait()

        @pl.when(has[0])
        def _():
            send_halo(chunk, 0).start()

        for block in range(HALO):
            arrived(chunk, block).wait()

        @pl.when(has[1])
        def _():
            send_halo(chunk, 1).start()

        for block in range(HALO, MEMBERS - HALO):
            arrived(chunk, block).wait()

    def split(value, into, first, columns=slice(0, 768)):
        high = value.astype(BF16)
        count, start, stop = value.shape[0], columns.start, columns.stop
        into[first : first + count, start:stop] = high
        into[first : first + count, chans + start : chans + stop] = (value - high.astype(F32)).astype(BF16)

    def inside(block):
        if 0 <= block < MEMBERS:
            return 1.0
        number = outer * MEMBERS + block
        return ((number >= 0) & (number < GROUPS * MEMBERS)).astype(F32)

    def conv(source, layer, spread, blocks, columns):
        total = bias[layer : layer + 1, columns]
        for tap in range(3):
            first = tap * spread * rows
            total = total + dot(source[first : first + blocks * rows, :], taps[layer, tap, :, columns])
        return total

    tiles = [slice(start, start + COLUMNS) for start in range(0, chans, COLUMNS)]

    def activate(chunk, blocks):
        for block in blocks:
            split(gelu(rows_in[block, span(chunk)]) * inside(block - HALO), active, block * rows)

    def first_layer(chunk):
        for columns in tiles:
            result = conv(active, 0, 1, MEMBERS + 4, columns)
            for block in range(MEMBERS + 4):
                at = slice(block * rows, (block + 1) * rows)
                total = rows_in[block + 1, span(chunk), columns] + result[at]
                field[at, columns] = total
                split(gelu(total) * inside(block - 2), second, block * rows, columns)

    def second_layer(chunk, columns):
        result = conv(second, 1, 2, MEMBERS, columns)
        for block in range(MEMBERS):
            before = field[(block + 2) * rows : (block + 3) * rows, columns]
            rows_out[block, span(chunk), columns] = before + result[block * rows : (block + 1) * rows]

    def shelf(run, whose):
        return pl.multiple_of((run * 2 + whose) * MEMBERS * MEMBERS, MEMBERS)

    def slot(run, of):
        return pl.ds(shelf(run, core) + shelf_place(of) * MEMBERS, MEMBERS)

    def column(run, of):
        return pl.ds(shelf(run, core) + of % 2 * (MEMBERS // 2 * MEMBERS), MEMBERS // 2 * MEMBERS)

    def send_pool(run, step):
        part_of = everyone.at[column(run, member) if step == 1 else slot(run, member)]
        return pltpu.make_async_remote_copy(
            src_ref=part_of,
            dst_ref=part_of,
            send_sem=pool_send.at[run, step],
            recv_sem=pool_recv.at[run, member],
            device_id=(outer, 2 * other(step) + core),
            device_id_type=MESH,
        )

    def share(run):
        half = pl.ds(shelf(run, core), MEMBERS * MEMBERS)
        return pltpu.make_async_remote_copy(
            src_ref=everyone.at[half],
            dst_ref=everyone.at[half],
            send_sem=share_send.at[run],
            recv_sem=share_recv.at[run],
            device_id=(outer, inner + 1 - 2 * core),
            device_id_type=MESH,
        )

    def start_pool(run):
        everyone[slot(run, member), :] = jnp.concatenate(
            [
                jnp.sum(rows_out[block, run * POOL : (run + 1) * POOL], axis=0, keepdims=True) * (1.0 / POOL)
                for block in range(MEMBERS)
            ],
            axis=0,
        )
        for step in ROUND:
            send_pool(run, step).start()

    def pass_pool(run):
        for step in ROUND:
            there = everyone.at[slot(run, other(step))]
            pltpu.make_async_copy(there, there, pool_recv.at[run, other(step)]).wait()
        send_pool(run, 1).start()

    def start_share(run):
        there = everyone.at[column(run, other(1))]
        pltpu.make_async_copy(there, there, pool_recv.at[run, other(1)]).wait()
        share(run).start()

    def finish_share(run):
        there = everyone.at[pl.ds(shelf(run, 1 - core), MEMBERS * MEMBERS)]
        pltpu.make_async_copy(there, there, share_recv.at[run]).wait()

    def bring(chunk):
        @pl.when(chunk + AHEAD < CHUNKS)
        def _():
            forward(chunk + AHEAD)

        @pl.when(chunk + AHEAD + IN_FLIGHT < CHUNKS)
        def _():
            start_in(chunk + AHEAD + IN_FLIGHT)

        for side in range(2):

            @pl.when(has[1 - side])
            def _():
                send_halo(chunk, side).wait_recv()

    blocks = range(MEMBERS + 2 * HALO)
    for chunk in range(IN_FLIGHT):
        start_in(chunk)
    for which in every_tap:
        load_taps(*which).start()
    for side in range(2):
        @pl.when(jnp.logical_not(has[side]))
        def _():
            rows_in[0 if side else HALO + MEMBERS : HALO if side else 2 * HALO + MEMBERS] = jnp.zeros(
                (HALO, part, chans), F32
            )

    for chunk in range(AHEAD):
        forward(chunk)
        start_in(chunk + IN_FLIGHT)
    bring(0)
    for k in range(4):
        load_heads(k).start()
    activate(0, blocks)
    for which in every_tap:
        load_taps(*which).wait()
    first_layer(0)

    def step_of(chunk, _):
        bring(chunk)
        for k, columns in enumerate(tiles):
            second_layer(chunk - 1, columns)
            activate(chunk, blocks[k :: len(tiles)])
        first_layer(chunk)

        @pl.when(chunk == HELD)
        def _():
            start_out(0)

        @pl.when(chunk >= HELD)
        def _():
            start_out(chunk - HELD + 1)

        @pl.when(chunk == CHUNKS // 2)
        def _():
            start_pool(0)

        @pl.when(chunk == CHUNKS // 2 + 1)
        def _():
            pass_pool(0)

        @pl.when(chunk == CHUNKS // 2 + 2)
        def _():
            start_share(0)

        return 0

    lax.fori_loop(1, CHUNKS, step_of, 0)
    for columns in tiles:
        second_layer(CHUNKS - 1, columns)
    start_pool(1)
    start_out(CHUNKS - HELD + 1)
    pass_pool(1)
    start_out(CHUNKS - HELD + 2)
    start_share(1)
    for chunk in range(CHUNKS - HELD + 3, CHUNKS):
        start_out(chunk)
    for k in range(4):
        load_heads(k).wait()
    finish_share(0)
    finish_share(1)

    runs = part // POOL
    count = MEMBERS * runs
    total = 2 * MEMBERS * count
    for k, third in enumerate(thirds(everyone[...])):
        split_rows[k * total : (k + 1) * total, :] = third

    def stacked(value, weight):
        size = value.shape[0] // 3
        result = dot(value, weight)
        return (result[2 * size :] + result[size : 2 * size]) + result[:size]

    place = lax.broadcasted_iota(jnp.int32, (count, total), 0)
    wanted = ((place % runs * 2 + core) * MEMBERS + shelf_place(swapped(place // runs, outer))) * MEMBERS + member
    chosen = (lax.broadcasted_iota(jnp.int32, (count, total), 1) == wanted).astype(F32).astype(BF16)
    own_parts = [dot(chosen, split_rows[k * total : (k + 1) * total, :]) for k in range(3)]
    own = (own_parts[2] + own_parts[1]) + own_parts[0]
    own_rows = jnp.concatenate([value.astype(BF16) for value in own_parts], axis=0)
    width = HEADS_AT_ONCE * HEAD_DIM
    head = lax.broadcasted_iota(jnp.int32, (1, width), 1) // HEAD_DIM
    masks = [(head == k).astype(F32) for k in range(HEADS_AT_ONCE)]

    for start in range(0, chans, width):
        columns = slice(start, start + width)
        queries = stacked(own_rows, heads_weight[0, :, columns]) * (HEAD_DIM**-0.5)
        keys = stacked(split_rows[...], heads_weight[1, :, columns])
        vals = stacked(split_rows[...], heads_weight[2, :, columns])
        scores = lax.dot_general(
            jnp.concatenate([queries * mask for mask in masks], axis=0),
            keys,
            (((1,), (1,)), ((), ())),
            precision=lax.Precision.HIGHEST,
            preferred_element_type=F32,
        )
        powers = jnp.exp(scores - jnp.max(scores, axis=1, keepdims=True))
        probs = powers / jnp.sum(powers, axis=1, keepdims=True)
        each = jnp.dot(probs, vals, precision=lax.Precision.HIGHEST, preferred_element_type=F32)
        mixed[:, columns] = sum(each[k * count : (k + 1) * count] * mask for k, mask in enumerate(masks))

    attended[...] = own + stacked(jnp.concatenate(thirds(mixed[...]), axis=0), heads_weight[3])

    for run in range(runs):
        share(run).wait_send()
        for step in (1, *ROUND):
            send_pool(run, step).wait_send()

    def finish(chunk, _):
        for side in range(2):

            @pl.when(has[side])
            def _():
                send_halo(chunk, side).wait_send()

        for step in range(1, MEMBERS):
            send_in(chunk, step).wait_send()
            send_out(chunk, step).wait_send()
        for index in range(MEMBERS):
            returned(chunk, index).wait()
        return 0

    lax.fori_loop(0, CHUNKS, finish, 0)


def shards(stem_activity, convolution_weight, convolution_bias, query_weight, key_weight, value_weight, output_weight):
    length, chans = stem_activity.shape
    part = length // MEMBERS
    rows = part // CHUNKS
    blocks = MEMBERS + 2 * HALO
    pooled = length // POOL
    dma, vmem = pltpu.SemaphoreType.DMA, pltpu.VMEM
    far, on_core = pl.BlockSpec(memory_space=pltpu.HBM), pl.BlockSpec(memory_space=vmem)
    return pl.pallas_call(
        tower_kernel,
        out_shape=(
            vmem((length, chans), F32),
            jax.ShapeDtypeStruct((pooled, chans), F32),
        ),
        in_specs=[far, far, on_core, far, far, far, far],
        out_specs=(on_core, on_core),
        scratch_shapes=[
            vmem((blocks, part, chans), F32),
            vmem((MEMBERS, part, chans), F32),
            vmem((2, 3, 2 * chans, chans), BF16),
            vmem((blocks * rows, 2 * chans), BF16),
            vmem(((blocks - 2) * rows, 2 * chans), BF16),
            vmem(((blocks - 2) * rows, chans), F32),
            vmem((2 * MEMBERS * pooled, chans), F32),
            vmem((3 * 2 * MEMBERS * pooled, chans), BF16),
            vmem((pooled, chans), F32),
            vmem((4, chans, chans), BF16),
            dma((2, 3, 2)),
            dma((4,)),
            dma((CHUNKS, MEMBERS)),
            dma((CHUNKS, MEMBERS)),
            dma((CHUNKS, 2)),
            dma((CHUNKS, 2)),
            dma((CHUNKS, MEMBERS)),
            dma((CHUNKS, MEMBERS)),
            dma((2, MEMBERS)),
            dma((2, MEMBERS)),
            dma((2,)),
            dma((2,)),
        ],
        compiler_params=pltpu.CompilerParams(
            collective_id=0, has_side_effects=True, vmem_limit_bytes=50 * 1024 * 1024
        ),
        cost_estimate=pl.CostEstimate(
            flops=5 * 2 * 2 * 3 * length * chans * chans, bytes_accessed=8 * length * chans, transcendentals=0
        ),
        name="tower",
    )(
        stem_activity, convolution_weight, convolution_bias,
        query_weight, key_weight, value_weight, output_weight,
    )


def solution(mesh):
    return jax.shard_map(
        shards,
        mesh=mesh,
        in_specs=(P(("outer", "inner"), None), P(), P(), P(), P(), P(), P()),
        out_specs=(P(("outer", "inner"), None), P(("outer", "inner"), None)),
        check_vma=False,
    )
```
